32 devices in a mesh: tower: 2 (over x), batch: 16 (over z, y, core).
Axes of the slice: x: 2, y: 2, z: 4, core: 2. Of those that a mesh axis runs over, the one named last changes fastest.
Arguments:
- hidden_in: bfloat16 [2, 2, 8192, 768], P(None, 'tower', 'batch'), may hold values from -6 to 6
- query_lengths: int32 [2, 272], P(None, 'batch'), may hold values from 4 to 30, as said below
- passage_lengths: int32 [2, 32], P(None, 'batch'), may hold values from 20 to 200, as said below
- positives: int32 [2, 272], P(None, 'batch'), may hold values from 0 to 31
- query_weight: bfloat16 [768, 768], P(('tower', 'batch')), may hold values from -0.21875 to 0.21875
- query_bias: bfloat16 [768], P(('tower', 'batch')), may hold values from -3 to 3
- key_weight: bfloat16 [768, 768], P(('tower', 'batch')), may hold values from -0.21875 to 0.21875
- value_weight: bfloat16 [768, 768], P(('tower', 'batch')), may hold values from -0.21875 to 0.21875
- value_bias: bfloat16 [768], P(('tower', 'batch')), may hold values from -3 to 3
- output_weight: bfloat16 [768, 768], P(('tower', 'batch')), may hold values from -1.25 to 1.25
- output_bias: bfloat16 [768], P(('tower', 'batch')), may hold values from -3 to 3
- first_gain: bfloat16 [768], P(('tower', 'batch')), may hold values from 0.5 to 1.5
- first_shift: bfloat16 [768], P(('tower', 'batch')), may hold values from -2 to 2
- inner_weight: bfloat16 [768, 3072], P(('tower', 'batch')), may hold values from -0.21875 to 0.21875
- inner_bias: bfloat16 [3072], P(('tower', 'batch')), may hold values from -3 to 3
- outer_weight: bfloat16 [3072, 768], P(('tower', 'batch')), may hold values from -0.109375 to 0.109375
- outer_bias: bfloat16 [768], P(('tower', 'batch')), may hold values from -3 to 3
- second_gain: bfloat16 [768], P(('tower', 'batch')), may hold values from 0.5 to 1.5
- second_shift: bfloat16 [768], P(('tower', 'batch')), may hold values from -2 to 2
Outputs:
- hidden_out: bfloat16 [2, 2, 8192, 768], P(None, 'tower', 'batch')
- input_grad: bfloat16 [2, 2, 8192, 768], P(None, 'tower', 'batch')
- query_weight_grad: float32 [768, 768], P(('tower', 'batch'))
- query_bias_grad: float32 [768], P(('tower', 'batch'))
- key_weight_grad: float32 [768, 768], P(('tower', 'batch'))
- value_weight_grad: float32 [768, 768], P(('tower', 'batch'))
- value_bias_grad: float32 [768], P(('tower', 'batch'))
- output_weight_grad: float32 [768, 768], P(('tower', 'batch'))
- output_bias_grad: float32 [768], P(('tower', 'batch'))
- first_gain_grad: float32 [768], P(('tower', 'batch'))
- first_shift_grad: float32 [768], P(('tower', 'batch'))
- inner_weight_grad: float32 [768, 3072], P(('tower', 'batch'))
- inner_bias_grad: float32 [3072], P(('tower', 'batch'))
- outer_weight_grad: float32 [3072, 768], P(('tower', 'batch'))
- outer_bias_grad: float32 [768], P(('tower', 'batch'))
- second_gain_grad: float32 [768], P(('tower', 'batch'))
- second_shift_grad: float32 [768], P(('tower', 'batch'))
The draws below stay inside these ranges and needn't reach their ends.
Inputs may be any that keep to these rules, and one draw needn't show every extreme that they name: `query_lengths`: within each block of 17 consecutive lengths (one stream) exactly one is 30; each block sums to at most 512. `passage_lengths`: within each block of 2 consecutive lengths (one stream) exactly one is 200; each block sums to at most 512.
All inputs are finite; a program needn't handle non-finite values.
Results may differ from the reference program's by a relative error of at most 0.034.
Values may be sent and summed in bfloat16 or wider, within the bound.
A program may use at most 192 MiB of HBM per device.

```python
import jax
import jax.numpy as jnp
from jax import lax

D = 768
HEADS = 12
FF = 3072
TOK_DEV = 512
MICRO = 2
QLEN_MIN = 4
QLEN = 30
PLEN_MIN = 20
PLEN = 200
QSEQ = 17
PSEQ = 2
TOKENS = 8192
NQ = 272
NP = 32
N_BATCH = 16


def skewed_lengths(key, blocks, slot_count, shortest, longest):
    spread = longest - shortest
    draw_key, pick_key = jax.random.split(key)
    drawn = jax.random.randint(draw_key, (MICRO, blocks, slot_count), 0, spread)
    lengths = shortest + drawn * drawn // spread
    chosen = jax.random.randint(pick_key, (MICRO, blocks, 1), 0, slot_count)
    places = jnp.arange(slot_count, dtype=jnp.int32)[None, None, :]
    lengths = jnp.where(places == chosen, longest, lengths)
    return lengths.reshape(MICRO, blocks * slot_count).astype(jnp.int32)


def draw_query_lengths(key, part):
    key = jax.random.fold_in(key, 11)
    return skewed_lengths(key, NQ // QSEQ, QSEQ, QLEN_MIN, QLEN)


def draw_passage_lengths(key, part):
    key = jax.random.fold_in(key, 23)
    return skewed_lengths(key, NP // PSEQ, PSEQ, PLEN_MIN, PLEN)


def set_ends(values, rng, least, top_value):
    spot = [jax.random.randint(jax.random.fold_in(rng, axis), (), 0, length) for axis, length in enumerate(values.shape)]
    main_axis = values.shape.index(max(values.shape))
    neighbour = spot[:main_axis] + [(spot[main_axis] + 1) % values.shape[main_axis]] + spot[main_axis + 1:]
    return values.at[tuple(spot)].set(least).at[tuple(neighbour)].set(top_value)


def raised(entries, rng, source, target, parts, factor):
    owner, partner = [(jnp.arange(entries.shape[axis_at]) // (entries.shape[axis_at] // parts)).reshape([-1 if axis == axis_at else 1 for axis in range(entries.ndim)]) for axis_at in (source, target)]
    chosen = jax.random.permutation(rng, parts)[partner]
    strong = (owner == chosen) | (owner == (partner + parts // 2) % parts)
    return jnp.where(strong, factor * entries, entries)


def steps_of(stream_key, shape, pieces, least, high):
    level = 1.0
    for axis_at, parts in pieces:
        draws = jax.random.uniform(jax.random.fold_in(jax.random.fold_in(stream_key, 6), axis_at), (parts,), jnp.float32, least / len(pieces), high / len(pieces))
        level = level * jnp.repeat(jnp.exp(draws), shape[axis_at] // parts).reshape((-1,) + (1,) * (len(shape) - 1 - axis_at))
    return level


def scatter_about(own_key, shape, deviation, most, shards=(), held_as=jnp.bfloat16):
    result = jax.random.normal(own_key, shape, jnp.float32) * deviation
    if len(shards) > 0:
        result = steps_of(own_key, shape, shards, -0.22, 0.18) * result
    return jnp.clip(result, min=-most, max=most).astype(held_as)


def heavy_noise(rng, dims, scale, limit, shards, heavy, kind=jnp.bfloat16):
    values = scale * jax.random.normal(rng, dims, jnp.float32)
    if shards:
        values = values * steps_of(rng, dims, shards, -0.22, 0.18)
    return jnp.clip(raised(values, jax.random.fold_in(rng, 3), *heavy), -limit, limit).astype(kind)


def setup_inputs(seed: int = 0) -> dict:
    arg_keys = jax.random.split(jax.random.key(seed), 20)
    return {
        "hidden_in": heavy_noise(arg_keys[0], (MICRO, 2, TOKENS, D), 1.0, 6.0, ((1, 2), (2, 16)), (2, 3, 16, 2.0)),
        "query_lengths": draw_query_lengths(jax.random.fold_in(arg_keys[19], 71), 0),
        "passage_lengths": draw_passage_lengths(jax.random.fold_in(arg_keys[19], 71), 0),
        "positives": set_ends(jax.random.randint(arg_keys[3], (MICRO, NQ), 0, NP), jax.random.fold_in(arg_keys[3], 1), 0, NP - 1).astype(jnp.int32),
        "query_weight": scatter_about(arg_keys[4], (D, D), D ** -0.5, 0.21875, ((0, 32),)),
        "query_bias": scatter_about(arg_keys[5], (D,), 0.5, 3.0, ((0, 32),)),
        "key_weight": scatter_about(arg_keys[6], (D, D), D ** -0.5, 0.21875, ((0, 32),)),
        "value_weight": scatter_about(arg_keys[7], (D, D), D ** -0.5, 0.21875, ((0, 32),)),
        "value_bias": scatter_about(arg_keys[8], (D,), 0.5, 3.0, ((0, 32),)),
        "output_weight": scatter_about(arg_keys[9], (D, D), (D // 32) ** -0.5, 1.25, ((0, 32),)),
        "output_bias": scatter_about(arg_keys[10], (D,), 0.5, 3.0, ((0, 32),)),
        "first_gain": jnp.clip(1.0 + 0.1 * jax.random.normal(arg_keys[11], (D,), jnp.float32), 0.5, 1.5).astype(jnp.bfloat16),
        "first_shift": scatter_about(arg_keys[12], (D,), 0.3, 2.0, ((0, 32),)),
        "inner_weight": scatter_about(arg_keys[13], (D, FF), D ** -0.5, 0.21875, ((0, 32),)),
        "inner_bias": scatter_about(arg_keys[14], (FF,), 0.5, 3.0, ((0, 32),)),
        "outer_weight": scatter_about(arg_keys[15], (FF, D), FF ** -0.5, 0.109375, ((0, 32),)),
        "outer_bias": scatter_about(arg_keys[16], (D,), 0.5, 3.0, ((0, 32),)),
        "second_gain": jnp.clip(1.0 + 0.1 * jax.random.normal(arg_keys[17], (D,), jnp.float32), 0.5, 1.5).astype(jnp.bfloat16),
        "second_shift": scatter_about(arg_keys[18], (D,), 0.3, 2.0, ((0, 32),)),
    }


@jax.custom_vjp
def low(v):
    return lax.optimization_barrier(v.astype(jnp.bfloat16)).astype(jnp.float32)

@jax.custom_vjp
def low_back(v):
    return v

def low_keep(v):
    return (low(v), None)

def low_pass(kept, grad):
    return (grad,)

def back_keep(v):
    return (v, None)

def back_low(kept, grad):
    return (low(grad),)
low.defvjp(low_keep, low_pass)
low_back.defvjp(back_keep, back_low)
EPSILON = 1e-12
MASKED = -1e+30
HIGHEST = lax.Precision.HIGHEST

def product(left, right):
    return jnp.dot(left, right, precision=HIGHEST, preferred_element_type=jnp.float32)

def normalize(values, gains, shifts):
    average = lax.optimization_barrier(jnp.mean(values, -1, keepdims=True))
    centred = values - average
    spread = lax.optimization_barrier(jnp.mean(centred * centred, -1, keepdims=True))
    return centred * lax.rsqrt(spread + EPSILON) * gains + shifts

def segments(lengths):
    ends = jnp.cumsum(lengths).astype(jnp.int32)
    places = jnp.arange(TOK_DEV, dtype=jnp.int32)
    labels = lax.optimization_barrier(jnp.sum((places[:, None] >= ends[None, :]).astype(jnp.int32), 1))
    return (labels, places < ends[-1], (ends - lengths).astype(jnp.int32))

def stream(inputs, labels, params):
    query_mat, query_vec, key_mat, value_mat, value_vec, out_mat, out_vec, gain_one, shift_one, inner_mat, inner_vec, outer_mat, outer_vec, gain_two, shift_two = params
    head_size = D // HEADS
    queries = low(low_back(product(inputs, query_mat) + query_vec)).reshape(TOK_DEV, HEADS, head_size)
    keys = low(low_back(product(inputs, key_mat))).reshape(TOK_DEV, HEADS, head_size)
    values = low(low_back(product(inputs, value_mat) + value_vec)).reshape(TOK_DEV, HEADS, head_size)
    scores = jnp.einsum('qhd,khd->hqk', queries, keys, precision=HIGHEST) * head_size ** (-0.5)
    scores = low_back(scores)
    allowed = labels[None, :, None] == labels[None, None, :]
    shares = low(jax.nn.softmax(jnp.where(allowed, scores, MASKED), -1))
    attended = jnp.einsum('hqk,khd->qhd', shares, values, precision=HIGHEST).reshape(TOK_DEV, D)
    attended = low(low_back(attended))
    branch = low_back(product(attended, out_mat) + out_vec)
    hidden = low(normalize(inputs + branch, gain_one, shift_one))
    inner = low_back(product(hidden, inner_mat) + inner_vec)
    active = low(jax.nn.gelu(inner, approximate=False))
    outer = low_back(product(active, outer_mat) + outer_vec)
    return normalize(hidden + outer, gain_two, shift_two)

def pick_rows(stream_rows, places):
    return stream_rows[places]

def reference(hidden_in, query_lengths, passage_lengths, positives, query_weight, query_bias, key_weight, value_weight, value_bias, output_weight, output_bias, first_gain, first_shift, inner_weight, inner_bias, outer_weight, outer_bias, second_gain, second_shift):
    weights = tuple((item.astype(jnp.float32) for item in (query_weight, query_bias, key_weight, value_weight, value_bias, output_weight, output_bias, first_gain, first_shift, inner_weight, inner_bias, outer_weight, outer_bias, second_gain, second_shift)))
    query_labels, query_valid, query_starts = jax.vmap(jax.vmap(segments))(query_lengths.reshape(MICRO, N_BATCH, QSEQ))
    passage_labels, passage_valid, passage_starts = jax.vmap(jax.vmap(segments))(passage_lengths.reshape(MICRO, N_BATCH, PSEQ))
    all_labels = jnp.stack([query_labels, passage_labels], 1)
    all_valid = jnp.stack([query_valid, passage_valid], 1)
    inputs_all = hidden_in.astype(jnp.float32).reshape(MICRO, 2, N_BATCH, TOK_DEV, D)
    checked = jax.checkpoint(stream)

    def whole(params, inputs_all):

        def run(pair):
            return checked(pair[0], pair[1], params)
        outputs = lax.map(run, (inputs_all.reshape(-1, TOK_DEV, D), all_labels.reshape(-1, TOK_DEV)))
        outputs = outputs.reshape(MICRO, 2, N_BATCH, TOK_DEV, D)
        query_cls = low(jax.vmap(jax.vmap(pick_rows))(outputs[:, 0], query_starts).reshape(MICRO, NQ, D))
        passage_cls = low(jax.vmap(jax.vmap(pick_rows))(outputs[:, 1], passage_starts).reshape(MICRO, NP, D))
        logits = jnp.einsum('mqd,mpd->mqp', query_cls, passage_cls, precision=HIGHEST) * D ** (-0.5)
        logits = low_back(logits)
        picked = jnp.take_along_axis(logits, positives[:, :, None], 2)[:, :, 0]
        loss = jnp.sum(jax.nn.logsumexp(logits, -1) - picked) / MICRO
        shown = jnp.where(all_valid[..., None], outputs, 0.0).reshape(MICRO, 2, TOKENS, D)
        return (loss, shown)
    loss, pullback, shown = jax.vjp(whole, weights, inputs_all, has_aux=True)
    weight_grads, input_grads = pullback(jnp.ones_like(loss))
    return (shown.astype(jnp.bfloat16), input_grads.reshape(MICRO, 2, TOKENS, D).astype(jnp.bfloat16), weight_grads[0], weight_grads[1], weight_grads[2], weight_grads[3], weight_grads[4], weight_grads[5], weight_grads[6], weight_grads[7], weight_grads[8], weight_grads[9], weight_grads[10], weight_grads[11], weight_grads[12], weight_grads[13], weight_grads[14])
```

```python
import functools

import jax
import jax.numpy as jnp
from jax import lax
from jax.experimental import pallas as pl
from jax.experimental.pallas import tpu as pltpu
from jax.sharding import PartitionSpec as P

HEADS = 12


EPSILON = 1e-12
MASKED = -1e30


def partner_2(x, axis, apart):
    return lax.ppermute(x, axis, [(i, i ^ 1 << apart) for i in range(lax.axis_size(axis))])


def as_sent(x):
    return jax.tree.map(lambda a: a.astype(jnp.bfloat16) if a.dtype == jnp.float32 else a, x)


def product(left, right):
    return jnp.dot(left, right, preferred_element_type=jnp.float32)


def product_tn(left, right):
    return jnp.einsum("ta,tb->ab", left, right, preferred_element_type=jnp.float32)


def product_nt(left, right):
    return jnp.einsum("ra,ba->rb", left, right, preferred_element_type=jnp.float32)


def normalize(values, gains, shifts):
    average = jnp.mean(values, -1, keepdims=True)
    centred = values - average
    inverse = lax.rsqrt(jnp.mean(centred * centred, -1, keepdims=True) + EPSILON)
    normed = centred * inverse
    return (normed * gains + shifts, normed, inverse)


def normalize_back(upstream, normed, inverse, gains):
    scaled = upstream * gains
    inner = (
        scaled
        - jnp.mean(scaled, -1, keepdims=True)
        - normed * jnp.mean(scaled * normed, -1, keepdims=True)
    )
    return (inner * inverse, jnp.sum(upstream * normed, 0), jnp.sum(upstream, 0))


def gelu_slope(values):
    return (
        0.5 * (1.0 + lax.erf(values * 0.7071067811865476))
        + values * jnp.exp(-0.5 * values * values) * 0.3989422804014327
    )


def segments(lengths, token_rows):
    ends = jnp.cumsum(lengths)
    places = jnp.arange(token_rows, dtype=jnp.int32)
    labels = jnp.sum((places[:, None] >= ends[None, :]).astype(jnp.int32), 1)
    starts = jnp.minimum(ends - lengths, token_rows - 1)
    return (labels, places < ends[-1], starts, lengths > 0)


def tail(inputs, attended, params):
    out_mat, out_vec, gain_one, shift_one = (params[5], params[6], params[7], params[8])
    inner_mat, inner_vec, outer_mat, outer_vec, gain_two, shift_two = params[9:15]
    branch = product(attended, out_mat) + out_vec
    hidden_full, normed_one, inverse_one = normalize(
        inputs.astype(jnp.float32) + branch, gain_one, shift_one
    )
    hidden_low = hidden_full.astype(jnp.bfloat16)
    inner = product(hidden_low, inner_mat) + inner_vec
    active = jax.nn.gelu(inner, approximate=False).astype(jnp.bfloat16)
    outer = product(active, outer_mat) + outer_vec
    result, normed_two, inverse_two = normalize(
        hidden_low.astype(jnp.float32) + outer, gain_two, shift_two
    )
    return (result, (normed_one, inverse_one, hidden_low, inner, active, normed_two, inverse_two))


def forward(inputs, labels, valid, params):
    query_mat, query_vec, key_mat, value_mat, value_vec = params[0:5]
    token_rows, width = inputs.shape
    head_size = width // HEADS
    scale = head_size ** (-0.5)
    queries = (product(inputs, query_mat) + query_vec).astype(jnp.bfloat16)
    keys = product(inputs, key_mat).astype(jnp.bfloat16)
    values = (product(inputs, value_mat) + value_vec).astype(jnp.bfloat16)
    block_rows = min(512, token_rows)

    def one_block(first_row):
        allowed = labels[:, None] == labels[None, :]

        def one_head(head_index):
            head_queries = lax.dynamic_slice_in_dim(queries, head_index * head_size, head_size, 1)
            head_keys = lax.dynamic_slice_in_dim(keys, head_index * head_size, head_size, 1)
            head_values = lax.dynamic_slice_in_dim(values, head_index * head_size, head_size, 1)
            scores = jnp.where(allowed, product_nt(head_queries, head_keys) * scale, MASKED)
            highest = jnp.max(scores, -1, keepdims=True)
            powers = jnp.exp(scores - highest)
            totals = jnp.sum(powers, -1, keepdims=True)
            shares = (powers / totals).astype(jnp.bfloat16)
            return (product(shares, head_values), (highest + jnp.log(totals))[:, 0])

        head_out, head_lse = lax.map(one_head, jnp.arange(HEADS, dtype=jnp.int32))
        attended = (
            jnp.transpose(head_out, (1, 0, 2)).reshape(block_rows, width).astype(jnp.bfloat16)
        )
        result, unused = tail(inputs, attended, params)
        shown = jnp.where(valid[:, None], result, 0.0).astype(jnp.bfloat16)
        return (attended, head_lse, shown)

    firsts = jnp.arange(token_rows // block_rows, dtype=jnp.int32) * block_rows
    attended, lse_blocks, shown = lax.map(one_block, firsts)
    attended = attended.reshape(token_rows, width)
    shown = shown.reshape(token_rows, width)
    lse_all = jnp.transpose(lse_blocks, (1, 0, 2)).reshape(HEADS, token_rows)
    return ((queries, keys, values, attended, lse_all), shown)


def backward(inputs, labels, cotangent, starts, live, saved, params):
    queries, keys, values, attended, lse_all = saved
    query_mat, key_mat, value_mat, out_mat = (params[0], params[2], params[3], params[5])
    gain_one, inner_mat, outer_mat, gain_two = (params[7], params[9], params[11], params[13])
    token_rows, width = inputs.shape
    head_size = width // HEADS
    scale = head_size ** (-0.5)
    slot_count = starts.shape[0]
    row_inputs = inputs[starts]
    row_attended = attended[starts]
    unused, kept = tail(row_inputs, row_attended, params)
    normed_one, inverse_one, hidden_low, inner, active, normed_two, inverse_two = kept
    upstream = jnp.where(live[:, None], cotangent, 0.0)
    grad_sum_two, grad_gain_two, grad_shift_two = normalize_back(
        upstream, normed_two, inverse_two, gain_two
    )
    grad_outer = grad_sum_two.astype(jnp.bfloat16)
    grad_outer_mat = product_tn(active, grad_outer)
    grad_outer_vec = jnp.sum(grad_outer.astype(jnp.float32), 0)
    grad_inner = (product_nt(grad_outer, outer_mat) * gelu_slope(inner)).astype(jnp.bfloat16)
    grad_inner_mat = product_tn(hidden_low, grad_inner)
    grad_inner_vec = jnp.sum(grad_inner.astype(jnp.float32), 0)
    grad_hidden = grad_sum_two + product_nt(grad_inner, inner_mat)
    grad_sum_one, grad_gain_one, grad_shift_one = normalize_back(
        grad_hidden, normed_one, inverse_one, gain_one
    )
    grad_branch = grad_sum_one.astype(jnp.bfloat16)
    grad_out_mat = product_tn(row_attended, grad_branch)
    grad_out_vec = jnp.sum(grad_branch.astype(jnp.float32), 0)
    grad_attended = (
        product_nt(grad_branch, out_mat).astype(jnp.bfloat16).reshape(slot_count, HEADS, head_size)
    )
    row_queries = queries[starts].reshape(slot_count, HEADS, head_size)
    keys_split = keys.reshape(token_rows, HEADS, head_size)
    values_split = values.reshape(token_rows, HEADS, head_size)
    allowed = labels[starts][None, :, None] == labels[None, None, :]
    scores = (
        jnp.einsum("rhd,thd->hrt", row_queries, keys_split, preferred_element_type=jnp.float32)
        * scale
    )
    shares = jnp.where(allowed, jnp.exp(scores - lse_all[:, starts][:, :, None]), 0.0)
    shares_low = shares.astype(jnp.bfloat16)
    grad_shares = jnp.einsum(
        "rhd,thd->hrt", grad_attended, values_split, preferred_element_type=jnp.float32
    )
    grad_scores = (
        shares * (grad_shares - jnp.sum(grad_shares * shares, -1, keepdims=True))
    ).astype(jnp.bfloat16)
    grad_queries = (
        jnp.einsum("hrt,thd->rhd", grad_scores, keys_split, preferred_element_type=jnp.float32)
        * scale
    )
    grad_queries = grad_queries.reshape(slot_count, width).astype(jnp.bfloat16)
    grad_keys = (
        jnp.einsum("hrt,rhd->thd", grad_scores, row_queries, preferred_element_type=jnp.float32)
        * scale
    )
    grad_keys = grad_keys.reshape(token_rows, width).astype(jnp.bfloat16)
    grad_values = jnp.einsum(
        "hrt,rhd->thd", shares_low, grad_attended, preferred_element_type=jnp.float32
    )
    grad_values = grad_values.reshape(token_rows, width).astype(jnp.bfloat16)
    grad_inputs = product_nt(grad_keys, key_mat) + product_nt(grad_values, value_mat)
    grad_inputs = grad_inputs.at[starts].add(product_nt(grad_queries, query_mat) + grad_sum_one)
    grads = (
        product_tn(row_inputs, grad_queries),
        jnp.sum(grad_queries.astype(jnp.float32), 0),
        product_tn(inputs, grad_keys),
        product_tn(inputs, grad_values),
        jnp.sum(grad_values.astype(jnp.float32), 0),
        grad_out_mat,
        grad_out_vec,
        grad_gain_one,
        grad_shift_one,
        grad_inner_mat,
        grad_inner_vec,
        grad_outer_mat,
        grad_outer_vec,
        grad_gain_two,
        grad_shift_two,
    )
    return (grad_inputs.astype(jnp.bfloat16), grads)


def cast_params(gathered):
    vector_places = (1, 4, 6, 7, 8, 10, 12, 13, 14)
    return tuple(
        (
            item.astype(jnp.float32) if place in vector_places else item
            for place, item in enumerate(gathered)
        )
    )


def split_halves(grads, side):
    keep_list = []
    give_list = []
    for item in grads:
        half = item.shape[0] // 2
        keep_list.append(lax.dynamic_slice_in_dim(item, side * half, half, 0))
        give_list.append(lax.dynamic_slice_in_dim(item, (1 - side) * half, half, 0))
    return (tuple(keep_list), tuple(give_list))


MESH = pl.DeviceIdType.MESH
BLOCK = 40


class Place:
    def __init__(self):
        self.x = lax.axis_index("tower")
        batch = lax.axis_index("batch")
        self.core = batch % 2
        self.y = (batch // 2) % 2
        self.z = batch // 4

    def device(self, x=None, y=None, z=None, core=None):
        x = self.x if x is None else x
        y = self.y if y is None else y
        z = self.z if z is None else z
        core = self.core if core is None else core
        return (x, z * 4 + y * 2 + core)

    def chip(self, x=None, y=None, z=None):
        x = self.x if x is None else x
        y = self.y if y is None else y
        z = self.z if z is None else z
        return x * 8 + z * 2 + y

    def layer(self, step):
        if step == 0:
            return self.z
        if step == 1:
            return self.z + 1 - 2 * (self.z % 2)
        if step == 2:
            return (self.z + 2) % 4
        return 3 - self.z


def greet(place):
    barrier = pltpu.get_barrier_semaphore()
    peers = [place.device(z=place.layer(step)) for step in (1, 2, 3)]
    peers += [place.device(x=1 - place.x), place.device(y=1 - place.y), place.device(core=1 - place.core)]
    for peer in peers:
        pl.semaphore_signal(barrier, inc=1, device_id=peer, device_id_type=MESH)
    pl.semaphore_wait(barrier, len(peers))


class Sender:
    def __init__(self, send_sems, recv_sems):
        self.send_sems = send_sems
        self.recv_sems = recv_sems
        self.used = 0
        self.open = []

    def send(self, src, dst, slot, peer):
        copy = pltpu.make_async_remote_copy(
            src_ref=src,
            dst_ref=dst,
            send_sem=self.send_sems.at[self.used],
            recv_sem=self.recv_sems.at[slot],
            device_id=peer,
            device_id_type=MESH,
        )
        self.used += 1
        copy.start()
        self.open.append(copy)

    def arrived(self, dst, slot, peer):
        pltpu.make_async_remote_copy(
            src_ref=dst,
            dst_ref=dst,
            send_sem=self.send_sems.at[0],
            recv_sem=self.recv_sems.at[slot],
            device_id=peer,
            device_id_type=MESH,
        ).wait_recv()

    def close(self):
        for copy in self.open:
            copy.wait_send()
        self.open = []


def slot_of(chunk, kind, place_index):
    return (chunk * 9 + kind) * 4 + place_index


def gather_kernel(widths, wide_ref, tall_ref, all_wide, all_tall, stage, send_sems, recv_sems):
    place = Place()
    sender = Sender(send_sems, recv_sems)
    greet(place)
    own_rows = wide_ref.shape[0] * 3 // 4
    tall_rows = tall_ref.shape[0]
    sibling = place.device(core=1 - place.core)
    starts = [0, 2 * widths[0]]
    offsets = [0, widths[0]]

    def wide_view(ref, chunk, core, chip):
        rows = pl.ds(pl.multiple_of(chip * 2 * own_rows, 16), 2 * own_rows)
        first = pl.multiple_of(starts[chunk] + core * widths[chunk], 128)
        return ref.at[rows, pl.ds(first, widths[chunk])]

    def view(chunk, core, chip):
        if chunk < 2:
            return wide_view(all_wide, chunk, core, chip)
        rows = pl.ds(pl.multiple_of((chip * 2 + core) * tall_rows, 16), tall_rows)
        return all_tall.at[rows, :]

    for chunk in range(2):
        first = pl.multiple_of(starts[chunk] + (1 - place.core) * widths[chunk], 128)
        sender.send(
            wide_ref.at[:, pl.ds(first, widths[chunk])],
            stage.at[:, pl.ds(offsets[chunk], widths[chunk])],
            slot_of(chunk, 8, 0),
            sibling,
        )
    own_tall = view(2, place.core, place.chip())
    own_tall[...] = tall_ref[...]

    def assemble(chunk):
        landed = stage.at[:, pl.ds(offsets[chunk], widths[chunk])]
        sender.arrived(landed, slot_of(chunk, 8, 0), sibling)
        first = pl.multiple_of(starts[chunk] + place.core * widths[chunk], 128)
        mine = wide_ref[pl.ds(0, own_rows), pl.ds(first, widths[chunk])].astype(jnp.float32)
        other = stage[pl.ds(0, own_rows), pl.ds(offsets[chunk], widths[chunk])].astype(jnp.float32)
        is_first = place.core == 0
        joined = jnp.concatenate([jnp.where(is_first, mine, other), jnp.where(is_first, other, mine)], 0)
        rows = pl.ds(pl.multiple_of(place.chip() * 2 * own_rows, 16), 2 * own_rows)
        all_wide[rows, pl.ds(first, widths[chunk])] = joined.astype(jnp.bfloat16)

    def begin(chunk):
        own = view(chunk, place.core, place.chip())
        for step in (3, 2, 1):
            sender.send(own, own, slot_of(chunk, 0, place.z), place.device(z=place.layer(step)))
        sender.send(own, own, slot_of(chunk, 1, place.z), place.device(x=1 - place.x))
        sender.send(own, own, slot_of(chunk, 2, place.z), place.device(y=1 - place.y))
        sender.send(own, own, slot_of(chunk, 4, place.z), sibling)

    def along(chunk):
        for step in (1, 2, 3):
            layer = place.layer(step)
            block = view(chunk, place.core, place.chip(z=layer))
            sender.arrived(block, slot_of(chunk, 0, layer), sibling)
            sender.send(block, block, slot_of(chunk, 1, layer), place.device(x=1 - place.x))
            sender.send(block, block, slot_of(chunk, 2, layer), place.device(y=1 - place.y))
            sender.send(block, block, slot_of(chunk, 4, layer), sibling)

    def across(chunk):
        for step in range(4):
            layer = place.layer(step)
            from_x = view(chunk, place.core, place.chip(x=1 - place.x, z=layer))
            sender.arrived(from_x, slot_of(chunk, 1, layer), sibling)
            if step < 2:
                sender.send(from_x, from_x, slot_of(chunk, 3, layer), place.device(y=1 - place.y))
            sender.send(from_x, from_x, slot_of(chunk, 5, layer), sibling)
            from_y = view(chunk, place.core, place.chip(y=1 - place.y, z=layer))
            sender.arrived(from_y, slot_of(chunk, 2, layer), sibling)
            if step >= 2:
                sender.send(from_y, from_y, slot_of(chunk, 3, layer), place.device(x=1 - place.x))
            sender.send(from_y, from_y, slot_of(chunk, 6, layer), sibling)

    def corner(chunk):
        for step in range(4):
            layer = place.layer(step)
            block = view(chunk, place.core, place.chip(x=1 - place.x, y=1 - place.y, z=layer))
            sender.arrived(block, slot_of(chunk, 3, layer), sibling)
            sender.send(block, block, slot_of(chunk, 7, layer), sibling)

    def twin(chunk):
        for step in range(4):
            layer = place.layer(step)
            for kind, x, y in ((4, 0, 0), (5, 1, 0), (6, 0, 1), (7, 1, 1)):
                chip = place.chip(
                    x=1 - place.x if x else place.x, y=1 - place.y if y else place.y, z=layer
                )
                sender.arrived(view(chunk, 1 - place.core, chip), slot_of(chunk, kind, layer), sibling)

    assemble(0)
    begin(0)
    assemble(1)
    begin(1)
    begin(2)
    for chunk in range(3):
        along(chunk)
        across(chunk)
        corner(chunk)
    for chunk in range(3):
        twin(chunk)
    sender.close()


def gather_weights(wide, tall, widths):
    owners = lax.axis_size(("tower", "batch"))
    rows = wide.shape[0] * 3 // 4
    return pl.pallas_call(
        functools.partial(gather_kernel, widths),
        out_shape=(
            jax.ShapeDtypeStruct((rows * owners, wide.shape[1]), wide.dtype),
            jax.ShapeDtypeStruct((tall.shape[0] * owners, tall.shape[1]), tall.dtype),
        ),
        in_specs=[pl.BlockSpec(memory_space=pltpu.VMEM)] * 2,
        out_specs=[pl.BlockSpec(memory_space=pltpu.VMEM)] * 2,
        scratch_shapes=[
            pltpu.VMEM((wide.shape[0], wide.shape[1] // 2), wide.dtype),
            pltpu.SemaphoreType.DMA((100,)),
            pltpu.SemaphoreType.DMA((108,)),
        ],
        compiler_params=pltpu.CompilerParams(
            collective_id=0, has_side_effects=True, vmem_limit_bytes=48 * 2**20
        ),
    )(wide, tall)


def cls_kernel(block_ref, out_ref, merged, stage, send_sems, recv_sems):
    place = Place()
    sender = Sender(send_sems, recv_sems)
    greet(place)
    rows, width = block_ref.shape
    half = width // 2
    sibling = place.device(core=1 - place.core)
    across_x = place.device(x=1 - place.x)
    mine = pl.ds(pl.multiple_of(place.core * half, 128), half)
    other = pl.ds(pl.multiple_of((1 - place.core) * half, 128), half)
    sender.send(block_ref.at[:, other], stage.at[0], 0, sibling)
    sender.arrived(stage.at[0], 0, sibling)
    merged[...] = (block_ref[:, mine].astype(jnp.float32) + stage[0].astype(jnp.float32)).astype(jnp.bfloat16)
    sender.send(merged, stage.at[1], 1, across_x)
    sender.arrived(stage.at[1], 1, across_x)

    def view(core, y, z):
        first = pl.multiple_of((z * 2 + y) * rows, 16)
        return out_ref.at[pl.ds(first, rows), pl.ds(pl.multiple_of(core * half, 128), half)]

    own = view(place.core, place.y, place.z)
    own[...] = (merged[...].astype(jnp.float32) + stage[1].astype(jnp.float32)).astype(jnp.bfloat16)
    for step in (3, 2, 1):
        sender.send(own, own, 2 + place.z, place.device(z=place.layer(step)))
    for step in range(4):
        layer = place.layer(step)
        block = view(place.core, place.y, layer)
        if step > 0:
            sender.arrived(block, 2 + layer, sibling)
        sender.send(block, block, 6 + layer, place.device(y=1 - place.y))
        sender.send(block, block, 10 + layer, sibling)
    for step in range(4):
        layer = place.layer(step)
        block = view(place.core, 1 - place.y, layer)
        sender.arrived(block, 6 + layer, sibling)
        sender.send(block, block, 14 + layer, sibling)
    for step in range(4):
        layer = place.layer(step)
        sender.arrived(view(1 - place.core, place.y, layer), 10 + layer, sibling)
        sender.arrived(view(1 - place.core, 1 - place.y, layer), 14 + layer, sibling)
    sender.close()


def gather_cls(block):
    rows, width = block.shape
    chips = lax.axis_size("batch") // 2
    return pl.pallas_call(
        cls_kernel,
        out_shape=jax.ShapeDtypeStruct((rows * chips, width), block.dtype),
        in_specs=[pl.BlockSpec(memory_space=pltpu.VMEM)],
        out_specs=pl.BlockSpec(memory_space=pltpu.VMEM),
        scratch_shapes=[
            pltpu.VMEM((rows, width // 2), block.dtype),
            pltpu.VMEM((2, rows, width // 2), block.dtype),
            pltpu.SemaphoreType.DMA((20,)),
            pltpu.SemaphoreType.DMA((18,)),
        ],
        compiler_params=pltpu.CompilerParams(
            collective_id=1, has_side_effects=True, vmem_limit_bytes=48 * 2**20
        ),
    )(block)


def scatter_kernel(part_ref, out_ref, work, stage_core, stage_pair, stage_z, final, stage_last, send_sems, recv_sems):
    place = Place()
    sender = Sender(send_sems, recv_sems)
    greet(place)
    half = part_ref.shape[1] // 2
    chip_rows = part_ref.shape[0] // 16
    sibling = place.device(core=1 - place.core)
    mine = pl.ds(pl.multiple_of(place.core * half, 128), half)
    other = pl.ds(pl.multiple_of((1 - place.core) * half, 128), half)
    other_x, other_y = place.device(x=1 - place.x), place.device(y=1 - place.y)

    def rows_of(x, y, z):
        return pl.ds(pl.multiple_of(place.chip(x, y, z) * chip_rows, 16), chip_rows)

    flips = [(1, 1), (1, 0), (0, 1), (0, 0)]
    blocks = [(dx, dy, z) for z in range(4) for dx, dy in flips]

    def target(dx, dy):
        return (1 - place.x if dx else place.x, 1 - place.y if dy else place.y)

    def rows_for(dx, dy, z):
        x, y = target(dx, dy)
        return rows_of(x, y, z)

    def first_dim(z):
        return 0 if z % 2 == 0 else 1

    for index, (dx, dy, z) in enumerate(blocks):
        rows = rows_for(dx, dy, z)
        sender.send(part_ref.at[rows, other], stage_core.at[index], index, sibling)
    base = 16
    for index, (dx, dy, z) in enumerate(blocks):
        sender.arrived(stage_core.at[index], index, sibling)
        rows = rows_for(dx, dy, z)
        total = part_ref[rows, mine].astype(jnp.float32) + stage_core[index].astype(jnp.float32)
        work[index] = total.astype(jnp.bfloat16)
        goes_first = dx if first_dim(z) == 0 else dy
        if goes_first:
            peer = other_x if first_dim(z) == 0 else other_y
            sender.send(work.at[index], stage_pair.at[index], base + index, peer)
    base_second = 32
    for z in range(4):
        dim = first_dim(z)
        for second in (1, 0):
            keep = (0, second) if dim == 0 else (second, 0)
            sent = (1, second) if dim == 0 else (second, 1)
            index = blocks.index((keep[0], keep[1], z))
            source = blocks.index((sent[0], sent[1], z))
            peer = other_x if dim == 0 else other_y
            sender.arrived(stage_pair.at[source], base + source, peer)
            work[index] = (work[index].astype(jnp.float32) + stage_pair[source].astype(jnp.float32)).astype(jnp.bfloat16)
            if second:
                peer = other_y if dim == 0 else other_x
                sender.send(work.at[index], stage_pair.at[index], base_second + index, peer)
    base_z = 48
    for z in range(4):
        dim = first_dim(z)
        crossed = (0, 1) if dim == 0 else (1, 0)
        source = blocks.index((crossed[0], crossed[1], z))
        index = blocks.index((0, 0, z))
        peer = other_y if dim == 0 else other_x
        sender.arrived(stage_pair.at[source], base_second + source, peer)
        work[index] = (work[index].astype(jnp.float32) + stage_pair[source].astype(jnp.float32)).astype(jnp.bfloat16)
    own_first = blocks.index((0, 0, 0))
    for step in (3, 2, 1):
        layer = place.layer(step)
        sender.send(work.at[own_first + layer * 4], stage_z.at[step], base_z + step, place.device(z=layer))
    total = work[own_first + place.z * 4].astype(jnp.float32)
    for step in (1, 2, 3):
        sender.arrived(stage_z.at[step], base_z + step, sibling)
        total = total + stage_z[step].astype(jnp.float32)
    dev_rows = chip_rows // 2
    first, second = total[:dev_rows], total[dev_rows:]
    is_first = place.core == 0
    keep = jnp.where(is_first, first, second)
    final[...] = jnp.where(is_first, second, first)
    sender.send(final, stage_last, base_z + 4, sibling)
    out_ref[:, mine] = keep
    sender.arrived(stage_last, base_z + 4, sibling)
    out_ref[:, other] = stage_last[...]
    sender.close()


def scatter_sums(part):
    rows, width = part.shape
    owners = lax.axis_size(("tower", "batch"))
    half = width // 2
    chip_rows = rows // 16
    return pl.pallas_call(
        scatter_kernel,
        out_shape=jax.ShapeDtypeStruct((rows // owners, width), jnp.float32),
        in_specs=[pl.BlockSpec(memory_space=pltpu.VMEM)],
        out_specs=pl.BlockSpec(memory_space=pltpu.VMEM),
        scratch_shapes=[
            pltpu.VMEM((16, chip_rows, half), jnp.bfloat16),
            pltpu.VMEM((16, chip_rows, half), jnp.bfloat16),
            pltpu.VMEM((16, chip_rows, half), jnp.bfloat16),
            pltpu.VMEM((4, chip_rows, half), jnp.bfloat16),
            pltpu.VMEM((rows // owners, half), jnp.float32),
            pltpu.VMEM((rows // owners, half), jnp.float32),
            pltpu.SemaphoreType.DMA((34,)),
            pltpu.SemaphoreType.DMA((56,)),
        ],
        compiler_params=pltpu.CompilerParams(
            collective_id=2, has_side_effects=True, vmem_limit_bytes=48 * 2**20
        ),
    )(part)


def fast(hidden_in, query_lengths, passage_lengths, positives, stored):
    (query_weight, query_bias, key_weight, value_weight, value_bias, output_weight, output_bias, first_gain,
     first_shift, inner_weight, inner_bias, outer_weight, outer_bias, second_gain, second_shift) = stored
    micro, token_rows, width = hidden_in.shape[0], hidden_in.shape[2], hidden_in.shape[3]
    inputs = hidden_in[:, 0]
    side = lax.axis_index("tower")
    batch = lax.axis_index("batch")
    device = side * lax.axis_size("batch") + batch
    is_query = side == 0
    own_rows = query_weight.shape[0]
    ff_rows = outer_weight.shape[0]
    ff = inner_weight.shape[1]
    head_size = width // HEADS
    scale = head_size ** (-0.5)
    vec_cols = jnp.stack(
        [query_bias, value_bias, output_bias, first_gain, first_shift, outer_bias, second_gain, second_shift], 1
    )
    vec_cols = jnp.concatenate([vec_cols, inner_bias.reshape(-1, own_rows).T], 1)
    vec_cols = jnp.pad(vec_cols, ((0, 0), (0, 128 - vec_cols.shape[1])))
    cut = width // 2
    inner_cut = 1152
    wide = jnp.concatenate(
        [query_weight, value_weight[:, :cut], vec_cols, key_weight, value_weight[:, cut:], jnp.zeros_like(vec_cols),
         output_weight, inner_weight], 1)
    wide = jnp.pad(wide, ((0, own_rows // 3), (0, 0)))
    widths = (width + cut + 128, width + inner_cut)
    all_wide, outer_mat = gather_weights(wide, outer_weight, widths)
    query_mat = all_wide[:, :width]
    vecs = all_wide[:, width + cut : width + cut + 12].astype(jnp.float32).T
    key_mat = all_wide[:, widths[0] : widths[0] + width]
    value_mat = jnp.concatenate(
        [all_wide[:, width : width + cut], all_wide[:, widths[0] + width : widths[0] + width + cut]], 1)
    out_mat = all_wide[:, 2 * widths[0] : 2 * widths[0] + width]
    inner_mat = all_wide[:, 2 * widths[0] + width :]
    query_vec, value_vec, out_vec, gain_one, shift_one, outer_vec, gain_two, shift_two = [vecs[i] for i in range(8)]
    inner_vec = vecs[8:12].reshape(ff // ff_rows, -1, own_rows) if False else (
        vecs[8:12].reshape(4, -1, own_rows).transpose(1, 0, 2).reshape(ff))
    params = (query_mat, query_vec, key_mat, value_mat, value_vec, out_mat, out_vec, gain_one, shift_one, inner_mat,
              inner_vec, outer_mat, outer_vec, gain_two, shift_two)

    slot_count = query_lengths.shape[1]
    passage_count = passage_lengths.shape[1]
    passage_part = jnp.pad(passage_lengths, ((0, 0), (0, slot_count - passage_count)))
    lengths = jnp.where(is_query, query_lengths, passage_part)
    labels, valid, starts, live = jax.vmap(segments, (0, None))(lengths, token_rows)
    flat = inputs.reshape(micro * token_rows, width)
    queries = (product(flat, query_mat) + query_vec).astype(jnp.bfloat16).reshape(micro, token_rows, HEADS, head_size)
    keys = product(flat, key_mat).astype(jnp.bfloat16).reshape(micro, token_rows, HEADS, head_size)
    values = (product(flat, value_mat) + value_vec).astype(jnp.bfloat16).reshape(micro, token_rows, HEADS, head_size)
    allowed = labels[:, None, :, None] == labels[:, None, None, :]
    scores = jnp.einsum("mqhd,mkhd->mhqk", queries, keys, preferred_element_type=jnp.float32) * scale
    scores = jnp.where(allowed, scores, MASKED)
    highest = jnp.max(scores, -1, keepdims=True)
    powers = jnp.exp(scores - highest)
    shares = (powers / jnp.sum(powers, -1, keepdims=True)).astype(jnp.bfloat16)
    attended = jnp.einsum("mhqk,mkhd->mqhd", shares, values, preferred_element_type=jnp.float32)
    attended = attended.astype(jnp.bfloat16).reshape(micro, token_rows, width)
    result, unused = tail(flat, attended.reshape(micro * token_rows, width), params)
    shown = jnp.where(valid.reshape(-1)[:, None], result, 0.0).astype(jnp.bfloat16)
    hidden_out = shown.reshape(micro, 1, token_rows, width)

    row_inputs = jnp.take_along_axis(inputs, starts[:, :, None], 1)
    row_attended = jnp.take_along_axis(attended, starts[:, :, None], 1)
    both = jnp.concatenate([row_inputs, row_attended], 2)
    query_block = jnp.concatenate([both[0], both[1], jnp.zeros((BLOCK - 2 * slot_count, 2 * width), both.dtype)], 0)
    coded = jnp.pad(positives.astype(both.dtype), ((0, 0), (0, 2 * width - slot_count)))
    passage_block = jnp.concatenate(
        [jnp.zeros((2 * slot_count, 2 * width), both.dtype), both[0, :passage_count], both[1, :passage_count], coded], 0)
    block = jnp.where(is_query, query_block, passage_block)
    nothing = jnp.zeros_like(block)
    first_core = batch % 2 == 0
    block = jnp.concatenate([jnp.where(first_core, block, nothing), jnp.where(first_core, nothing, block)], 0)
    cls = gather_cls(block)

    count = cls.shape[0]
    place = jnp.arange(count, dtype=jnp.int32) % BLOCK
    group = jnp.arange(count, dtype=jnp.int32) // BLOCK
    query_row = place < micro * slot_count
    passage_row = (place >= micro * slot_count) & (place < micro * (slot_count + passage_count))
    row_micro = jnp.where(query_row, place // slot_count, (place - micro * slot_count) // passage_count)
    used = query_row | passage_row
    codes = cls.reshape(-1, BLOCK, 2 * width)[:, micro * (slot_count + passage_count) :, :slot_count]
    codes = jnp.pad(codes.reshape(-1, micro * slot_count), ((0, 0), (0, BLOCK - micro * slot_count)))
    codes = codes.reshape(count).astype(jnp.int32)
    target_col = BLOCK * (codes // passage_count) + micro * slot_count + row_micro * passage_count + codes % passage_count
    cls_in = jnp.where(used[:, None], cls[:, :width], 0)
    cls_att = jnp.where(used[:, None], cls[:, width:], 0)
    result, kept = tail(cls_in, cls_att, params)
    normed_one, inverse_one, hidden_low, inner, active, normed_two, inverse_two = kept
    vectors = result.astype(jnp.bfloat16)
    cls_scale = width ** (-0.5)
    logits = product_nt(vectors, vectors) * cls_scale
    paired = query_row[:, None] & passage_row[None, :] & (row_micro[:, None] == row_micro[None, :])
    logits = jnp.where(paired, logits, MASKED)
    powers = jnp.where(paired, jnp.exp(logits - jnp.max(logits, -1, keepdims=True)), 0.0)
    total = jnp.sum(powers, -1, keepdims=True)
    hit = (jnp.arange(count, dtype=jnp.int32)[None, :] == target_col[:, None]) & paired
    grad_logits = (powers / jnp.where(total > 0, total, 1.0) - hit.astype(jnp.float32)) / micro
    grad_logits = grad_logits.astype(jnp.bfloat16)
    upstream = (product(grad_logits, vectors) + product_tn(grad_logits, vectors)) * cls_scale

    grad_sum_two, grad_gain_two, grad_shift_two = normalize_back(upstream, normed_two, inverse_two, gain_two)
    grad_outer = grad_sum_two.astype(jnp.bfloat16)
    grad_outer_vec = jnp.sum(grad_outer.astype(jnp.float32), 0)
    grad_inner = (product_nt(grad_outer, outer_mat) * gelu_slope(inner)).astype(jnp.bfloat16)
    grad_inner_vec = jnp.sum(grad_inner.astype(jnp.float32), 0)
    grad_hidden = grad_sum_two + product_nt(grad_inner, inner_mat)
    grad_sum_one, grad_gain_one, grad_shift_one = normalize_back(grad_hidden, normed_one, inverse_one, gain_one)
    grad_branch = grad_sum_one.astype(jnp.bfloat16)
    grad_out_vec = jnp.sum(grad_branch.astype(jnp.float32), 0)

    def own_columns(array, columns):
        return lax.dynamic_slice_in_dim(array, device * columns, columns, 1)

    def own_part(vector, length):
        return lax.dynamic_slice_in_dim(vector, device * length, length, 0)

    grad_outer_mat = product_tn(own_columns(active, ff_rows), grad_outer)
    grad_inner_mat = product_tn(own_columns(hidden_low, own_rows), grad_inner)
    grad_out_mat = product_tn(own_columns(cls_att, own_rows), grad_branch)

    def own_slots(array):
        rows = lax.dynamic_slice_in_dim(array, batch * BLOCK, BLOCK, 0)
        ours = rows[: micro * slot_count].reshape(micro, slot_count, width)
        theirs = rows[micro * slot_count : micro * (slot_count + passage_count)].reshape(micro, passage_count, width)
        theirs = jnp.pad(theirs, ((0, 0), (0, slot_count - passage_count), (0, 0)))
        return jnp.where(live[:, :, None], jnp.where(is_query, ours, theirs), 0)

    own_branch = own_slots(grad_branch)
    own_sum_one = own_slots(grad_sum_one)
    grad_attended = product_nt(own_branch.reshape(-1, width), out_mat).astype(jnp.bfloat16)
    grad_attended = grad_attended.reshape(micro, slot_count, HEADS, head_size)
    row_queries = jnp.take_along_axis(queries, starts[:, :, None, None], 1)
    row_labels = jnp.take_along_axis(labels, starts, 1)
    row_allowed = row_labels[:, None, :, None] == labels[:, None, None, :]
    scores = jnp.einsum("mrhd,mthd->mhrt", row_queries, keys, preferred_element_type=jnp.float32) * scale
    scores = jnp.where(row_allowed, scores, MASKED)
    powers = jnp.exp(scores - jnp.max(scores, -1, keepdims=True))
    shares = powers / jnp.sum(powers, -1, keepdims=True)
    shares_low = shares.astype(jnp.bfloat16)
    grad_shares = jnp.einsum("mrhd,mthd->mhrt", grad_attended, values, preferred_element_type=jnp.float32)
    grad_scores = (shares * (grad_shares - jnp.sum(grad_shares * shares, -1, keepdims=True))).astype(jnp.bfloat16)
    grad_queries = jnp.einsum("mhrt,mthd->mrhd", grad_scores, keys, preferred_element_type=jnp.float32) * scale
    grad_queries = grad_queries.astype(jnp.bfloat16).reshape(micro, slot_count, width)
    grad_keys = jnp.einsum("mhrt,mrhd->mthd", grad_scores, row_queries, preferred_element_type=jnp.float32) * scale
    grad_keys = grad_keys.astype(jnp.bfloat16).reshape(micro * token_rows, width)
    grad_values = jnp.einsum("mhrt,mrhd->mthd", shares_low, grad_attended, preferred_element_type=jnp.float32)
    grad_values = grad_values.astype(jnp.bfloat16).reshape(micro * token_rows, width)
    grad_inputs = product_nt(grad_keys, key_mat) + product_nt(grad_values, value_mat)
    grad_rows = product_nt(grad_queries.reshape(-1, width), query_mat) + own_sum_one.reshape(-1, width)
    row_index = (starts + jnp.arange(micro, dtype=jnp.int32)[:, None] * token_rows).reshape(-1)
    grad_inputs = grad_inputs.at[row_index].add(grad_rows)
    input_grad = grad_inputs.astype(jnp.bfloat16).reshape(micro, 1, token_rows, width)
    lanes = jnp.arange(128, dtype=jnp.int32)[None, :]
    flat_queries = grad_queries.reshape(-1, width)
    sums = product_tn(flat_queries, jnp.broadcast_to(lanes == 0, (flat_queries.shape[0], 128)).astype(jnp.bfloat16))
    sums = sums + product_tn(grad_values, jnp.broadcast_to(lanes == 1, (grad_values.shape[0], 128)).astype(jnp.bfloat16))
    partial = jnp.concatenate(
        [product_tn(row_inputs.reshape(-1, width), flat_queries), product_tn(flat, grad_keys),
         product_tn(flat, grad_values), sums, jnp.zeros_like(sums)], 1).astype(jnp.bfloat16)
    shard = scatter_sums(partial)
    return (
        hidden_out,
        input_grad,
        shard[:, :width],
        shard[:, 3 * width],
        shard[:, width : 2 * width],
        shard[:, 2 * width : 3 * width],
        shard[:, 3 * width + 1],
        grad_out_mat,
        own_part(grad_out_vec, own_rows),
        own_part(grad_gain_one, own_rows),
        own_part(grad_shift_one, own_rows),
        grad_inner_mat,
        own_part(grad_inner_vec, ff_rows),
        grad_outer_mat,
        own_part(grad_outer_vec, own_rows),
        own_part(grad_gain_two, own_rows),
        own_part(grad_shift_two, own_rows),
    )


def local(
    hidden_in,
    query_lengths,
    passage_lengths,
    positives,
    query_weight,
    query_bias,
    key_weight,
    value_weight,
    value_bias,
    output_weight,
    output_bias,
    first_gain,
    first_shift,
    inner_weight,
    inner_bias,
    outer_weight,
    outer_bias,
    second_gain,
    second_shift,
):
    stored = (
        query_weight,
        query_bias,
        key_weight,
        value_weight,
        value_bias,
        output_weight,
        output_bias,
        first_gain,
        first_shift,
        inner_weight,
        inner_bias,
        outer_weight,
        outer_bias,
        second_gain,
        second_shift,
    )
    if lax.axis_size("tower") == 2 and lax.axis_size("batch") == 16 and hidden_in.shape[3] == 768:
        return fast(hidden_in, query_lengths, passage_lengths, positives, stored)
    micro = hidden_in.shape[0]
    width = hidden_in.shape[3]
    cls_scale = width ** (-0.5)
    side = lax.axis_index("tower")
    is_query = side == 0
    slot_count = query_lengths.shape[1]
    passage_count = passage_lengths.shape[1]
    half_count = (slot_count + 1) // 2
    extra_rows = 2 * half_count - slot_count
    owners = lax.axis_size(("tower", "batch"))
    totals = tuple(
        (jnp.zeros((item.shape[0] * owners,) + item.shape[1:], jnp.float32) for item in stored)
    )
    half_totals = tuple(
        (jnp.zeros((item.shape[0] * owners // 2,) + item.shape[1:], jnp.float32) for item in stored)
    )
    shown_list = []
    grad_list = []
    for micro_step in range(micro):
        gathered = (
            lax.all_gather(query_weight, ("tower", "batch"), axis=0, tiled=True),
            lax.all_gather(query_bias, ("tower", "batch"), axis=0, tiled=True),
            lax.all_gather(key_weight, ("tower", "batch"), axis=0, tiled=True),
            lax.all_gather(value_weight, ("tower", "batch"), axis=0, tiled=True),
            lax.all_gather(value_bias, ("tower", "batch"), axis=0, tiled=True),
            lax.all_gather(output_weight, ("tower", "batch"), axis=0, tiled=True),
            lax.all_gather(output_bias, ("tower", "batch"), axis=0, tiled=True),
            lax.all_gather(first_gain, ("tower", "batch"), axis=0, tiled=True),
            lax.all_gather(first_shift, ("tower", "batch"), axis=0, tiled=True),
            lax.all_gather(inner_weight, ("tower", "batch"), axis=0, tiled=True),
            lax.all_gather(inner_bias, ("tower", "batch"), axis=0, tiled=True),
            lax.all_gather(outer_weight, ("tower", "batch"), axis=0, tiled=True),
            lax.all_gather(outer_bias, ("tower", "batch"), axis=0, tiled=True),
            lax.all_gather(second_gain, ("tower", "batch"), axis=0, tiled=True),
            lax.all_gather(second_shift, ("tower", "batch"), axis=0, tiled=True),
        )
        params = cast_params(gathered)
        inputs = hidden_in[micro_step, 0]
        passage_part = jnp.pad(passage_lengths[micro_step], (0, slot_count - passage_count))
        lengths = jnp.where(is_query, query_lengths[micro_step], passage_part)
        labels, valid, starts, live = segments(lengths, inputs.shape[0])
        saved, shown = forward(inputs, labels, valid, params)
        shown_list.append(shown)
        mine = jnp.where(live[:, None], shown[starts], 0.0)
        partner = partner_2(mine, "tower", 0)
        query_cls = jnp.where(is_query, mine, partner)
        passage_cls = jnp.where(is_query, partner, mine)[:passage_count]
        pooled = lax.all_gather(passage_cls, "batch", axis=0, tiled=True)
        padded_queries = jnp.pad(query_cls, ((0, extra_rows), (0, 0)))
        padded_targets = jnp.pad(positives[micro_step], (0, extra_rows))
        my_queries = lax.dynamic_slice_in_dim(padded_queries, side * half_count, half_count, 0)
        my_targets = lax.dynamic_slice_in_dim(padded_targets, side * half_count, half_count, 0)
        logits = product_nt(my_queries, pooled) * cls_scale
        highest = jnp.max(logits, -1, keepdims=True)
        powers = jnp.exp(logits - highest)
        shares = powers / jnp.sum(powers, -1, keepdims=True)
        columns = jnp.arange(pooled.shape[0], dtype=jnp.int32)
        target = (columns[None, :] == my_targets[:, None]).astype(jnp.float32)
        grad_logits = ((shares - target) / micro).astype(jnp.bfloat16)
        own_grad = product(grad_logits, pooled) * cls_scale
        pooled_grad = product_tn(grad_logits, my_queries) * cls_scale
        summed = lax.psum_scatter(pooled_grad, "batch", scatter_dimension=0, tiled=True)
        other_queries, other_passages = (
            partner_2(own_grad.astype(jnp.bfloat16), "tower", 0).astype(own_grad.dtype),
            partner_2(summed.astype(jnp.bfloat16), "tower", 0).astype(summed.dtype),
        )
        query_grad = jnp.concatenate([own_grad, other_queries], 0)[:slot_count]
        passage_grad = jnp.pad(summed + other_passages, ((0, slot_count - passage_count), (0, 0)))
        cotangent = jnp.where(is_query, query_grad, passage_grad)
        input_part, step_grads = backward(inputs, labels, cotangent, starts, live, saved, params)
        grad_list.append(input_part)
        totals = tuple((first + second for first, second in zip(totals, step_grads)))
    keep_all, give_all = split_halves(totals, side)
    came_all = jax.tree.map(
        lambda part, own: part.astype(own.dtype), partner_2(as_sent(give_all), "tower", 0), give_all
    )
    half_totals = tuple((first + second for first, second in zip(keep_all, came_all)))
    shards = lax.psum_scatter(half_totals, "batch", scatter_dimension=0, tiled=True)
    hidden_out = jnp.stack(shown_list)[:, None]
    input_grad = jnp.stack(grad_list)[:, None]
    return (
        hidden_out,
        input_grad,
        shards[0],
        shards[1],
        shards[2],
        shards[3],
        shards[4],
        shards[5],
        shards[6],
        shards[7],
        shards[8],
        shards[9],
        shards[10],
        shards[11],
        shards[12],
        shards[13],
        shards[14],
    )


def solution(mesh):
    placed = (
        P(None, "tower", "batch", None),
        P(None, "batch"),
        P(None, "batch"),
        P(None, "batch"),
        P(("tower", "batch"), None),
        P(("tower", "batch")),
        P(("tower", "batch"), None),
        P(("tower", "batch"), None),
        P(("tower", "batch")),
        P(("tower", "batch"), None),
        P(("tower", "batch")),
        P(("tower", "batch")),
        P(("tower", "batch")),
        P(("tower", "batch"), None),
        P(("tower", "batch")),
        P(("tower", "batch"), None),
        P(("tower", "batch")),
        P(("tower", "batch")),
        P(("tower", "batch")),
    )
    return jax.shard_map(
        local,
        mesh=mesh,
        in_specs=placed,
        out_specs=(
            P(None, "tower", "batch", None),
            P(None, "tower", "batch", None),
            P(("tower", "batch"), None),
            P(("tower", "batch")),
            P(("tower", "batch"), None),
            P(("tower", "batch"), None),
            P(("tower", "batch")),
            P(("tower", "batch"), None),
            P(("tower", "batch")),
            P(("tower", "batch")),
            P(("tower", "batch")),
            P(("tower", "batch"), None),
            P(("tower", "batch")),
            P(("tower", "batch"), None),
            P(("tower", "batch")),
            P(("tower", "batch")),
            P(("tower", "batch")),
        ),
        check_vma=False,
    )
```

```python
import jax
import jax.numpy as jnp
from jax import lax
from jax.experimental import pallas as pl
from jax.experimental.pallas import tpu as pltpu
from jax.sharding import PartitionSpec as P

HEADS = 12


EPSILON = 1e-12
MASKED = -1e30


def partner_2(x, axis, apart):
    return lax.ppermute(x, axis, [(i, i ^ 1 << apart) for i in range(lax.axis_size(axis))])


def as_sent(x):
    return jax.tree.map(lambda a: a.astype(jnp.bfloat16) if a.dtype == jnp.float32 else a, x)


def product(left, right):
    return jnp.dot(left, right, preferred_element_type=jnp.float32)


def product_tn(left, right):
    return jnp.einsum("ta,tb->ab", left, right, preferred_element_type=jnp.float32)


def product_nt(left, right):
    return jnp.einsum("ra,ba->rb", left, right, preferred_element_type=jnp.float32)


def normalize(values, gains, shifts):
    average = jnp.mean(values, -1, keepdims=True)
    centred = values - average
    inverse = lax.rsqrt(jnp.mean(centred * centred, -1, keepdims=True) + EPSILON)
    normed = centred * inverse
    return (normed * gains + shifts, normed, inverse)


def normalize_back(upstream, normed, inverse, gains):
    scaled = upstream * gains
    inner = (
        scaled
        - jnp.mean(scaled, -1, keepdims=True)
        - normed * jnp.mean(scaled * normed, -1, keepdims=True)
    )
    return (inner * inverse, jnp.sum(upstream * normed, 0), jnp.sum(upstream, 0))


def gelu_slope(values):
    return (
        0.5 * (1.0 + lax.erf(values * 0.7071067811865476))
        + values * jnp.exp(-0.5 * values * values) * 0.3989422804014327
    )


def segments(lengths, token_rows):
    ends = jnp.cumsum(lengths)
    places = jnp.arange(token_rows, dtype=jnp.int32)
    labels = jnp.sum((places[:, None] >= ends[None, :]).astype(jnp.int32), 1)
    starts = jnp.minimum(ends - lengths, token_rows - 1)
    return (labels, places < ends[-1], starts, lengths > 0)


def tail(inputs, attended, params):
    out_mat, out_vec, gain_one, shift_one = (params[5], params[6], params[7], params[8])
    inner_mat, inner_vec, outer_mat, outer_vec, gain_two, shift_two = params[9:15]
    branch = product(attended, out_mat) + out_vec
    hidden_full, normed_one, inverse_one = normalize(
        inputs.astype(jnp.float32) + branch, gain_one, shift_one
    )
    hidden_low = hidden_full.astype(jnp.bfloat16)
    inner = product(hidden_low, inner_mat) + inner_vec
    active = jax.nn.gelu(inner, approximate=False).astype(jnp.bfloat16)
    outer = product(active, outer_mat) + outer_vec
    result, normed_two, inverse_two = normalize(
        hidden_low.astype(jnp.float32) + outer, gain_two, shift_two
    )
    return (result, (normed_one, inverse_one, hidden_low, inner, active, normed_two, inverse_two))


def forward(inputs, labels, valid, params):
    query_mat, query_vec, key_mat, value_mat, value_vec = params[0:5]
    token_rows, width = inputs.shape
    head_size = width // HEADS
    scale = head_size ** (-0.5)
    queries = (product(inputs, query_mat) + query_vec).astype(jnp.bfloat16)
    keys = product(inputs, key_mat).astype(jnp.bfloat16)
    values = (product(inputs, value_mat) + value_vec).astype(jnp.bfloat16)
    block_rows = min(512, token_rows)

    def one_block(first_row):
        allowed = labels[:, None] == labels[None, :]

        def one_head(head_index):
            head_queries = lax.dynamic_slice_in_dim(queries, head_index * head_size, head_size, 1)
            head_keys = lax.dynamic_slice_in_dim(keys, head_index * head_size, head_size, 1)
            head_values = lax.dynamic_slice_in_dim(values, head_index * head_size, head_size, 1)
            scores = jnp.where(allowed, product_nt(head_queries, head_keys) * scale, MASKED)
            highest = jnp.max(scores, -1, keepdims=True)
            powers = jnp.exp(scores - highest)
            totals = jnp.sum(powers, -1, keepdims=True)
            shares = (powers / totals).astype(jnp.bfloat16)
            return (product(shares, head_values), (highest + jnp.log(totals))[:, 0])

        head_out, head_lse = lax.map(one_head, jnp.arange(HEADS, dtype=jnp.int32))
        attended = (
            jnp.transpose(head_out, (1, 0, 2)).reshape(block_rows, width).astype(jnp.bfloat16)
        )
        result, unused = tail(inputs, attended, params)
        shown = jnp.where(valid[:, None], result, 0.0).astype(jnp.bfloat16)
        return (attended, head_lse, shown)

    firsts = jnp.arange(token_rows // block_rows, dtype=jnp.int32) * block_rows
    attended, lse_blocks, shown = lax.map(one_block, firsts)
    attended = attended.reshape(token_rows, width)
    shown = shown.reshape(token_rows, width)
    lse_all = jnp.transpose(lse_blocks, (1, 0, 2)).reshape(HEADS, token_rows)
    return ((queries, keys, values, attended, lse_all), shown)


def backward(inputs, labels, cotangent, starts, live, saved, params):
    queries, keys, values, attended, lse_all = saved
    query_mat, key_mat, value_mat, out_mat = (params[0], params[2], params[3], params[5])
    gain_one, inner_mat, outer_mat, gain_two = (params[7], params[9], params[11], params[13])
    token_rows, width = inputs.shape
    head_size = width // HEADS
    scale = head_size ** (-0.5)
    slot_count = starts.shape[0]
    row_inputs = inputs[starts]
    row_attended = attended[starts]
    unused, kept = tail(row_inputs, row_attended, params)
    normed_one, inverse_one, hidden_low, inner, active, normed_two, inverse_two = kept
    upstream = jnp.where(live[:, None], cotangent, 0.0)
    grad_sum_two, grad_gain_two, grad_shift_two = normalize_back(
        upstream, normed_two, inverse_two, gain_two
    )
    grad_outer = grad_sum_two.astype(jnp.bfloat16)
    grad_outer_mat = product_tn(active, grad_outer)
    grad_outer_vec = jnp.sum(grad_outer.astype(jnp.float32), 0)
    grad_inner = (product_nt(grad_outer, outer_mat) * gelu_slope(inner)).astype(jnp.bfloat16)
    grad_inner_mat = product_tn(hidden_low, grad_inner)
    grad_inner_vec = jnp.sum(grad_inner.astype(jnp.float32), 0)
    grad_hidden = grad_sum_two + product_nt(grad_inner, inner_mat)
    grad_sum_one, grad_gain_one, grad_shift_one = normalize_back(
        grad_hidden, normed_one, inverse_one, gain_one
    )
    grad_branch = grad_sum_one.astype(jnp.bfloat16)
    grad_out_mat = product_tn(row_attended, grad_branch)
    grad_out_vec = jnp.sum(grad_branch.astype(jnp.float32), 0)
    grad_attended = (
        product_nt(grad_branch, out_mat).astype(jnp.bfloat16).reshape(slot_count, HEADS, head_size)
    )
    row_queries = queries[starts].reshape(slot_count, HEADS, head_size)
    keys_split = keys.reshape(token_rows, HEADS, head_size)
    values_split = values.reshape(token_rows, HEADS, head_size)
    allowed = labels[starts][None, :, None] == labels[None, None, :]
    scores = (
        jnp.einsum("rhd,thd->hrt", row_queries, keys_split, preferred_element_type=jnp.float32)
        * scale
    )
    shares = jnp.where(allowed, jnp.exp(scores - lse_all[:, starts][:, :, None]), 0.0)
    shares_low = shares.astype(jnp.bfloat16)
    grad_shares = jnp.einsum(
        "rhd,thd->hrt", grad_attended, values_split, preferred_element_type=jnp.float32
    )
    grad_scores = (
        shares * (grad_shares - jnp.sum(grad_shares * shares, -1, keepdims=True))
    ).astype(jnp.bfloat16)
    grad_queries = (
        jnp.einsum("hrt,thd->rhd", grad_scores, keys_split, preferred_element_type=jnp.float32)
        * scale
    )
    grad_queries = grad_queries.reshape(slot_count, width).astype(jnp.bfloat16)
    grad_keys = (
        jnp.einsum("hrt,rhd->thd", grad_scores, row_queries, preferred_element_type=jnp.float32)
        * scale
    )
    grad_keys = grad_keys.reshape(token_rows, width).astype(jnp.bfloat16)
    grad_values = jnp.einsum(
        "hrt,rhd->thd", shares_low, grad_attended, preferred_element_type=jnp.float32
    )
    grad_values = grad_values.reshape(token_rows, width).astype(jnp.bfloat16)
    grad_inputs = product_nt(grad_keys, key_mat) + product_nt(grad_values, value_mat)
    grad_inputs = grad_inputs.at[starts].add(product_nt(grad_queries, query_mat) + grad_sum_one)
    grads = (
        product_tn(row_inputs, grad_queries),
        jnp.sum(grad_queries.astype(jnp.float32), 0),
        product_tn(inputs, grad_keys),
        product_tn(inputs, grad_values),
        jnp.sum(grad_values.astype(jnp.float32), 0),
        grad_out_mat,
        grad_out_vec,
        grad_gain_one,
        grad_shift_one,
        grad_inner_mat,
        grad_inner_vec,
        grad_outer_mat,
        grad_outer_vec,
        grad_gain_two,
        grad_shift_two,
    )
    return (grad_inputs.astype(jnp.bfloat16), grads)


def cast_params(gathered):
    vector_places = (1, 4, 6, 7, 8, 10, 12, 13, 14)
    return tuple(
        (
            item.astype(jnp.float32) if place in vector_places else item
            for place, item in enumerate(gathered)
        )
    )


def split_halves(grads, side):
    keep_list = []
    give_list = []
    for item in grads:
        half = item.shape[0] // 2
        keep_list.append(lax.dynamic_slice_in_dim(item, side * half, half, 0))
        give_list.append(lax.dynamic_slice_in_dim(item, (1 - side) * half, half, 0))
    return (tuple(keep_list), tuple(give_list))


MESH = pl.DeviceIdType.MESH
BLOCK = 40
QS, PS, STREAM, WIDTH, FF, MICRO = 17, 2, 512, 768, 3072, 2
ROWS = MICRO * STREAM
CLS = 16 * BLOCK
HALF = 1280
PART = (HALF, 1920)
OWN = 24
FF_OWN = 96
BF, F32 = jnp.bfloat16, jnp.float32


class Place:
    def __init__(self):
        self.x = lax.axis_index("tower")
        self.batch = lax.axis_index("batch")
        self.core = self.batch % 2
        self.y = (self.batch // 2) % 2
        self.z = self.batch // 4
        self.index = self.x * 16 + self.batch

    def device(self, x=None, y=None, z=None, core=None):
        x = self.x if x is None else x
        y = self.y if y is None else y
        z = self.z if z is None else z
        core = self.core if core is None else core
        return (x, z * 4 + y * 2 + core)

    def chip(self, x=None, y=None, z=None):
        x = self.x if x is None else x
        y = self.y if y is None else y
        z = self.z if z is None else z
        return x * 8 + z * 2 + y

    def layer(self, step):
        if step == 0:
            return self.z
        if step == 1:
            return self.z + 1 - 2 * (self.z % 2)
        if step == 2:
            return (self.z + 2) % 4
        return 3 - self.z

    @property
    def sibling(self):
        return self.device(core=1 - self.core)

    @property
    def over_x(self):
        return self.device(x=1 - self.x)

    @property
    def over_y(self):
        return self.device(y=1 - self.y)


def greet(place):
    barrier = pltpu.get_barrier_semaphore()
    peers = [place.device(z=place.layer(step)) for step in (1, 2, 3)]
    peers += [place.over_x, place.over_y, place.sibling]
    for peer in peers:
        pl.semaphore_signal(barrier, inc=1, device_id=peer, device_id_type=MESH)
    pl.semaphore_wait(barrier, len(peers))


class Sender:
    def __init__(self, place, send_sems, recv_sems):
        self.place = place
        self.send_sems = send_sems
        self.recv_sems = recv_sems
        self.used = 0
        self.open = []

    def send(self, src, dst, slot, peer):
        copy = pltpu.make_async_remote_copy(
            src_ref=src,
            dst_ref=dst,
            send_sem=self.send_sems.at[self.used],
            recv_sem=self.recv_sems.at[slot],
            device_id=peer,
            device_id_type=MESH,
        )
        self.used += 1
        copy.start()
        self.open.append(copy)

    def arrived(self, dst, slot):
        pltpu.make_async_remote_copy(
            src_ref=dst,
            dst_ref=dst,
            send_sem=self.send_sems.at[0],
            recv_sem=self.recv_sems.at[slot],
            device_id=self.place.sibling,
            device_id_type=MESH,
        ).wait_recv()

    def close(self):
        for copy in self.open:
            copy.wait_send()
        self.open = []


def tile(index, size, unit):
    return pl.ds(pl.multiple_of(index * unit, unit), size)


def loop(count, body):
    def step(index, carry):
        body(index)
        return carry

    lax.fori_loop(0, count, step, 0)


def dot(left, right):
    return jnp.dot(left, right, preferred_element_type=F32)


def dot_nt(left, right):
    return lax.dot_general(left, right, (((1,), (1,)), ((), ())), preferred_element_type=F32)


def dot_tn(left, right):
    return lax.dot_general(left, right, (((0,), (0,)), ((), ())), preferred_element_type=F32)


def iota(shape, dim):
    return lax.broadcasted_iota(jnp.int32, shape, dim)


def centre(values):
    average = jnp.mean(values, -1, keepdims=True)
    centred = values - average
    inverse = lax.rsqrt(jnp.mean(centred * centred, -1, keepdims=True) + EPSILON)
    return centred * inverse, inverse


def centre_back(scaled, normed, inverse):
    return inverse * (
        scaled - jnp.mean(scaled, -1, keepdims=True) - normed * jnp.mean(scaled * normed, -1, keepdims=True)
    )


def weight_steps(place, sender, all_wide, all_tall):
    def view(chunk, core, chip):
        if chunk < 2:
            first = pl.multiple_of((0, 2 * HALF)[chunk] + core * PART[chunk], 128)
            return all_wide.at[tile(chip, 2 * OWN, 2 * OWN), pl.ds(first, PART[chunk])]
        return all_tall.at[tile(chip * 2 + core, FF_OWN, FF_OWN), :]

    def slot(chunk, kind, layer):
        return (chunk * 8 + kind) * 4 + layer

    def begin(chunk):
        own = view(chunk, place.core, place.chip())
        for step in (3, 2, 1):
            sender.send(own, own, slot(chunk, 0, place.z), place.device(z=place.layer(step)))
        sender.send(own, own, slot(chunk, 1, place.z), place.over_x)
        sender.send(own, own, slot(chunk, 2, place.z), place.over_y)
        sender.send(own, own, slot(chunk, 4, place.z), place.sibling)

    def along(chunk):
        for step in (1, 2, 3):
            layer = place.layer(step)
            block = view(chunk, place.core, place.chip(z=layer))
            sender.arrived(block, slot(chunk, 0, layer))
            sender.send(block, block, slot(chunk, 1, layer), place.over_x)
            sender.send(block, block, slot(chunk, 2, layer), place.over_y)
            sender.send(block, block, slot(chunk, 4, layer), place.sibling)
            yield

    def across(chunk):
        for step in range(4):
            layer = place.layer(step)
            from_x = view(chunk, place.core, place.chip(x=1 - place.x, z=layer))
            sender.arrived(from_x, slot(chunk, 1, layer))
            if step < 2:
                sender.send(from_x, from_x, slot(chunk, 3, layer), place.over_y)
            sender.send(from_x, from_x, slot(chunk, 5, layer), place.sibling)
            from_y = view(chunk, place.core, place.chip(y=1 - place.y, z=layer))
            sender.arrived(from_y, slot(chunk, 2, layer))
            if step >= 2:
                sender.send(from_y, from_y, slot(chunk, 3, layer), place.over_x)
            sender.send(from_y, from_y, slot(chunk, 6, layer), place.sibling)
            yield

    def corner(chunk):
        for step in range(4):
            layer = place.layer(step)
            block = view(chunk, place.core, place.chip(x=1 - place.x, y=1 - place.y, z=layer))
            sender.arrived(block, slot(chunk, 3, layer))
            sender.send(block, block, slot(chunk, 7, layer), place.sibling)
            yield

    def twin(chunk):
        for step in range(4):
            layer = place.layer(step)
            for kind, x, y in ((4, 0, 0), (5, 1, 0), (6, 0, 1), (7, 1, 1)):
                chip = place.chip(x=1 - place.x if x else place.x, y=1 - place.y if y else place.y, z=layer)
                sender.arrived(view(chunk, 1 - place.core, chip), slot(chunk, kind, layer))
        yield

    return begin, along, across, corner, twin


def cls_steps(place, sender, base, block_ref, merged, stage, out_ref):
    rows, half = 2 * BLOCK, WIDTH
    mine = tile(place.core, half, half)
    other = tile(1 - place.core, half, half)

    def view(core, y, z):
        return out_ref.at[tile(z * 2 + y, rows, rows), tile(core, half, half)]

    sender.send(block_ref.at[:, other], stage.at[0], base, place.sibling)
    yield
    sender.arrived(stage.at[0], base)
    merged[...] = (block_ref[:, mine].astype(F32) + stage[0].astype(F32)).astype(BF)
    sender.send(merged, stage.at[1], base + 1, place.over_x)
    yield
    sender.arrived(stage.at[1], base + 1)
    own = view(place.core, place.y, place.z)
    own[...] = (merged[...].astype(F32) + stage[1].astype(F32)).astype(BF)
    for step in (3, 2, 1):
        sender.send(own, own, base + 2 + place.z, place.device(z=place.layer(step)))
    for step in range(4):
        layer = place.layer(step)
        block = view(place.core, place.y, layer)
        if step > 0:
            yield
            sender.arrived(block, base + 2 + layer)
        sender.send(block, block, base + 6 + layer, place.over_y)
        sender.send(block, block, base + 10 + layer, place.sibling)
    for step in range(4):
        yield
        layer = place.layer(step)
        block = view(place.core, 1 - place.y, layer)
        sender.arrived(block, base + 6 + layer)
        sender.send(block, block, base + 14 + layer, place.sibling)
    yield
    for step in range(4):
        layer = place.layer(step)
        sender.arrived(view(1 - place.core, place.y, layer), base + 10 + layer)
        sender.arrived(view(1 - place.core, 1 - place.y, layer), base + 14 + layer)


def sum_steps(place, sender, base, part_ref, work, stage_core, stage_pair, stage_z, final, stage_last, out_ref):
    mine = tile(place.core, HALF, HALF)
    other = tile(1 - place.core, HALF, HALF)
    blocks = [(dx, dy, z) for z in range(4) for dx, dy in ((1, 1), (1, 0), (0, 1), (0, 0))]

    def rows_of(dx, dy, z):
        chip = place.chip(1 - place.x if dx else place.x, 1 - place.y if dy else place.y, z)
        return tile(chip, 2 * OWN, 2 * OWN)

    def add(index, landed):
        work[index] = (work[index].astype(F32) + landed.astype(F32)).astype(BF)

    for index, (dx, dy, z) in enumerate(blocks):
        sender.send(part_ref.at[rows_of(dx, dy, z), other], stage_core.at[index], base + index, place.sibling)
    for index, (dx, dy, z) in enumerate(blocks):
        if index % 4 == 0:
            yield
        sender.arrived(stage_core.at[index], base + index)
        work[index] = (part_ref[rows_of(dx, dy, z), mine].astype(F32) + stage_core[index].astype(F32)).astype(BF)
        if (dx if z % 2 == 0 else dy) == 1:
            sender.send(work.at[index], stage_pair.at[index], base + 16 + index, place.over_x if z % 2 == 0 else place.over_y)
    for z in range(4):
        yield
        for second in (1, 0):
            keep = (0, second) if z % 2 == 0 else (second, 0)
            sent = (1, second) if z % 2 == 0 else (second, 1)
            index, source = blocks.index(keep + (z,)), blocks.index(sent + (z,))
            sender.arrived(stage_pair.at[source], base + 16 + source)
            add(index, stage_pair[source])
            if second:
                peer = place.over_y if z % 2 == 0 else place.over_x
                sender.send(work.at[index], stage_pair.at[index], base + 32 + index, peer)
    first = blocks.index((0, 0, 0))
    for z in range(4):
        yield
        source = blocks.index(((0, 1) if z % 2 == 0 else (1, 0)) + (z,))
        sender.arrived(stage_pair.at[source], base + 32 + source)
        add(first + 4 * z, stage_pair[source])
    for step in (3, 2, 1):
        layer = place.layer(step)
        sender.send(work.at[first + layer * 4], stage_z.at[step], base + 48 + step, place.device(z=layer))
    yield
    total = work[first + place.z * 4].astype(F32)
    for step in (1, 2, 3):
        sender.arrived(stage_z.at[step], base + 48 + step)
        total = total + stage_z[step].astype(F32)
    top, low = total[:OWN], total[OWN:]
    is_first = place.core == 0
    final[...] = jnp.where(is_first, low, top)
    sender.send(final, stage_last, base + 52, place.sibling)
    out_ref[:, mine] = jnp.where(is_first, top, low)
    yield
    sender.arrived(stage_last, base + 52)
    out_ref[:, other] = stage_last[...]


def run(steps, count=None):
    while count is None or count > 0:
        if next(steps, "end") == "end":
            return
        if count is not None:
            count -= 1


def layer_kernel(
    x_ref, vec_ref, wq_ref, wk_ref, wv_ref, wo_ref, w1_ref, w2_ref, qlen_ref, plen_ref, pos_ref,
    hidden_ref, igrad_ref, qw_ref, qb_ref, kw_ref, vw_ref, vb_ref, ow_ref, ob_ref, g1_ref, s1_ref, iw_ref, ib_ref,
    tw_ref, tb_ref, g2_ref, s2_ref,
    wide, stage, wa, wb, vecs, b1, q_s, k_s, v_s, bias, sel, code,
    block, merged, cls_stage, cls, n1, inv1, h_low, slope, act, n2, inv2, y_low, d_out, d_branch, sums, sums_b1,
    q_rows, dq, dkv, part, work, stage_core, stage_pair, stage_z, final, stage_last, summed,
    send_sems, recv_sems,
):
    place = Place()
    sender = Sender(place, send_sems, recv_sems)
    is_query = place.x == 0
    core = place.core
    scr = n1.at[pl.ds(0, 256), :]
    hid_blk = y_low.at[pl.ds(0, 256), :]

    cut = WIDTH // 2
    vec_cols = vec_ref[...].T[:OWN, :].astype(BF)
    filled = (
        (wq_ref, 0, WIDTH, 0), (wv_ref, 0, cut, 768), (wk_ref, 0, WIDTH, 1280), (wv_ref, cut, cut, 2048),
        (wo_ref, 0, WIDTH, 2560), (w1_ref, 0, FF, 3328),
    )
    wide[...] = jnp.zeros_like(wide)
    for ref, start, size, at in filled:
        wide[pl.ds(0, OWN), pl.ds(at, size)] = ref[:, pl.ds(start, size)]
    wide[pl.ds(0, OWN), pl.ds(1152, 128)] = vec_cols
    greet(place)

    begin, along, across, corner, twin = weight_steps(place, sender, wa, wb)
    offsets = (0, HALF)
    for chunk in range(2):
        first = pl.multiple_of((0, 2 * HALF)[chunk] + (1 - core) * PART[chunk], 128)
        sender.send(
            wide.at[:, pl.ds(first, PART[chunk])], stage.at[:, pl.ds(offsets[chunk], PART[chunk])], 96 + chunk,
            place.sibling,
        )
    wb[tile(place.index, FF_OWN, FF_OWN), :] = w2_ref[...]

    def assemble(chunk):
        sender.arrived(stage.at[:, pl.ds(offsets[chunk], PART[chunk])], 96 + chunk)
        first = pl.multiple_of((0, 2 * HALF)[chunk] + core * PART[chunk], 128)
        mine = wide[pl.ds(0, OWN), pl.ds(first, PART[chunk])].astype(F32)
        other = stage[pl.ds(0, OWN), pl.ds(offsets[chunk], PART[chunk])].astype(F32)
        top, low = jnp.where(core == 0, mine, other), jnp.where(core == 0, other, mine)
        wa[tile(place.chip(), 2 * OWN, 2 * OWN), pl.ds(first, PART[chunk])] = jnp.concatenate([top, low], 0).astype(BF)

    assemble(0)
    begin(0)
    assemble(1)
    begin(1)
    begin(2)

    ends, starts = [], []
    for m in range(MICRO):
        end = jnp.int32(0)
        ends.append([])
        starts.append([])
        for i in range(QS):
            length = jnp.where(is_query, qlen_ref[m, i], plen_ref[m, i] if i < PS else 0)
            starts[m].append(end)
            end = end + length
            ends[m].append(end)
    row_of_key = iota((8, STREAM), 1)
    row_of_query = iota((STREAM, 128), 0)
    for m in range(MICRO):
        key_label = jnp.zeros((8, STREAM), jnp.int32)
        query_label = jnp.zeros((STREAM, 128), jnp.int32)
        for end in ends[m]:
            key_label += (row_of_key >= end).astype(jnp.int32)
            query_label += (row_of_query >= end).astype(jnp.int32)
        code[:, pl.ds(m * STREAM, STREAM)] = key_label + m * 64
        same = query_label[:, :1] == key_label[:1, :]
        bias[pl.ds(m * STREAM, STREAM), :] = jnp.where(same, 0.0, MASKED).astype(BF)

    def cls_places(rows, offset):
        at = iota((rows, 128), 0)
        found = jnp.full((rows, 128), -1, jnp.int32)
        label = jnp.full((rows, 128), -1, jnp.int32)
        for m in range(MICRO):
            for i in range(QS):
                row = jnp.where(is_query, QS * m + i, MICRO * QS + PS * m + i if i < PS else -1000) + offset
                found = jnp.where(at == row, m * STREAM + starts[m][i], found)
                label = jnp.where(at == row, m * 64 + i, label)
        return found[:, :1], label[:, :1]

    found, unused = cls_places(2 * BLOCK, BLOCK * core)
    sel[...] = (found == iota((2 * BLOCK, ROWS), 1)).astype(BF)
    coded = jnp.zeros((2 * BLOCK, 128), jnp.int32)
    at_row, at_lane = iota((2 * BLOCK, 128), 0), iota((2 * BLOCK, 128), 1)
    for m in range(MICRO):
        row = jnp.where(is_query, -1000, BLOCK - MICRO + m) + BLOCK * core
        for i in range(QS):
            coded = jnp.where((at_row == row) & (at_lane == i), pos_ref[m, i], coded)
    row_inputs = dot(sel[...], x_ref[...])
    block[:, pl.ds(0, WIDTH)] = row_inputs.astype(BF)
    block[:, pl.ds(0, 128)] = (row_inputs[:, :128] + coded.astype(F32)).astype(BF)

    for stage_steps in (along, across, corner, twin):
        run(stage_steps(0))

    vecs[...] = wa[:, pl.ds(1152, 128)].astype(F32).T[:16, :]
    low_at, out_at = iota((FF_OWN, 384), 0), iota((FF_OWN, 384), 1)
    spread = jnp.zeros((FF_OWN, 384), jnp.bool_)
    row8, lane8 = iota((8, 384), 0), iota((8, 384), 1)
    pick = jnp.zeros((8, 384), jnp.bool_)
    for a in range(4):
        pick |= (lane8 >= 96 * a + 24 * row8) & (lane8 < 96 * a + 24 * row8 + 24) & (row8 < 4)
        for j in range(4):
            spread |= (low_at >= 24 * a) & (low_at < 24 * a + 24) & (out_at - low_at == 72 * a + 24 * j)
    spread = spread.astype(BF)
    for t in range(8):
        found_b1 = dot_tn(wa[pl.ds(FF_OWN * t, FF_OWN), pl.ds(1152, 128)], spread)
        b1[:, pl.ds(384 * t, 384)] = jnp.sum(jnp.where(pick, found_b1[8:16], 0.0), 0, keepdims=True)

    def vec(i):
        return vecs[pl.ds(i, 1), :]

    def project(i):
        rows = tile(i, 256, 256)
        xb = x_ref[rows, :]
        q_s[rows, :] = ((dot(xb, wa[:, pl.ds(0, WIDTH)]) + vec(0)).astype(BF).astype(F32) * 0.125).astype(BF)
        v_s[rows, pl.ds(0, cut)] = (dot(xb, wa[:, pl.ds(WIDTH, cut)]) + vecs[pl.ds(1, 1), pl.ds(0, cut)]).astype(BF)
        k_s[rows, :] = dot(xb, wa[:, pl.ds(HALF, WIDTH)]).astype(BF)
        v_s[rows, pl.ds(cut, cut)] = (
            dot(xb, wa[:, pl.ds(HALF + WIDTH, cut)]) + vecs[pl.ds(1, 1), pl.ds(cut, cut)]
        ).astype(BF)

    steps = along(1)
    loop(2, project)
    run(steps, 1)
    loop(2, lambda i: project(i + 2))
    run(steps)

    def attend(pair):
        cols = pl.ds(128 * pair, 128)

        def unit(i):
            rows = tile(i, 256, 256)
            keys = tile(i // 2, STREAM, STREAM)
            q2 = q_s[rows, cols].astype(F32)
            low_lanes = iota((256, 128), 1) < 64
            k2, v2 = k_s[keys, cols], v_s[keys, cols]
            outs = []
            for head in range(2):
                qh = jnp.where(low_lanes if head == 0 else ~low_lanes, q2, 0.0).astype(BF)
                scores = dot_nt(qh, k2) + bias[rows, :].astype(F32)
                powers = jnp.exp(scores - jnp.max(scores, -1, keepdims=True))
                shares = powers * (1.0 / jnp.sum(powers, -1, keepdims=True))
                outs.append(dot(shares.astype(BF), v2))
            igrad_ref[rows, cols] = jnp.where(low_lanes, outs[0], outs[1]).astype(BF)

        loop(4, unit)

    steps = across(1)
    for pair in range(6):
        attend(pair)
        run(steps, 1)
    run(steps)

    block[:, pl.ds(WIDTH, WIDTH)] = dot(sel[...], igrad_ref[...]).astype(BF)
    steps = cls_steps(place, sender, 98, block, merged, cls_stage, cls)
    run(steps, 1)
    run(corner(1))
    run(steps, 1)
    run(twin(1))
    run(along(2))
    run(steps)

    def cls_first(i):
        rows = tile(i, 320, 320)
        at = iota((320, 1), 0) + i * 320
        group = jnp.zeros((320, 1), jnp.int32)
        for b in range(1, 16):
            group += (at >= BLOCK * b).astype(jnp.int32)
        xin = jnp.where(at - BLOCK * group < BLOCK - MICRO, cls[rows, pl.ds(0, WIDTH)].astype(F32), 0.0)
        normed, inverse = centre(xin + (dot(cls[rows, pl.ds(WIDTH, WIDTH)], wa[:, pl.ds(2560, WIDTH)]) + vec(2)))
        n1[rows, :] = normed
        inv1[rows, :] = inverse
        h_low[rows, :] = (normed * vec(3) + vec(4)).astype(BF)

    loop(2, cls_first)

    def cls_inner(i):
        rows = tile(i // 6, 320, 320)
        cols = tile(i % 6, 512, 512)
        wcols = pl.ds(pl.multiple_of(3328 + (i % 6) * 512, 128), 512)
        u = dot(h_low[rows, :], wa[:, wcols]) + b1[:, cols]
        phi = 0.5 * (1.0 + lax.erf(u * 0.7071067811865476))
        act[rows, cols] = (u * phi).astype(BF)
        slope[rows, cols] = (phi + u * jnp.exp(-0.5 * u * u) * 0.3989422804014327).astype(BF)

    loop(6, cls_inner)
    run(across(2))
    loop(6, lambda i: cls_inner(i + 6))
    run(corner(2))
    run(twin(2))

    def cls_second(i):
        rows = tile(i, 320, 320)
        r = h_low[rows, :].astype(F32) + (dot(act[rows, :], wb[...]) + vec(5))
        normed, inverse = centre(r)
        n2[rows, :] = normed
        inv2[rows, :] = inverse
        y_low[rows, :] = (normed * vec(6) + vec(7)).astype(BF)

    loop(2, cls_second)

    at = iota((CLS, 1), 0)
    at_col = iota((1, CLS), 1)

    def kinds(index):
        group = jnp.zeros(index.shape, jnp.int32)
        for b in range(1, 16):
            group += (index >= BLOCK * b).astype(jnp.int32)
        inner = index - BLOCK * group
        query_m = (inner >= QS).astype(jnp.int32)
        is_q = inner < MICRO * QS
        passage_m = (inner >= MICRO * QS + PS).astype(jnp.int32)
        is_p = (inner >= MICRO * QS) & (inner < MICRO * (QS + PS))
        return group, inner, is_q, query_m, is_p, passage_m

    group, inner, is_q, query_m, unused, unused = kinds(at)
    unused, unused, unused, unused, col_p, col_m = kinds(at_col)
    paired = is_q & col_p & (query_m == col_m)
    source = (group * BLOCK + (BLOCK - MICRO) + query_m == at_col).astype(BF)
    codes = dot(source, cls[:, pl.ds(0, 128)])
    wanted = jnp.sum(jnp.where(iota((CLS, 128), 1) == inner - QS * query_m, codes, 0.0), 1, keepdims=True)
    wanted = wanted.astype(jnp.int32)
    target = 20 * wanted + MICRO * QS + PS * query_m - 19 * (wanted & 1)
    hit = paired & (target == at_col)
    y_all = y_low[...]
    logits = jnp.where(paired, dot_nt(y_all, y_all) * WIDTH ** -0.5, MASKED)
    powers = jnp.where(paired, jnp.exp(logits - jnp.max(logits, -1, keepdims=True)), 0.0)
    total = jnp.sum(powers, -1, keepdims=True)
    shares = powers * (1.0 / jnp.where(is_q, total, 1.0))
    d_logits = ((shares - hit.astype(F32)) * (1.0 / MICRO)).astype(BF)
    d_y = (dot(d_logits, y_all) + dot_tn(d_logits, y_all)) * WIDTH ** -0.5
    normed = n2[...]
    sums[pl.ds(0, 1), :] = jnp.sum(d_y * normed, 0, keepdims=True)
    sums[pl.ds(1, 1), :] = jnp.sum(d_y, 0, keepdims=True)
    d_sum = centre_back(d_y * vec(6), normed, inv2[...])
    n2[...] = d_sum
    d_out[...] = d_sum.astype(BF)
    sums[pl.ds(2, 1), :] = jnp.sum(d_out[...].astype(F32), 0, keepdims=True)

    def cls_inner_back(i):
        cols = tile(i, 512, 512)
        d_act = dot_nt(d_out[...], wb[cols, :])
        d_u = (d_act * slope[:, cols].astype(F32)).astype(BF)
        slope[:, cols] = d_u
        sums_b1[:, cols] = jnp.sum(d_u.astype(F32), 0, keepdims=True)

    loop(6, cls_inner_back)

    def cls_first_back(i):
        rows = tile(i, 320, 320)
        d_hidden = n2[rows, :] + dot_nt(slope[rows, :], wa[:, pl.ds(3328, FF)])
        normed = n1[rows, :]
        gains = jnp.sum(d_hidden * normed, 0, keepdims=True)
        shifts = jnp.sum(d_hidden, 0, keepdims=True)
        d_sum = centre_back(d_hidden * vec(3), normed, inv1[rows, :])
        n2[rows, :] = d_sum
        d_low = d_sum.astype(BF)
        d_branch[rows, :] = d_low
        totals = (gains, shifts, jnp.sum(d_low.astype(F32), 0, keepdims=True))
        for place_in, value in enumerate(totals):
            line = pl.ds(3 + place_in, 1)
            sums[line, :] = jnp.where(i == 0, value, sums[line, :] + value)

    loop(2, cls_first_back)

    found, label = cls_places(BLOCK, 0)
    sel40 = (found == iota((BLOCK, ROWS), 1)).astype(BF)
    ours = label >= 0
    q_rows[...] = dot(sel40, q_s[...])
    x_rows = dot(sel40, x_ref[...]).astype(BF)
    own_sum = jnp.where(ours, n2[tile(place.batch, BLOCK, BLOCK), :], 0.0)
    d_att = dot_nt(own_sum.astype(BF), wa[:, pl.ds(2560, WIDTH)]).astype(BF).astype(F32)
    seen = label == code[pl.ds(0, 1), :]
    seen2 = jnp.concatenate([seen.astype(F32), seen.astype(F32)], 0) > 0.5
    low_lanes = iota((BLOCK, 128), 1) < 64

    def both(rows):
        return jnp.concatenate([jnp.where(low_lanes, rows, 0.0), jnp.where(low_lanes, 0.0, rows)], 0).astype(BF)

    for pair in range(6):
        cols = pl.ds(128 * pair, 128)
        q2 = both(q_rows[:, cols])
        d_a2 = both(d_att[:, 128 * pair : 128 * pair + 128])
        k2, v2 = k_s[:, cols], v_s[:, cols]
        scores = jnp.where(seen2, dot_nt(q2, k2), MASKED)
        powers = jnp.where(seen2, jnp.exp(scores - jnp.max(scores, -1, keepdims=True)), 0.0)
        total = jnp.sum(powers, -1, keepdims=True)
        shares = powers * (1.0 / jnp.where(total > 0, total, 1.0))
        d_shares = dot_nt(d_a2, v2)
        d_scores = (shares * (d_shares - jnp.sum(d_shares * shares, -1, keepdims=True))).astype(BF)
        d_q2 = dot(d_scores, k2)
        dq[:, cols] = (jnp.where(low_lanes, d_q2[:BLOCK], d_q2[BLOCK:]) * 0.125).astype(BF)
        dkv[:, cols] = dot_tn(d_scores, q2).astype(BF)
        dkv[:, pl.ds(WIDTH + 128 * pair, 128)] = dot_tn(shares.astype(BF), d_a2).astype(BF)

    part[:, pl.ds(0, WIDTH)] = dot_tn(x_rows, dq[...]).astype(BF)

    def project_back(i):
        cols = tile(i, 256, 256)
        out = dot_tn(x_ref[...], dkv[:, cols])
        part[:, pl.ds(pl.multiple_of(WIDTH + i * 256, 128), 256)] = out.astype(BF)

    loop(6, project_back)
    line = iota((128, WIDTH), 0)
    q_line = jnp.sum(dq[...].astype(F32), 0, keepdims=True)
    v_line = jnp.sum(dkv[:, pl.ds(WIDTH, WIDTH)].astype(F32), 0, keepdims=True)
    lines = jnp.where(line == 0, q_line, jnp.where(line == 1, v_line, 0.0))
    part[:, pl.ds(3 * WIDTH, 128)] = lines.T.astype(BF)
    part[:, pl.ds(3 * WIDTH + 128, 128)] = jnp.zeros((WIDTH, 128), BF)

    steps = sum_steps(place, sender, 116, part, work, stage_core, stage_pair, stage_z, final, stage_last, summed)
    run(steps, 1)

    def all_rows(i):
        rows = tile(i, 256, 256)
        branch = dot(igrad_ref[rows, :], wa[:, pl.ds(2560, WIDTH)]) + vec(2)
        normed, unused = centre(x_ref[rows, :].astype(F32) + branch)
        low = (normed * vec(3) + vec(4)).astype(BF)
        hid_blk[...] = low
        scr[...] = low.astype(F32) + vec(5)

        def inner_cols(j):
            cols = tile(j, 512, 512)
            u = dot(hid_blk[...], wa[:, pl.ds(pl.multiple_of(3328 + j * 512, 128), 512)]) + b1[:, cols]
            active = (u * (0.5 * (1.0 + lax.erf(u * 0.7071067811865476)))).astype(BF)
            scr[...] += dot(active, wb[cols, :])

        loop(6, inner_cols)
        normed, unused = centre(scr[...])
        last = jnp.where(i < 2, ends[0][QS - 1], ends[1][QS - 1])
        valid = iota((256, 1), 0) + (i % 2) * 256 < last
        hidden_ref[rows, :] = jnp.where(valid, normed * vec(6) + vec(7), 0.0).astype(BF)

    for i in range(4):
        loop(1, lambda j: all_rows(j + i))
        run(steps, 3)

    back_rows = dot_nt(dq[...], wa[:, pl.ds(0, WIDTH)]) + own_sum
    q_s[:, pl.ds(0, 128)] = jnp.concatenate([sel40.astype(F32), jnp.zeros((128 - BLOCK, ROWS), F32)], 0).T.astype(BF)
    back_low = jnp.concatenate([back_rows, jnp.zeros((128 - BLOCK, WIDTH), F32)], 0)
    back_rest = (back_low - back_low.astype(BF).astype(F32)).astype(BF)
    back_low = back_low.astype(BF)

    def input_back(i):
        rows = tile(i, 256, 256)
        total = dot_nt(dkv[rows, pl.ds(0, WIDTH)], wa[:, pl.ds(HALF, WIDTH)])
        total += dot_nt(dkv[rows, pl.ds(WIDTH, cut)], wa[:, pl.ds(WIDTH, cut)])
        total += dot_nt(dkv[rows, pl.ds(WIDTH + cut, cut)], wa[:, pl.ds(HALF + WIDTH, cut)])
        hit_rows = q_s[rows, pl.ds(0, 128)]
        total += dot(hit_rows, back_low) + dot(hit_rows, back_rest)
        igrad_ref[rows, :] = total.astype(BF)

    loop(4, input_back)

    tall_first = jnp.minimum(place.index * FF_OWN // 128, (FF - 256) // 128) * 128
    tall_at = place.index * FF_OWN - tall_first
    own_first = jnp.minimum(place.index * OWN // 128, (WIDTH - 256) // 128) * 128
    own_at = place.index * OWN - own_first

    scr[...] = dot_tn(act[:, pl.ds(pl.multiple_of(tall_first, 128), 256)], d_out[...])
    tw_ref[...] = scr[pl.ds(pl.multiple_of(tall_at, 8), FF_OWN), :]
    own_cols = pl.ds(pl.multiple_of(own_first, 128), 256)
    own_lines = pl.ds(pl.multiple_of(own_at, 8), OWN)
    att_cols = pl.ds(pl.multiple_of(own_first + WIDTH, 128), 256)
    scr[...] = dot_tn(cls[:, att_cols], d_branch[...])
    ow_ref[...] = scr[own_lines, :]
    for j in range(4):
        scr[...] = dot_tn(h_low[:, own_cols], slope[:, pl.ds(WIDTH * j, WIDTH)])
        iw_ref[:, pl.ds(WIDTH * j, WIDTH)] = scr[own_lines, :]

    def own_lanes(line, first, shift, size):
        window = jnp.broadcast_to(line[:, pl.ds(pl.multiple_of(first, 128), 256)], (8, 256))
        return pltpu.roll(window, 256 - shift, 1)[:1, :size]

    for ref, i in ((g2_ref, 0), (s2_ref, 1), (tb_ref, 2), (g1_ref, 3), (s1_ref, 4), (ob_ref, 5)):
        ref[...] = own_lanes(sums.at[pl.ds(i, 1), :], own_first, own_at, OWN)
    ib_ref[...] = own_lanes(sums_b1, tall_first, tall_at, FF_OWN)

    run(steps)
    qw_ref[...] = summed[:, pl.ds(0, WIDTH)]
    kw_ref[...] = summed[:, pl.ds(WIDTH, WIDTH)]
    vw_ref[...] = summed[:, pl.ds(2 * WIDTH, WIDTH)]
    lines = jnp.concatenate([summed[:, pl.ds(3 * WIDTH, 128)], jnp.zeros((128 - OWN, 128), F32)], 0).T
    qb_ref[...] = lines[0:1, :OWN]
    vb_ref[...] = lines[1:2, :OWN]
    sender.close()


def fast(hidden_in, query_lengths, passage_lengths, positives, stored):
    (query_weight, query_bias, key_weight, value_weight, value_bias, output_weight, output_bias, first_gain,
     first_shift, inner_weight, inner_bias, outer_weight, outer_bias, second_gain, second_shift) = stored
    vectors = jnp.concatenate(
        [query_bias, value_bias, output_bias, first_gain, first_shift, outer_bias, second_gain, second_shift, inner_bias]
    ).astype(F32).reshape(12, OWN)
    vectors = jnp.pad(vectors, ((0, 116), (0, 128 - OWN)))
    shapes = [
        ((ROWS, WIDTH), BF), ((ROWS, WIDTH), BF), ((OWN, WIDTH), F32), ((1, OWN), F32), ((OWN, WIDTH), F32),
        ((OWN, WIDTH), F32), ((1, OWN), F32), ((OWN, WIDTH), F32), ((1, OWN), F32), ((1, OWN), F32), ((1, OWN), F32),
        ((OWN, FF), F32), ((1, FF_OWN), F32), ((FF_OWN, WIDTH), F32), ((1, OWN), F32), ((1, OWN), F32), ((1, OWN), F32),
    ]
    scratch = [
        pltpu.VMEM((32, 6400), BF), pltpu.VMEM((32, 3200), BF), pltpu.VMEM((WIDTH, 6400), BF), pltpu.VMEM((FF, WIDTH), BF),
        pltpu.VMEM((16, WIDTH), F32), pltpu.VMEM((1, FF), F32),
        pltpu.VMEM((ROWS, WIDTH), BF), pltpu.VMEM((ROWS, WIDTH), BF), pltpu.VMEM((ROWS, WIDTH), BF),
        pltpu.VMEM((ROWS, STREAM), BF), pltpu.VMEM((2 * BLOCK, ROWS), BF), pltpu.VMEM((8, ROWS), jnp.int32),
        pltpu.VMEM((2 * BLOCK, 2 * WIDTH), BF), pltpu.VMEM((2 * BLOCK, WIDTH), BF), pltpu.VMEM((2, 2 * BLOCK, WIDTH), BF),
        pltpu.VMEM((CLS, 2 * WIDTH), BF),
        pltpu.VMEM((CLS, WIDTH), F32), pltpu.VMEM((CLS, 1), F32), pltpu.VMEM((CLS, WIDTH), BF),
        pltpu.VMEM((CLS, FF), BF), pltpu.VMEM((CLS, FF), BF),
        pltpu.VMEM((CLS, WIDTH), F32), pltpu.VMEM((CLS, 1), F32), pltpu.VMEM((CLS, WIDTH), BF),
        pltpu.VMEM((CLS, WIDTH), BF), pltpu.VMEM((CLS, WIDTH), BF),
        pltpu.VMEM((8, WIDTH), F32), pltpu.VMEM((1, FF), F32),
        pltpu.VMEM((BLOCK, WIDTH), F32), pltpu.VMEM((BLOCK, WIDTH), BF), pltpu.VMEM((ROWS, 2 * WIDTH), BF),
        pltpu.VMEM((WIDTH, 2 * HALF), BF),
        pltpu.VMEM((16, 2 * OWN, HALF), BF), pltpu.VMEM((16, 2 * OWN, HALF), BF), pltpu.VMEM((16, 2 * OWN, HALF), BF),
        pltpu.VMEM((4, 2 * OWN, HALF), BF), pltpu.VMEM((OWN, HALF), F32), pltpu.VMEM((OWN, HALF), F32),
        pltpu.VMEM((OWN, 2 * HALF), F32),
        pltpu.SemaphoreType.DMA((160,)), pltpu.SemaphoreType.DMA((170,)),
    ]
    vmem = pl.BlockSpec(memory_space=pltpu.VMEM)
    smem = pl.BlockSpec(memory_space=pltpu.SMEM)
    outs = pl.pallas_call(
        layer_kernel,
        out_shape=[jax.ShapeDtypeStruct(shape, kind) for shape, kind in shapes],
        in_specs=[vmem] * 8 + [smem] * 3,
        out_specs=[vmem] * len(shapes),
        scratch_shapes=scratch,
        compiler_params=pltpu.CompilerParams(collective_id=0, has_side_effects=True, vmem_limit_bytes=63 * 2**20),
    )(
        hidden_in.reshape(ROWS, WIDTH), vectors, query_weight, key_weight, value_weight, output_weight, inner_weight,
        outer_weight, query_lengths, passage_lengths, positives,
    )
    shape = hidden_in.shape
    return tuple(
        out.reshape(shape) if i < 2 else (out.reshape(-1) if out.shape[0] == 1 else out) for i, out in enumerate(outs)
    )


def local(
    hidden_in,
    query_lengths,
    passage_lengths,
    positives,
    query_weight,
    query_bias,
    key_weight,
    value_weight,
    value_bias,
    output_weight,
    output_bias,
    first_gain,
    first_shift,
    inner_weight,
    inner_bias,
    outer_weight,
    outer_bias,
    second_gain,
    second_shift,
):
    stored = (
        query_weight,
        query_bias,
        key_weight,
        value_weight,
        value_bias,
        output_weight,
        output_bias,
        first_gain,
        first_shift,
        inner_weight,
        inner_bias,
        outer_weight,
        outer_bias,
        second_gain,
        second_shift,
    )
    sizes = (lax.axis_size("tower"), lax.axis_size("batch"), hidden_in.shape, inner_weight.shape)
    if sizes == (2, 16, (MICRO, 1, STREAM, WIDTH), (OWN, FF)) and query_lengths.shape[1] == QS:
        return fast(hidden_in, query_lengths, passage_lengths, positives, stored)
    micro = hidden_in.shape[0]
    width = hidden_in.shape[3]
    cls_scale = width ** (-0.5)
    side = lax.axis_index("tower")
    is_query = side == 0
    slot_count = query_lengths.shape[1]
    passage_count = passage_lengths.shape[1]
    half_count = (slot_count + 1) // 2
    extra_rows = 2 * half_count - slot_count
    owners = lax.axis_size(("tower", "batch"))
    totals = tuple(
        (jnp.zeros((item.shape[0] * owners,) + item.shape[1:], jnp.float32) for item in stored)
    )
    half_totals = tuple(
        (jnp.zeros((item.shape[0] * owners // 2,) + item.shape[1:], jnp.float32) for item in stored)
    )
    shown_list = []
    grad_list = []
    for micro_step in range(micro):
        gathered = (
            lax.all_gather(query_weight, ("tower", "batch"), axis=0, tiled=True),
            lax.all_gather(query_bias, ("tower", "batch"), axis=0, tiled=True),
            lax.all_gather(key_weight, ("tower", "batch"), axis=0, tiled=True),
            lax.all_gather(value_weight, ("tower", "batch"), axis=0, tiled=True),
            lax.all_gather(value_bias, ("tower", "batch"), axis=0, tiled=True),
            lax.all_gather(output_weight, ("tower", "batch"), axis=0, tiled=True),
            lax.all_gather(output_bias, ("tower", "batch"), axis=0, tiled=True),
            lax.all_gather(first_gain, ("tower", "batch"), axis=0, tiled=True),
            lax.all_gather(first_shift, ("tower", "batch"), axis=0, tiled=True),
            lax.all_gather(inner_weight, ("tower", "batch"), axis=0, tiled=True),
            lax.all_gather(inner_bias, ("tower", "batch"), axis=0, tiled=True),
            lax.all_gather(outer_weight, ("tower", "batch"), axis=0, tiled=True),
            lax.all_gather(outer_bias, ("tower", "batch"), axis=0, tiled=True),
            lax.all_gather(second_gain, ("tower", "batch"), axis=0, tiled=True),
            lax.all_gather(second_shift, ("tower", "batch"), axis=0, tiled=True),
        )
        params = cast_params(gathered)
        inputs = hidden_in[micro_step, 0]
        passage_part = jnp.pad(passage_lengths[micro_step], (0, slot_count - passage_count))
        lengths = jnp.where(is_query, query_lengths[micro_step], passage_part)
        labels, valid, starts, live = segments(lengths, inputs.shape[0])
        saved, shown = forward(inputs, labels, valid, params)
        shown_list.append(shown)
        mine = jnp.where(live[:, None], shown[starts], 0.0)
        partner = partner_2(mine, "tower", 0)
        query_cls = jnp.where(is_query, mine, partner)
        passage_cls = jnp.where(is_query, partner, mine)[:passage_count]
        pooled = lax.all_gather(passage_cls, "batch", axis=0, tiled=True)
        padded_queries = jnp.pad(query_cls, ((0, extra_rows), (0, 0)))
        padded_targets = jnp.pad(positives[micro_step], (0, extra_rows))
        my_queries = lax.dynamic_slice_in_dim(padded_queries, side * half_count, half_count, 0)
        my_targets = lax.dynamic_slice_in_dim(padded_targets, side * half_count, half_count, 0)
        logits = product_nt(my_queries, pooled) * cls_scale
        highest = jnp.max(logits, -1, keepdims=True)
        powers = jnp.exp(logits - highest)
        shares = powers / jnp.sum(powers, -1, keepdims=True)
        columns = jnp.arange(pooled.shape[0], dtype=jnp.int32)
        target = (columns[None, :] == my_targets[:, None]).astype(jnp.float32)
        grad_logits = ((shares - target) / micro).astype(jnp.bfloat16)
        own_grad = product(grad_logits, pooled) * cls_scale
        pooled_grad = product_tn(grad_logits, my_queries) * cls_scale
        summed = lax.psum_scatter(pooled_grad, "batch", scatter_dimension=0, tiled=True)
        other_queries, other_passages = (
            partner_2(own_grad.astype(jnp.bfloat16), "tower", 0).astype(own_grad.dtype),
            partner_2(summed.astype(jnp.bfloat16), "tower", 0).astype(summed.dtype),
        )
        query_grad = jnp.concatenate([own_grad, other_queries], 0)[:slot_count]
        passage_grad = jnp.pad(summed + other_passages, ((0, slot_count - passage_count), (0, 0)))
        cotangent = jnp.where(is_query, query_grad, passage_grad)
        input_part, step_grads = backward(inputs, labels, cotangent, starts, live, saved, params)
        grad_list.append(input_part)
        totals = tuple((first + second for first, second in zip(totals, step_grads)))
    keep_all, give_all = split_halves(totals, side)
    came_all = jax.tree.map(
        lambda part, own: part.astype(own.dtype), partner_2(as_sent(give_all), "tower", 0), give_all
    )
    half_totals = tuple((first + second for first, second in zip(keep_all, came_all)))
    shards = lax.psum_scatter(half_totals, "batch", scatter_dimension=0, tiled=True)
    hidden_out = jnp.stack(shown_list)[:, None]
    input_grad = jnp.stack(grad_list)[:, None]
    return (
        hidden_out,
        input_grad,
        shards[0],
        shards[1],
        shards[2],
        shards[3],
        shards[4],
        shards[5],
        shards[6],
        shards[7],
        shards[8],
        shards[9],
        shards[10],
        shards[11],
        shards[12],
        shards[13],
        shards[14],
    )


def solution(mesh):
    placed = (
        P(None, "tower", "batch", None),
        P(None, "batch"),
        P(None, "batch"),
        P(None, "batch"),
        P(("tower", "batch"), None),
        P(("tower", "batch")),
        P(("tower", "batch"), None),
        P(("tower", "batch"), None),
        P(("tower", "batch")),
        P(("tower", "batch"), None),
        P(("tower", "batch")),
        P(("tower", "batch")),
        P(("tower", "batch")),
        P(("tower", "batch"), None),
        P(("tower", "batch")),
        P(("tower", "batch"), None),
        P(("tower", "batch")),
        P(("tower", "batch")),
        P(("tower", "batch")),
    )
    return jax.shard_map(
        local,
        mesh=mesh,
        in_specs=placed,
        out_specs=(
            P(None, "tower", "batch", None),
            P(None, "tower", "batch", None),
            P(("tower", "batch"), None),
            P(("tower", "batch")),
            P(("tower", "batch"), None),
            P(("tower", "batch"), None),
            P(("tower", "batch")),
            P(("tower", "batch"), None),
            P(("tower", "batch")),
            P(("tower", "batch")),
            P(("tower", "batch")),
            P(("tower", "batch"), None),
            P(("tower", "batch")),
            P(("tower", "batch"), None),
            P(("tower", "batch")),
            P(("tower", "batch")),
            P(("tower", "batch")),
        ),
        check_vma=False,
    )
```

```python
import functools

import jax
import jax.numpy as jnp
from jax import lax
from jax.experimental import pallas as pl
from jax.experimental.pallas import tpu as pltpu
from jax.sharding import PartitionSpec as P

HEADS = 12


EPSILON = 1e-12
MASKED = -1e30


def partner_2(x, axis, apart):
    return lax.ppermute(x, axis, [(i, i ^ 1 << apart) for i in range(lax.axis_size(axis))])


def as_sent(x):
    return jax.tree.map(lambda a: a.astype(jnp.bfloat16) if a.dtype == jnp.float32 else a, x)


def product(left, right):
    return jnp.dot(left, right, preferred_element_type=jnp.float32)


def product_tn(left, right):
    return jnp.einsum("ta,tb->ab", left, right, preferred_element_type=jnp.float32)


def product_nt(left, right):
    return jnp.einsum("ra,ba->rb", left, right, preferred_element_type=jnp.float32)


def normalize(values, gains, shifts):
    average = jnp.mean(values, -1, keepdims=True)
    centred = values - average
    inverse = lax.rsqrt(jnp.mean(centred * centred, -1, keepdims=True) + EPSILON)
    normed = centred * inverse
    return (normed * gains + shifts, normed, inverse)


def normalize_back(upstream, normed, inverse, gains):
    scaled = upstream * gains
    inner = (
        scaled
        - jnp.mean(scaled, -1, keepdims=True)
        - normed * jnp.mean(scaled * normed, -1, keepdims=True)
    )
    return (inner * inverse, jnp.sum(upstream * normed, 0), jnp.sum(upstream, 0))


def gelu_slope(values):
    return (
        0.5 * (1.0 + lax.erf(values * 0.7071067811865476))
        + values * jnp.exp(-0.5 * values * values) * 0.3989422804014327
    )


def segments(lengths, token_rows):
    ends = jnp.cumsum(lengths)
    places = jnp.arange(token_rows, dtype=jnp.int32)
    labels = jnp.sum((places[:, None] >= ends[None, :]).astype(jnp.int32), 1)
    starts = jnp.minimum(ends - lengths, token_rows - 1)
    return (labels, places < ends[-1], starts, lengths > 0)


def tail(inputs, attended, params):
    out_mat, out_vec, gain_one, shift_one = (params[5], params[6], params[7], params[8])
    inner_mat, inner_vec, outer_mat, outer_vec, gain_two, shift_two = params[9:15]
    branch = product(attended, out_mat) + out_vec
    hidden_full, normed_one, inverse_one = normalize(
        inputs.astype(jnp.float32) + branch, gain_one, shift_one
    )
    hidden_low = hidden_full.astype(jnp.bfloat16)
    inner = product(hidden_low, inner_mat) + inner_vec
    active = jax.nn.gelu(inner, approximate=False).astype(jnp.bfloat16)
    outer = product(active, outer_mat) + outer_vec
    result, normed_two, inverse_two = normalize(
        hidden_low.astype(jnp.float32) + outer, gain_two, shift_two
    )
    return (result, (normed_one, inverse_one, hidden_low, inner, active, normed_two, inverse_two))


def forward(inputs, labels, valid, params):
    query_mat, query_vec, key_mat, value_mat, value_vec = params[0:5]
    token_rows, width = inputs.shape
    head_size = width // HEADS
    scale = head_size ** (-0.5)
    queries = (product(inputs, query_mat) + query_vec).astype(jnp.bfloat16)
    keys = product(inputs, key_mat).astype(jnp.bfloat16)
    values = (product(inputs, value_mat) + value_vec).astype(jnp.bfloat16)
    block_rows = min(512, token_rows)

    def one_block(first_row):
        allowed = labels[:, None] == labels[None, :]

        def one_head(head_index):
            head_queries = lax.dynamic_slice_in_dim(queries, head_index * head_size, head_size, 1)
            head_keys = lax.dynamic_slice_in_dim(keys, head_index * head_size, head_size, 1)
            head_values = lax.dynamic_slice_in_dim(values, head_index * head_size, head_size, 1)
            scores = jnp.where(allowed, product_nt(head_queries, head_keys) * scale, MASKED)
            highest = jnp.max(scores, -1, keepdims=True)
            powers = jnp.exp(scores - highest)
            totals = jnp.sum(powers, -1, keepdims=True)
            shares = (powers / totals).astype(jnp.bfloat16)
            return (product(shares, head_values), (highest + jnp.log(totals))[:, 0])

        head_out, head_lse = lax.map(one_head, jnp.arange(HEADS, dtype=jnp.int32))
        attended = (
            jnp.transpose(head_out, (1, 0, 2)).reshape(block_rows, width).astype(jnp.bfloat16)
        )
        result, unused = tail(inputs, attended, params)
        shown = jnp.where(valid[:, None], result, 0.0).astype(jnp.bfloat16)
        return (attended, head_lse, shown)

    firsts = jnp.arange(token_rows // block_rows, dtype=jnp.int32) * block_rows
    attended, lse_blocks, shown = lax.map(one_block, firsts)
    attended = attended.reshape(token_rows, width)
    shown = shown.reshape(token_rows, width)
    lse_all = jnp.transpose(lse_blocks, (1, 0, 2)).reshape(HEADS, token_rows)
    return ((queries, keys, values, attended, lse_all), shown)


def backward(inputs, labels, cotangent, starts, live, saved, params):
    queries, keys, values, attended, lse_all = saved
    query_mat, key_mat, value_mat, out_mat = (params[0], params[2], params[3], params[5])
    gain_one, inner_mat, outer_mat, gain_two = (params[7], params[9], params[11], params[13])
    token_rows, width = inputs.shape
    head_size = width // HEADS
    scale = head_size ** (-0.5)
    slot_count = starts.shape[0]
    row_inputs = inputs[starts]
    row_attended = attended[starts]
    unused, kept = tail(row_inputs, row_attended, params)
    normed_one, inverse_one, hidden_low, inner, active, normed_two, inverse_two = kept
    upstream = jnp.where(live[:, None], cotangent, 0.0)
    grad_sum_two, grad_gain_two, grad_shift_two = normalize_back(
        upstream, normed_two, inverse_two, gain_two
    )
    grad_outer = grad_sum_two.astype(jnp.bfloat16)
    grad_outer_mat = product_tn(active, grad_outer)
    grad_outer_vec = jnp.sum(grad_outer.astype(jnp.float32), 0)
    grad_inner = (product_nt(grad_outer, outer_mat) * gelu_slope(inner)).astype(jnp.bfloat16)
    grad_inner_mat = product_tn(hidden_low, grad_inner)
    grad_inner_vec = jnp.sum(grad_inner.astype(jnp.float32), 0)
    grad_hidden = grad_sum_two + product_nt(grad_inner, inner_mat)
    grad_sum_one, grad_gain_one, grad_shift_one = normalize_back(
        grad_hidden, normed_one, inverse_one, gain_one
    )
    grad_branch = grad_sum_one.astype(jnp.bfloat16)
    grad_out_mat = product_tn(row_attended, grad_branch)
    grad_out_vec = jnp.sum(grad_branch.astype(jnp.float32), 0)
    grad_attended = (
        product_nt(grad_branch, out_mat).astype(jnp.bfloat16).reshape(slot_count, HEADS, head_size)
    )
    row_queries = queries[starts].reshape(slot_count, HEADS, head_size)
    keys_split = keys.reshape(token_rows, HEADS, head_size)
    values_split = values.reshape(token_rows, HEADS, head_size)
    allowed = labels[starts][None, :, None] == labels[None, None, :]
    scores = (
        jnp.einsum("rhd,thd->hrt", row_queries, keys_split, preferred_element_type=jnp.float32)
        * scale
    )
    shares = jnp.where(allowed, jnp.exp(scores - lse_all[:, starts][:, :, None]), 0.0)
    shares_low = shares.astype(jnp.bfloat16)
    grad_shares = jnp.einsum(
        "rhd,thd->hrt", grad_attended, values_split, preferred_element_type=jnp.float32
    )
    grad_scores = (
        shares * (grad_shares - jnp.sum(grad_shares * shares, -1, keepdims=True))
    ).astype(jnp.bfloat16)
    grad_queries = (
        jnp.einsum("hrt,thd->rhd", grad_scores, keys_split, preferred_element_type=jnp.float32)
        * scale
    )
    grad_queries = grad_queries.reshape(slot_count, width).astype(jnp.bfloat16)
    grad_keys = (
        jnp.einsum("hrt,rhd->thd", grad_scores, row_queries, preferred_element_type=jnp.float32)
        * scale
    )
    grad_keys = grad_keys.reshape(token_rows, width).astype(jnp.bfloat16)
    grad_values = jnp.einsum(
        "hrt,rhd->thd", shares_low, grad_attended, preferred_element_type=jnp.float32
    )
    grad_values = grad_values.reshape(token_rows, width).astype(jnp.bfloat16)
    grad_inputs = product_nt(grad_keys, key_mat) + product_nt(grad_values, value_mat)
    grad_inputs = grad_inputs.at[starts].add(product_nt(grad_queries, query_mat) + grad_sum_one)
    grads = (
        product_tn(row_inputs, grad_queries),
        jnp.sum(grad_queries.astype(jnp.float32), 0),
        product_tn(inputs, grad_keys),
        product_tn(inputs, grad_values),
        jnp.sum(grad_values.astype(jnp.float32), 0),
        grad_out_mat,
        grad_out_vec,
        grad_gain_one,
        grad_shift_one,
        grad_inner_mat,
        grad_inner_vec,
        grad_outer_mat,
        grad_outer_vec,
        grad_gain_two,
        grad_shift_two,
    )
    return (grad_inputs.astype(jnp.bfloat16), grads)


def cast_params(gathered):
    vector_places = (1, 4, 6, 7, 8, 10, 12, 13, 14)
    return tuple(
        (
            item.astype(jnp.float32) if place in vector_places else item
            for place, item in enumerate(gathered)
        )
    )


def split_halves(grads, side):
    keep_list = []
    give_list = []
    for item in grads:
        half = item.shape[0] // 2
        keep_list.append(lax.dynamic_slice_in_dim(item, side * half, half, 0))
        give_list.append(lax.dynamic_slice_in_dim(item, (1 - side) * half, half, 0))
    return (tuple(keep_list), tuple(give_list))


MESH = pl.DeviceIdType.MESH
BLOCK = 40
QS, PS, STREAM, WIDTH, FF, MICRO = 17, 2, 512, 768, 3072, 2
ROWS = MICRO * STREAM
CLS = 16 * BLOCK
HALF = 1280
PART = (HALF, 1152, 768)
FIRST = (0, 2560, 4864)
CHUNKS = (
    (0, 0, 640, 256, 384), (0, 640, 640, 256, 384), (1, 0, 768, 256, 512), (1, 768, 384, 128, 256), (2, 0, 768, 256, 512),
    (3, 0, 48, 16, 32), (3, 48, 48, 16, 32),
)
SLOTS = 40 * len(CHUNKS)
OWN = 24
FF_OWN = 96
BF, F32 = jnp.bfloat16, jnp.float32
OFF = ()
RATE = (3, 4, 1.5, 2, 1)
START = (0, 0, 2, 3, 4, 5, 6)
LEAD = 2


class Place:
    def __init__(self):
        self.x = lax.axis_index("tower")
        self.batch = lax.axis_index("batch")
        self.core = self.batch % 2
        self.y = (self.batch // 2) % 2
        self.z = self.batch // 4
        self.index = self.x * 16 + self.batch

    def device(self, x=None, y=None, z=None, core=None):
        x = self.x if x is None else x
        y = self.y if y is None else y
        z = self.z if z is None else z
        core = self.core if core is None else core
        return (x, z * 4 + y * 2 + core)

    def chip(self, x=None, y=None, z=None):
        x = self.x if x is None else x
        y = self.y if y is None else y
        z = self.z if z is None else z
        return x * 8 + z * 2 + y

    def layer(self, step):
        if step == 0:
            return self.z
        if step == 1:
            return self.z + 1 - 2 * (self.z % 2)
        if step == 2:
            return (self.z + 2) % 4
        return 3 - self.z

    @property
    def sibling(self):
        return self.device(core=1 - self.core)

    @property
    def over_x(self):
        return self.device(x=1 - self.x)

    @property
    def over_y(self):
        return self.device(y=1 - self.y)


def greet(place):
    barrier = pltpu.get_barrier_semaphore()
    peers = [place.device(z=place.layer(step)) for step in (1, 2, 3)]
    peers += [place.over_x, place.over_y, place.sibling]
    for peer in peers:
        pl.semaphore_signal(barrier, inc=1, device_id=peer, device_id_type=MESH)
    pl.semaphore_wait(barrier, len(peers))


class Sender:
    def __init__(self, place, send_sems, recv_sems):
        self.place = place
        self.send_sems = send_sems
        self.recv_sems = recv_sems
        self.used = 0
        self.open = []

    def send(self, src, dst, slot, peer, only=None):
        copy = pltpu.make_async_remote_copy(
            src_ref=src,
            dst_ref=dst,
            send_sem=self.send_sems.at[self.used],
            recv_sem=self.recv_sems.at[slot],
            device_id=peer,
            device_id_type=MESH,
        )
        self.used += 1
        if only is None:
            copy.start()
        else:
            pl.when(only)(copy.start)
        self.open.append((copy, only))

    def arrived(self, dst, slot):
        pltpu.make_async_remote_copy(
            src_ref=dst,
            dst_ref=dst,
            send_sem=self.send_sems.at[0],
            recv_sem=self.recv_sems.at[slot],
            device_id=self.place.sibling,
            device_id_type=MESH,
        ).wait_recv()

    def close(self):
        for copy, only in self.open:
            if only is None:
                copy.wait_send()
            else:
                pl.when(only)(copy.wait_send)
        self.open = []


def tile(index, size, unit):
    return pl.ds(pl.multiple_of(index * unit, unit), size)


def loop(count, body):
    if getattr(body, '__name__', '') in OFF or 'all' in OFF:
        return
    def step(index, carry):
        body(index)
        return carry

    lax.fori_loop(0, count, step, 0)


def shifted(body, by):
    def moved(index):
        body(index + by)
    moved.__name__ = body.__name__
    return moved


def dot(left, right):
    return jnp.dot(left, right, preferred_element_type=F32)


def dot_nt(left, right):
    return lax.dot_general(left, right, (((1,), (1,)), ((), ())), preferred_element_type=F32)


def dot_tn(left, right):
    return lax.dot_general(left, right, (((0,), (0,)), ((), ())), preferred_element_type=F32)


def iota(shape, dim):
    return lax.broadcasted_iota(jnp.int32, shape, dim)


def centre(values):
    average = jnp.mean(values, -1, keepdims=True)
    centred = values - average
    inverse = lax.rsqrt(jnp.mean(centred * centred, -1, keepdims=True) + EPSILON)
    return centred * inverse, inverse


def centre_back(scaled, normed, inverse):
    return inverse * (
        scaled - jnp.mean(scaled, -1, keepdims=True) - normed * jnp.mean(scaled * normed, -1, keepdims=True)
    )


def weight_steps(place, sender, all_wide, all_tall):
    middle = (place.z == 1) | (place.z == 2)

    def view(chunk, core, chip, start=0, stop=None):
        part, offset, size, unused, unused = CHUNKS[chunk]
        size = (size if stop is None else stop) - start
        if part < 3:
            first = pl.multiple_of(FIRST[part] + core * PART[part] + offset + start, 128)
            return all_wide.at[tile(chip, 2 * OWN, 2 * OWN), pl.ds(first, size)]
        first = pl.multiple_of((chip * 2 + core) * FF_OWN + offset + start, 16)
        return all_tall.at[pl.ds(first, size), :]

    def slot(chunk, kind, layer):
        return (chunk * 10 + kind) * 4 + layer

    def along_z(block, at):
        sender.send(block, block, at, place.device(z=place.layer(1)))
        sender.send(block, block, at, place.device(z=place.layer(2)))
        sender.send(block, block, at, place.device(z=place.layer(3)), only=middle)

    def begin(chunk):
        own = view(chunk, place.core, place.chip())
        along_z(own, slot(chunk, 0, place.z))
        sender.send(own, own, slot(chunk, 1, place.z), place.over_x)
        sender.send(own, own, slot(chunk, 2, place.z), place.over_y)
        sender.send(own, own, slot(chunk, 5, place.z), place.sibling)

    def along(chunk, step):
        layer = place.layer(step)
        block = view(chunk, place.core, place.chip(z=layer))
        sender.arrived(block, slot(chunk, 0, layer))
        if step == 2:
            sender.send(block, block, slot(chunk, 0, layer), place.device(z=place.layer(1)), only=middle)
        sender.send(block, block, slot(chunk, 1, layer), place.over_x)
        sender.send(block, block, slot(chunk, 2, layer), place.over_y)
        sender.send(block, block, slot(chunk, 5, layer), place.sibling)

    def across(chunk, step):
        layer = place.layer(step)
        chip_x, chip_y = place.chip(x=1 - place.x, z=layer), place.chip(y=1 - place.y, z=layer)
        first, second = CHUNKS[chunk][3:]
        from_x, from_y = view(chunk, place.core, chip_x), view(chunk, place.core, chip_y)
        sender.arrived(from_x, slot(chunk, 1, layer))
        if step < 2:
            piece = view(chunk, place.core, chip_x, 0, second if step == 0 else first)
            sender.send(piece, piece, slot(chunk, 3, layer), place.over_y)
        sender.send(from_x, from_x, slot(chunk, 6, layer), place.sibling)
        sender.arrived(from_y, slot(chunk, 2, layer))
        if step >= 2:
            piece = view(chunk, place.core, chip_y, 0, first)
            sender.send(piece, piece, slot(chunk, 3, layer), place.over_x)
        if step == 0:
            piece = view(chunk, place.core, chip_y, second)
            sender.send(piece, piece, slot(chunk, 4, layer), place.over_x)
        sender.send(from_y, from_y, slot(chunk, 7, layer), place.sibling)

    def far(layer):
        return place.chip(x=1 - place.x, y=1 - place.y, z=layer)

    def corner(chunk):
        first, second = CHUNKS[chunk][3:]
        sender.arrived(view(chunk, place.core, far(place.z), 0, second), slot(chunk, 3, place.z))
        sender.arrived(view(chunk, place.core, far(place.z), second), slot(chunk, 4, place.z))
        rest = view(chunk, place.core, far(place.z), first)
        along_z(rest, slot(chunk, 4, place.z))
        block = view(chunk, place.core, far(place.z))
        sender.send(block, block, slot(chunk, 8, place.z), place.sibling)

    def corner_along(chunk, step):
        layer = place.layer(step)
        rest = view(chunk, place.core, far(layer), CHUNKS[chunk][3])
        sender.arrived(rest, slot(chunk, 4, layer))
        if step == 2:
            sender.send(rest, rest, slot(chunk, 4, layer), place.device(z=place.layer(1)), only=middle)
        sender.send(rest, rest, slot(chunk, 9, layer), place.sibling)

    def corner_third(chunk, step):
        layer = place.layer(step)
        piece = view(chunk, place.core, far(layer), 0, CHUNKS[chunk][3])
        sender.arrived(piece, slot(chunk, 3, layer))
        sender.send(piece, piece, slot(chunk, 8, layer), place.sibling)

    def twin(chunk):
        core = 1 - place.core
        for step in range(4):
            layer = place.layer(step)
            sender.arrived(view(chunk, core, place.chip(z=layer)), slot(chunk, 5, layer))
            sender.arrived(view(chunk, core, place.chip(x=1 - place.x, z=layer)), slot(chunk, 6, layer))
            sender.arrived(view(chunk, core, place.chip(y=1 - place.y, z=layer)), slot(chunk, 7, layer))
            if step == 0:
                sender.arrived(view(chunk, core, far(layer)), slot(chunk, 8, layer))
            else:
                sender.arrived(view(chunk, core, far(layer), 0, CHUNKS[chunk][3]), slot(chunk, 8, layer))
                sender.arrived(view(chunk, core, far(layer), CHUNKS[chunk][3]), slot(chunk, 9, layer))

    def steps():
        stages = (
            (5, twin, (None,)), (4, corner_along, (3,)), (3, corner_along, (1, 2)), (3, corner_third, (3,)),
            (2, corner, (None,)), (2, corner_third, (1, 2)), (2, across, (3,)), (1, across, (0, 1, 2)),
            (1, along, (3,)), (0, along, (1, 2)),
        )
        count = len(CHUNKS)
        for turn in range(START[-1] + 6):
            for late, stage, places in stages:
                for chunk in [c for c in range(count) if START[c] == turn - late]:
                    for step in places:
                        if step is None:
                            stage(chunk)
                        else:
                            stage(chunk, step)
                        yield chunk if stage is twin else None
            for chunk in [c for c in range(count) if START[c] == turn + LEAD]:
                begin(chunk)

    return begin, steps


def cls_steps(place, sender, base, block_ref, merged, stage, out_ref):
    rows, half = 2 * BLOCK, WIDTH // 2
    mine = tile(place.core, half, half)
    other = tile(1 - place.core, half, half)

    def view(core, y, z):
        return out_ref.at[tile(z * 2 + y, rows, rows), tile(core, half, half)]

    sender.send(block_ref.at[:, other], stage.at[0], base, place.sibling)
    yield
    sender.arrived(stage.at[0], base)
    merged[...] = (block_ref[:, mine].astype(F32) + stage[0].astype(F32)).astype(BF)
    sender.send(merged, stage.at[1], base + 1, place.over_x)
    yield
    sender.arrived(stage.at[1], base + 1)
    own = view(place.core, place.y, place.z)
    own[...] = (merged[...].astype(F32) + stage[1].astype(F32)).astype(BF)
    for step in (3, 2, 1):
        sender.send(own, own, base + 2 + place.z, place.device(z=place.layer(step)))
    for step in range(4):
        layer = place.layer(step)
        block = view(place.core, place.y, layer)
        if step > 0:
            yield
            sender.arrived(block, base + 2 + layer)
        sender.send(block, block, base + 6 + layer, place.over_y)
        sender.send(block, block, base + 10 + layer, place.sibling)
    for step in range(4):
        yield
        layer = place.layer(step)
        block = view(place.core, 1 - place.y, layer)
        sender.arrived(block, base + 6 + layer)
        sender.send(block, block, base + 14 + layer, place.sibling)
    yield
    for step in range(4):
        layer = place.layer(step)
        sender.arrived(view(1 - place.core, place.y, layer), base + 10 + layer)
        sender.arrived(view(1 - place.core, 1 - place.y, layer), base + 14 + layer)


def sum_steps(place, sender, base, part_ref, work, stage_core, stage_pair, stage_z, final, stage_last, out_ref):
    mine = tile(place.core, HALF, HALF)
    other = tile(1 - place.core, HALF, HALF)
    order = (3, 2, 1, 0)
    blocks = [(dx, dy, step) for step in order for dx, dy in ((1, 1), (1, 0), (0, 1), (0, 0))]

    def x_first(step):
        return step % 2 == 0

    def rows_of(dx, dy, step):
        chip = place.chip(1 - place.x if dx else place.x, 1 - place.y if dy else place.y, place.layer(step))
        return tile(chip, 2 * OWN, 2 * OWN)

    def add(index, landed):
        work[index] = (work[index].astype(F32) + landed.astype(F32)).astype(BF)

    for index, at in enumerate(blocks):
        sender.send(part_ref.at[rows_of(*at), other], stage_core.at[index], base + index, place.sibling)
    for index, at in enumerate(blocks):
        if index % 4 == 0:
            yield
        dx, dy, step = at
        sender.arrived(stage_core.at[index], base + index)
        work[index] = (part_ref[rows_of(*at), mine].astype(F32) + stage_core[index].astype(F32)).astype(BF)
        if (dx if x_first(step) else dy) == 1:
            peer = place.over_x if x_first(step) else place.over_y
            sender.send(work.at[index], stage_pair.at[index], base + 16 + index, peer)

    def first_add(step):
        for second in (1, 0):
            keep = (0, second) if x_first(step) else (second, 0)
            sent = (1, second) if x_first(step) else (second, 1)
            index, source = blocks.index(keep + (step,)), blocks.index(sent + (step,))
            sender.arrived(stage_pair.at[source], base + 16 + source)
            add(index, stage_pair[source])
            if second:
                peer = place.over_y if x_first(step) else place.over_x
                sender.send(work.at[index], stage_pair.at[index], base + 32 + index, peer)

    def second_add(step):
        index = blocks.index((0, 0, step))
        source = blocks.index(((0, 1) if x_first(step) else (1, 0)) + (step,))
        sender.arrived(stage_pair.at[source], base + 32 + source)
        add(index, stage_pair[source])
        if step:
            sender.send(work.at[index], stage_z.at[step], base + 48 + step, place.device(z=place.layer(step)))

    yield
    first_add(3)
    yield
    first_add(2)
    yield
    second_add(3)
    yield
    first_add(1)
    yield
    second_add(2)
    yield
    first_add(0)
    yield
    second_add(1)
    yield
    second_add(0)
    yield
    total = work[blocks.index((0, 0, 0))].astype(F32)
    for step in (3, 2, 1):
        sender.arrived(stage_z.at[step], base + 48 + step)
        total = total + stage_z[step].astype(F32)
    top, low = total[:OWN], total[OWN:]
    is_first = place.core == 0
    final[...] = jnp.where(is_first, low, top)
    sender.send(final, stage_last, base + 52, place.sibling)
    out_ref[:, mine] = jnp.where(is_first, top, low)
    yield
    sender.arrived(stage_last, base + 52)
    out_ref[:, other] = stage_last[...]


def weave(units, *steps):
    for index, unit in enumerate(units):
        unit()
        for generator, count in steps:
            run(generator, int((index + 1) * count) - int(index * count))


def run_to(steps, chunk):
    for done in steps:
        if done == chunk:
            return


def run(steps, count=None):
    while count is None or count > 0:
        if next(steps, "end") == "end":
            return
        if count is not None:
            count -= 1


def layer_kernel(
    x_ref, bq_ref, bv_ref, bo_ref, g1_in, s1_in, b2_ref, g2_in, s2_in, b1_ref, wq_ref, wk_ref, wv_ref, wo_ref, w1_ref, w2_ref, qlen_ref, plen_ref, pos_ref,
    hidden_ref, igrad_ref, qw_ref, qb_ref, kw_ref, vw_ref, vb_ref, ow_ref, ob_ref, g1_ref, s1_ref, iw_ref, ib_ref,
    tw_ref, tb_ref, g2_ref, s2_ref,
    lines_s, wide, stage, wa, wb, vecs, b1, q_s, k_s, v_s, bias, sel, code,
    block, merged, cls_stage, cls, att_block, att_merged, att_stage, cls_att, n1, columns, h_low, slope, act, n2, d_out, d_branch, sums, sums_b1,
    q_rows, x_rows, att_rows, dq, dkv, part, work, stage_core, stage_pair, stage_z, final, stage_last, summed,
    send_sems, cls_sems, recv_sems,
):
    place = Place()
    sender = Sender(place, send_sems, recv_sems)
    cls_sender = Sender(place, cls_sems, recv_sems)
    is_query = place.x == 0
    core = place.core
    scr = n1.at[pl.ds(0, STREAM), :]
    window = n1.at[pl.ds(0, 256), :]

    cut = WIDTH // 2
    lines_s[...] = jnp.zeros_like(lines_s)
    for i, ref in enumerate((bq_ref, bv_ref, bo_ref, g1_in, s1_in, b2_ref, g2_in, s2_in)):
        lines_s[pl.ds(i, 1), pl.ds(0, OWN)] = ref[...].astype(F32).reshape(1, OWN)
    lines_s[pl.ds(16, 1), pl.ds(0, FF_OWN)] = b1_ref[...].astype(F32).reshape(1, FF_OWN)
    long_line = jnp.broadcast_to(lines_s[pl.ds(16, 1), :], (8, 128))
    for i in range(4):
        turned = long_line if i == 0 else pltpu.roll(long_line, 128 - OWN * i, 1)
        lines_s[pl.ds(8 + i, 1), :] = turned[:1, :]
    vec_cols = lines_s[...].T[:OWN, :].astype(BF)
    filled = (
        (wq_ref, 0, WIDTH, 0), (wv_ref, 0, cut, 768), (wk_ref, 0, WIDTH, 1280), (wv_ref, cut, cut, 2048),
        (wo_ref, 0, WIDTH, 2560), (w1_ref, 0, FF, 3328),
    )
    wide[...] = jnp.zeros_like(wide)
    for ref, start, size, at in filled:
        wide[pl.ds(0, OWN), pl.ds(at, size)] = ref[:, pl.ds(start, size)]
    wide[pl.ds(0, OWN), pl.ds(1152, 128)] = vec_cols
    greet(place)

    begin, weight_parts = weight_steps(place, sender, wa, wb)
    offsets = (0, HALF, HALF + PART[1])
    for chunk in range(3):
        first = pl.multiple_of(FIRST[chunk] + (1 - core) * PART[chunk], 128)
        landing = stage.at[:, pl.ds(offsets[chunk], PART[chunk])]
        sender.send(wide.at[:, pl.ds(first, PART[chunk])], landing, SLOTS + chunk, place.sibling)
    wb[tile(place.index, FF_OWN, FF_OWN), :] = w2_ref[...]

    def assemble(chunk):
        sender.arrived(stage.at[:, pl.ds(offsets[chunk], PART[chunk])], SLOTS + chunk)
        first = pl.multiple_of(FIRST[chunk] + core * PART[chunk], 128)
        mine = wide[pl.ds(0, OWN), pl.ds(first, PART[chunk])].astype(F32)
        other = stage[pl.ds(0, OWN), pl.ds(offsets[chunk], PART[chunk])].astype(F32)
        top, low = jnp.where(core == 0, mine, other), jnp.where(core == 0, other, mine)
        wa[tile(place.chip(), 2 * OWN, 2 * OWN), pl.ds(first, PART[chunk])] = jnp.concatenate([top, low], 0).astype(BF)

    assemble(0)
    for chunk in range(len(CHUNKS)):
        if START[chunk] == 0:
            begin(chunk)
    assemble(1)
    assemble(2)
    for chunk in range(len(CHUNKS)):
        if 0 < START[chunk] < LEAD:
            begin(chunk)

    ends, starts = [], []
    for m in range(MICRO):
        end = jnp.int32(0)
        ends.append([])
        starts.append([])
        for i in range(QS):
            length = jnp.where(is_query, qlen_ref[m, i], plen_ref[m, i] if i < PS else 0)
            starts[m].append(end)
            end = end + length
            ends[m].append(end)
    weights = weight_parts()
    run(weights, 1)
    row_of_key = iota((8, STREAM), 1)
    row_of_query = iota((STREAM, 128), 0)
    for m in range(MICRO):
        key_label = jnp.zeros((8, STREAM), jnp.int32)
        query_label = jnp.zeros((STREAM, 128), jnp.int32)
        for end in ends[m]:
            key_label += (row_of_key >= end).astype(jnp.int32)
            query_label += (row_of_query >= end).astype(jnp.int32)
        code[:, pl.ds(m * STREAM, STREAM)] = key_label + m * 64
        same = query_label[:, :1] == key_label[:1, :]
        bias[pl.ds(m * STREAM, STREAM), :] = jnp.where(same, 0.0, MASKED).astype(BF)

    def cls_places(rows, offset):
        at = iota((rows, 128), 0)
        found = jnp.full((rows, 128), -1, jnp.int32)
        label = jnp.full((rows, 128), -1, jnp.int32)
        for m in range(MICRO):
            for i in range(QS):
                row = jnp.where(is_query, QS * m + i, MICRO * QS + PS * m + i if i < PS else -1000) + offset
                found = jnp.where(at == row, m * STREAM + starts[m][i], found)
                label = jnp.where(at == row, m * 64 + i, label)
        return found[:, :1], label[:, :1]

    found, label = cls_places(BLOCK, 0)
    sel[...] = (found == iota((BLOCK, ROWS), 1)).astype(BF)
    ours = label >= 0
    seen = (label == code[pl.ds(0, 1), :]).astype(F32)
    seen2 = jnp.concatenate([seen, seen], 0) > 0.5
    low_lanes = iota((BLOCK, 128), 1) < 64
    coded = jnp.zeros((BLOCK, 128), jnp.int32)
    at_row, at_lane = iota((BLOCK, 128), 0), iota((BLOCK, 128), 1)
    for m in range(MICRO):
        for i in range(QS):
            here = (at_row == jnp.where(is_query, -1000, BLOCK - MICRO + m)) & (at_lane == i)
            coded = jnp.where(here, pos_ref[m, i], coded)
    coded = coded.astype(F32)
    x_rows[...] = dot(sel[...], x_ref[...])

    def both(rows):
        return jnp.concatenate([jnp.where(low_lanes, rows, 0.0), jnp.where(low_lanes, 0.0, rows)], 0).astype(BF)

    def for_chip(rows):
        nothing = jnp.zeros_like(rows)
        return jnp.concatenate([jnp.where(core == 0, rows, nothing), jnp.where(core == 0, nothing, rows)], 0).astype(BF)

    run_to(weights, 1)

    vecs[...] = wa[:, pl.ds(1152, 128)].astype(F32).T[:16, :]
    low_at, out_at = iota((FF_OWN, 384), 0), iota((FF_OWN, 384), 1)
    spread = jnp.zeros((FF_OWN, 384), jnp.bool_)
    row8, lane8 = iota((8, 384), 0), iota((8, 384), 1)
    pick = jnp.zeros((8, 384), jnp.bool_)
    for a in range(4):
        pick |= (lane8 >= 96 * a + 24 * row8) & (lane8 < 96 * a + 24 * row8 + 24) & (row8 < 4)
        for j in range(4):
            spread |= (low_at >= 24 * a) & (low_at < 24 * a + 24) & (out_at - low_at == 72 * a + 24 * j)
    spread = spread.astype(BF)
    for t in range(8):
        found_b1 = dot_tn(wa[pl.ds(FF_OWN * t, FF_OWN), pl.ds(1152, 128)], spread)
        b1[:, pl.ds(384 * t, 384)] = jnp.sum(jnp.where(pick, found_b1[8:16], 0.0), 0, keepdims=True)

    def vec(i):
        return vecs[pl.ds(i, 1), :]

    def project_q(i):
        rows = tile(i, 512, 512)
        xb = x_ref[rows, :]
        q_s[rows, :] = ((dot(xb, wa[:, pl.ds(0, WIDTH)]) + vec(0)).astype(BF).astype(F32) * 0.125).astype(BF)

    def project_k(i):
        rows = tile(i, 512, 512)
        k_s[rows, :] = dot(x_ref[rows, :], wa[:, pl.ds(HALF, WIDTH)]).astype(BF)

    def project_v(i):
        rows = tile(i, 512, 512)
        xb = x_ref[rows, :]
        v_s[rows, pl.ds(0, cut)] = (dot(xb, wa[:, pl.ds(WIDTH, cut)]) + vecs[pl.ds(1, 1), pl.ds(0, cut)]).astype(BF)
        v_s[rows, pl.ds(cut, cut)] = (
            dot(xb, wa[:, pl.ds(HALF + WIDTH, cut)]) + vecs[pl.ds(1, 1), pl.ds(cut, cut)]
        ).astype(BF)

    run(weights, 1)
    weave([functools.partial(loop, 1, shifted(f, i)) for f in (project_q, project_k, project_v) for i in range(2)], (weights, RATE[3]))

    q_rows[...] = dot(sel[...], q_s[...])

    def own_shares(pair):
        q2 = both(q_rows[:, pl.ds(128 * pair, 128)])
        scores = jnp.where(seen2, dot_nt(q2, k_s[:, pl.ds(128 * pair, 128)]), MASKED)
        powers = jnp.where(seen2, jnp.exp(scores - jnp.max(scores, -1, keepdims=True)), 0.0)
        total = jnp.sum(powers, -1, keepdims=True)
        return q2, powers * (1.0 / jnp.where(total > 0, total, 1.0))

    def own_attend(pair):
        cols = pl.ds(128 * pair, 128)
        unused, shares = own_shares(pair)
        out = dot(shares.astype(BF), v_s[:, cols])
        att_rows[:, cols] = jnp.where(low_lanes, out[:BLOCK], out[BLOCK:])

    weave([functools.partial(own_attend, pair) for pair in range(6)], (weights, RATE[4]))
    run_to(weights, 2)

    summed_in = x_rows[...] + (dot(att_rows[...].astype(BF), wa[:, pl.ds(2560, WIDTH)]) + vec(2))
    summed_in = jnp.where(ours, summed_in - jnp.mean(summed_in, -1, keepdims=True), 0.0)
    block[...] = for_chip(summed_in)
    block[:, pl.ds(0, 128)] = for_chip(summed_in[:, :128] + coded)
    att_block[...] = for_chip(jnp.where(ours, att_rows[...], 0.0))
    cls_parts = cls_steps(place, cls_sender, SLOTS + 3, block, merged, cls_stage, cls)
    run(cls_parts, 1)

    def attend(pair, m):
        cols = pl.ds(128 * pair, 128)
        keys = pl.ds(m * STREAM, STREAM)
        k2, v2 = k_s[keys, cols], v_s[keys, cols].astype(F32)
        low_keys = iota((STREAM, 128), 1) < 64
        values = jnp.concatenate([jnp.where(low_keys, v2, 1.0), jnp.where(low_keys, 1.0, v2)], 1).astype(BF)
        low = iota((256, 128), 1) < 64
        for i in range(2):
            rows = pl.ds(m * STREAM + 256 * i, 256)
            q2 = q_s[rows, cols].astype(F32)
            heads = jnp.concatenate([jnp.where(low, q2, 0.0), jnp.where(low, 0.0, q2)], 0).astype(BF)
            scores = dot_nt(heads, k2)
            masked = bias[rows, :].astype(F32)
            powers = []
            for head in range(2):
                part_scores = scores[256 * head : 256 * head + 256] + masked
                powers.append(jnp.exp(part_scores - jnp.max(part_scores, -1, keepdims=True)).astype(BF))
            out = dot(jnp.concatenate(powers, 0), values)
            first, second = out[:256, :128], out[256:, 128:]
            sums_of = pltpu.roll(jnp.where(low, second, first), 64, 1)
            igrad_ref[rows, cols] = (jnp.where(low, first, second) * (1.0 / sums_of)).astype(BF)

    weave(
        [functools.partial(attend, pair, m) for pair in range(6) for m in range(MICRO)], (cls_parts, 1), (weights, RATE[0])
    )
    run(cls_parts)

    def cls_first(i):
        rows = tile(i, CLS, CLS)
        at = iota((CLS, 1), 0) + i * CLS
        group = jnp.zeros((CLS, 1), jnp.int32)
        for b in range(1, 16):
            group += (at >= BLOCK * b).astype(jnp.int32)
        xin = jnp.where(at - BLOCK * group < BLOCK - MICRO, cls[rows, :].astype(F32), 0.0)
        normed, inverse = centre(xin)
        n1[rows, :] = normed
        columns[rows, pl.ds(0, 1)] = inverse
        h_low[rows, :] = (normed * vec(3) + vec(4)).astype(BF)

    loop(1, cls_first)
    run(weights, 1)

    at = iota((CLS, 1), 0)
    at_col = iota((1, CLS), 1)

    def kinds(index):
        group = jnp.zeros(index.shape, jnp.int32)
        for b in range(1, 16):
            group += (index >= BLOCK * b).astype(jnp.int32)
        inner = index - BLOCK * group
        query_m = (inner >= QS).astype(jnp.int32)
        is_q = inner < MICRO * QS
        passage_m = (inner >= MICRO * QS + PS).astype(jnp.int32)
        is_p = (inner >= MICRO * QS) & (inner < MICRO * (QS + PS))
        return group, inner, is_q, query_m, is_p, passage_m

    group, inner, is_q, query_m, unused, unused = kinds(at)
    source = (group * BLOCK + (BLOCK - MICRO) + query_m == at_col).astype(BF)
    codes = dot(source, cls[:, pl.ds(0, 128)])
    wanted = jnp.sum(jnp.where(iota((CLS, 128), 1) == inner - QS * query_m, codes, 0.0), 1, keepdims=True)
    wanted = wanted.astype(jnp.int32)
    target = 20 * wanted + MICRO * QS + PS * query_m - 19 * (wanted & 1)
    columns[:, pl.ds(2, 1)] = target.astype(F32)
    cls_sender.close()
    y_low = cls
    hid_blk = y_low.at[pl.ds(0, STREAM), :]

    def cls_inner(i):
        rows = pl.ds(0, CLS)
        cols = tile(i, 512, 512)
        wcols = pl.ds(pl.multiple_of(3328 + i * 512, 128), 512)
        u = dot(h_low[rows, :], wa[:, wcols]) + b1[:, cols]
        phi = 0.5 * (1.0 + lax.erf(u * 0.7071067811865476))
        act[rows, cols] = (u * phi).astype(BF)
        slope[rows, cols] = (phi + u * jnp.exp(-0.5 * u * u) * 0.3989422804014327).astype(BF)

    weave([functools.partial(loop, 1, shifted(cls_inner, i)) for i in range(3)], (weights, RATE[1]))
    run_to(weights, 4)
    weave([functools.partial(loop, 1, shifted(cls_inner, i)) for i in range(3, 6)], (weights, RATE[1]))
    run_to(weights, 6)
    att_steps = cls_steps(place, sender, SLOTS + 21, att_block, att_merged, att_stage, cls_att)
    run(att_steps, 1)

    def cls_second(i):
        rows = tile(i, CLS, CLS)
        r = h_low[rows, :].astype(F32) + (dot(act[rows, :], wb[...]) + vec(5))
        normed, inverse = centre(r)
        n2[rows, :] = normed
        columns[rows, pl.ds(1, 1)] = inverse
        y_low[rows, :] = (normed * vec(6) + vec(7)).astype(BF)

    weave([functools.partial(loop, 1, cls_second)], (att_steps, 2))

    at_col = iota((1, CLS), 1)
    unused, unused, is_q, query_m, unused, unused = kinds(iota((CLS, 1), 0))
    unused, unused, unused, unused, col_p, col_m = kinds(at_col)
    paired = is_q & col_p & (query_m == col_m)
    hit = paired & (columns[:, pl.ds(2, 1)] == at_col.astype(F32))
    y_all = y_low[...]
    logits = jnp.where(paired, dot_nt(y_all, y_all) * WIDTH ** -0.5, MASKED)
    powers = jnp.where(paired, jnp.exp(logits - jnp.max(logits, -1, keepdims=True)), 0.0)
    total = jnp.sum(powers, -1, keepdims=True)
    shares = powers * (1.0 / jnp.where(is_q, total, 1.0))
    d_logits = ((shares - hit.astype(F32)) * (1.0 / MICRO)).astype(BF)
    d_y = (dot(d_logits, y_all) + dot_tn(d_logits, y_all)) * WIDTH ** -0.5
    normed = n2[...]
    sums[pl.ds(0, 1), :] = jnp.sum(d_y * normed, 0, keepdims=True)
    sums[pl.ds(1, 1), :] = jnp.sum(d_y, 0, keepdims=True)
    d_sum = centre_back(d_y * vec(6), normed, columns[:, pl.ds(1, 1)])
    n2[...] = d_sum
    d_out[...] = d_sum.astype(BF)
    sums[pl.ds(2, 1), :] = jnp.sum(d_out[...].astype(F32), 0, keepdims=True)

    def cls_inner_back(i):
        cols = tile(i, 512, 512)
        d_act = dot_nt(d_out[...], wb[cols, :])
        d_u = (d_act * slope[:, cols].astype(F32)).astype(BF)
        slope[:, cols] = d_u
        sums_b1[:, cols] = jnp.sum(d_u.astype(F32), 0, keepdims=True)

    run(att_steps, 1)
    weave([functools.partial(loop, 2, shifted(cls_inner_back, i)) for i in (0, 2, 4)], (att_steps, 2))

    def cls_first_back(i):
        rows = tile(i, CLS, CLS)
        d_hidden = n2[rows, :] + dot_nt(slope[rows, :], wa[:, pl.ds(3328, FF)])
        normed = n1[rows, :]
        gains = jnp.sum(d_hidden * normed, 0, keepdims=True)
        shifts = jnp.sum(d_hidden, 0, keepdims=True)
        d_sum = centre_back(d_hidden * vec(3), normed, columns[rows, pl.ds(0, 1)])
        n2[rows, :] = d_sum
        d_low = d_sum.astype(BF)
        d_branch[rows, :] = d_low
        totals = (gains, shifts, jnp.sum(d_low.astype(F32), 0, keepdims=True))
        for place_in, value in enumerate(totals):
            line = pl.ds(3 + place_in, 1)
            sums[line, :] = jnp.where(i == 0, value, sums[line, :] + value)

    weave([functools.partial(loop, 1, cls_first_back)], (att_steps, 2))

    own_sum = jnp.where(ours, n2[tile(place.batch, BLOCK, BLOCK), :], 0.0)
    d_att = dot_nt(own_sum.astype(BF), wa[:, pl.ds(2560, WIDTH)]).astype(BF).astype(F32)
    def own_back(pair):
        cols = pl.ds(128 * pair, 128)
        d_a2 = both(d_att[:, 128 * pair : 128 * pair + 128])
        k2, v2 = k_s[:, cols], v_s[:, cols]
        q2, shares = own_shares(pair)
        d_shares = dot_nt(d_a2, v2)
        d_scores = (shares * (d_shares - jnp.sum(d_shares * shares, -1, keepdims=True))).astype(BF)
        d_q2 = dot(d_scores, k2)
        dq[:, cols] = (jnp.where(low_lanes, d_q2[:BLOCK], d_q2[BLOCK:]) * 0.125).astype(BF)
        dkv[:, cols] = dot_tn(d_scores, q2).astype(BF)
        dkv[:, pl.ds(WIDTH + 128 * pair, 128)] = dot_tn(shares.astype(BF), d_a2).astype(BF)

    weave([functools.partial(own_back, pair) for pair in range(6)], (att_steps, 1))

    run(att_steps)
    part[:, pl.ds(0, WIDTH)] = dot_tn(x_rows[...].astype(BF), dq[...]).astype(BF)

    def project_back(i):
        out = dot_tn(x_ref[:, tile(i, 256, 256)], dkv[...])
        part[tile(i, 256, 256), pl.ds(WIDTH, 2 * WIDTH)] = out.astype(BF)

    loop(3, project_back)
    line = iota((128, WIDTH), 0)
    q_line = jnp.sum(dq[...].astype(F32), 0, keepdims=True)
    v_line = jnp.sum(dkv[:, pl.ds(WIDTH, WIDTH)].astype(F32), 0, keepdims=True)
    lines = jnp.where(line == 0, q_line, jnp.where(line == 1, v_line, 0.0))
    part[:, pl.ds(3 * WIDTH, 128)] = lines.T.astype(BF)
    part[:, pl.ds(3 * WIDTH + 128, 128)] = jnp.zeros((WIDTH, 128), BF)

    steps = sum_steps(place, sender, SLOTS + 39, part, work, stage_core, stage_pair, stage_z, final, stage_last, summed)
    run(steps, 1)

    def rows_first(i):
        rows = pl.ds(STREAM * i, STREAM)
        branch = dot(igrad_ref[rows, :], wa[:, pl.ds(2560, WIDTH)]) + vec(2)
        normed, unused = centre(x_ref[rows, :].astype(F32) + branch)
        low = (normed * vec(3) + vec(4)).astype(BF)
        hid_blk[...] = low
        scr[...] = low.astype(F32) + vec(5)

    def rows_inner(j):
        cols = [tile(2 * j + k, 512, 512) for k in range(2)]
        us = [
            dot(hid_blk[...], wa[:, pl.ds(pl.multiple_of(3328 + (2 * j + k) * 512, 128), 512)]) + b1[:, cols[k]]
            for k in range(2)
        ]
        actives = [(u * (0.5 * (1.0 + lax.erf(u * 0.7071067811865476)))).astype(BF) for u in us]
        scr[...] += dot(actives[0], wb[cols[0], :]) + dot(actives[1], wb[cols[1], :])

    def rows_second(i):
        normed, unused = centre(scr[...])
        valid = iota((STREAM, 1), 0) < ends[i][QS - 1]
        hidden_ref[pl.ds(STREAM * i, STREAM), :] = jnp.where(valid, normed * vec(6) + vec(7), 0.0).astype(BF)

    units = []
    for i in range(MICRO):
        units.append(functools.partial(rows_first, i))
        units += [functools.partial(loop, 1, shifted(rows_inner, j)) for j in range(3)]
        units.append(functools.partial(rows_second, i))
    weave(units, (steps, RATE[2]))

    back_rows = dot_nt(dq[...], wa[:, pl.ds(0, WIDTH)]) + own_sum
    q_s[:, pl.ds(0, 128)] = jnp.concatenate([sel[...].astype(F32), jnp.zeros((128 - BLOCK, ROWS), F32)], 0).T.astype(BF)
    back_low = jnp.concatenate([back_rows, jnp.zeros((128 - BLOCK, WIDTH), F32)], 0)
    back_rest = (back_low - back_low.astype(BF).astype(F32)).astype(BF)
    back_low = back_low.astype(BF)

    def input_back(i):
        rows = tile(i, 256, 256)
        total = dot_nt(dkv[rows, pl.ds(0, WIDTH)], wa[:, pl.ds(HALF, WIDTH)])
        total += dot_nt(dkv[rows, pl.ds(WIDTH, cut)], wa[:, pl.ds(WIDTH, cut)])
        total += dot_nt(dkv[rows, pl.ds(WIDTH + cut, cut)], wa[:, pl.ds(HALF + WIDTH, cut)])
        hit_rows = q_s[rows, pl.ds(0, 128)]
        total += dot(hit_rows, back_low) + dot(hit_rows, back_rest)
        igrad_ref[rows, :] = total.astype(BF)

    weave([functools.partial(loop, 2, shifted(input_back, i)) for i in (0, 2)], (steps, 1))

    tall_first = jnp.minimum(place.index * FF_OWN // 128, (FF - 256) // 128) * 128
    tall_at = place.index * FF_OWN - tall_first
    own_first = jnp.minimum(place.index * OWN // 128, (WIDTH - 256) // 128) * 128
    own_at = place.index * OWN - own_first

    window[...] = dot_tn(act[:, pl.ds(pl.multiple_of(tall_first, 128), 256)], d_out[...])
    tw_ref[...] = window[pl.ds(pl.multiple_of(tall_at, 8), FF_OWN), :]
    own_cols = pl.ds(pl.multiple_of(own_first, 128), 256)
    own_lines = pl.ds(pl.multiple_of(own_at, 8), OWN)
    window[...] = dot_tn(cls_att[:, own_cols], d_branch[...])
    ow_ref[...] = window[own_lines, :]
    for j in range(4):
        window[...] = dot_tn(h_low[:, own_cols], slope[:, pl.ds(WIDTH * j, WIDTH)])
        iw_ref[:, pl.ds(WIDTH * j, WIDTH)] = window[own_lines, :]

    def own_lanes(line, first, shift, size):
        window = jnp.broadcast_to(line[:, pl.ds(pl.multiple_of(first, 128), 256)], (8, 256))
        return pltpu.roll(window, 256 - shift, 1)[:1, :size]

    for ref, i in ((g2_ref, 0), (s2_ref, 1), (tb_ref, 2), (g1_ref, 3), (s1_ref, 4), (ob_ref, 5)):
        ref[...] = own_lanes(sums.at[pl.ds(i, 1), :], own_first, own_at, OWN)
    ib_ref[...] = own_lanes(sums_b1, tall_first, tall_at, FF_OWN)

    run(steps)
    qw_ref[...] = summed[:, pl.ds(0, WIDTH)]
    kw_ref[...] = summed[:, pl.ds(WIDTH, WIDTH)]
    vw_ref[...] = summed[:, pl.ds(2 * WIDTH, WIDTH)]
    lines = jnp.concatenate([summed[:, pl.ds(3 * WIDTH, 128)], jnp.zeros((128 - OWN, 128), F32)], 0).T
    qb_ref[...] = lines[0:1, :OWN]
    vb_ref[...] = lines[1:2, :OWN]
    sender.close()


def copy_kernel(count, *refs):
    ins, outs, held, sems = refs[:count], refs[count : 2 * count], refs[2 * count : 3 * count], refs[-1]
    first = [pltpu.make_async_copy(ins[i], held[i], sems.at[0, i]) for i in range(count)]
    second = [pltpu.make_async_copy(held[i], outs[i], sems.at[1, i]) for i in range(count)]
    for copy in first:
        copy.start()
    for i in range(count):
        first[i].wait()
        second[i].start()
    for copy in second:
        copy.wait()


def fast(hidden_in, query_lengths, passage_lengths, positives, stored):
    (query_weight, query_bias, key_weight, value_weight, value_bias, output_weight, output_bias, first_gain,
     first_shift, inner_weight, inner_bias, outer_weight, outer_bias, second_gain, second_shift) = stored
    shapes = [
        ((ROWS, WIDTH), BF), ((ROWS, WIDTH), BF), ((OWN, WIDTH), F32), ((1, OWN), F32), ((OWN, WIDTH), F32),
        ((OWN, WIDTH), F32), ((1, OWN), F32), ((OWN, WIDTH), F32), ((1, OWN), F32), ((1, OWN), F32), ((1, OWN), F32),
        ((OWN, FF), F32), ((1, FF_OWN), F32), ((FF_OWN, WIDTH), F32), ((1, OWN), F32), ((1, OWN), F32), ((1, OWN), F32),
    ]
    scratch = [
        pltpu.VMEM((128, 128), F32), pltpu.VMEM((32, 6400), BF), pltpu.VMEM((32, 3200), BF), pltpu.VMEM((WIDTH, 6400), BF), pltpu.VMEM((FF, WIDTH), BF),
        pltpu.VMEM((16, WIDTH), F32), pltpu.VMEM((1, FF), F32),
        pltpu.VMEM((ROWS, WIDTH), BF), pltpu.VMEM((ROWS, WIDTH), BF), pltpu.VMEM((ROWS, WIDTH), BF),
        pltpu.VMEM((ROWS, STREAM), BF), pltpu.VMEM((BLOCK, ROWS), BF), pltpu.VMEM((8, ROWS), jnp.int32),
        pltpu.VMEM((2 * BLOCK, WIDTH), BF), pltpu.VMEM((2 * BLOCK, WIDTH // 2), BF),
        pltpu.VMEM((2, 2 * BLOCK, WIDTH // 2), BF), pltpu.VMEM((CLS, WIDTH), BF),
        pltpu.VMEM((2 * BLOCK, WIDTH), BF), pltpu.VMEM((2 * BLOCK, WIDTH // 2), BF),
        pltpu.VMEM((2, 2 * BLOCK, WIDTH // 2), BF), pltpu.VMEM((CLS, WIDTH), BF),
        pltpu.VMEM((CLS, WIDTH), F32), pltpu.VMEM((CLS, 128), F32), pltpu.VMEM((CLS, WIDTH), BF),
        pltpu.VMEM((CLS, FF), BF), pltpu.VMEM((CLS, FF), BF),
        pltpu.VMEM((CLS, WIDTH), F32), pltpu.VMEM((CLS, WIDTH), BF), pltpu.VMEM((CLS, WIDTH), BF),
        pltpu.VMEM((8, WIDTH), F32), pltpu.VMEM((1, FF), F32),
        pltpu.VMEM((BLOCK, WIDTH), F32), pltpu.VMEM((BLOCK, WIDTH), F32), pltpu.VMEM((BLOCK, WIDTH), F32),
        pltpu.VMEM((BLOCK, WIDTH), BF), pltpu.VMEM((ROWS, 2 * WIDTH), BF),
        pltpu.VMEM((WIDTH, 2 * HALF), BF),
        pltpu.VMEM((16, 2 * OWN, HALF), BF), pltpu.VMEM((16, 2 * OWN, HALF), BF), pltpu.VMEM((16, 2 * OWN, HALF), BF),
        pltpu.VMEM((4, 2 * OWN, HALF), BF), pltpu.VMEM((OWN, HALF), F32), pltpu.VMEM((OWN, HALF), F32),
        pltpu.VMEM((OWN, 2 * HALF), F32),
        pltpu.SemaphoreType.DMA((380,)), pltpu.SemaphoreType.DMA((20,)), pltpu.SemaphoreType.DMA((SLOTS + 92,)),
    ]
    vmem = pl.BlockSpec(memory_space=pltpu.VMEM)
    smem = pl.BlockSpec(memory_space=pltpu.SMEM)
    outs = pl.pallas_call(
        layer_kernel,
        out_shape=[jax.ShapeDtypeStruct(shape, kind) for shape, kind in shapes],
        in_specs=[vmem] * 16 + [smem] * 3,
        out_specs=[vmem] * len(shapes),
        scratch_shapes=scratch,
        compiler_params=pltpu.CompilerParams(collective_id=0, has_side_effects=True, vmem_limit_bytes=63 * 2**20),
    )(
        hidden_in.reshape(ROWS, WIDTH), query_bias, value_bias, output_bias, first_gain, first_shift, outer_bias,
        second_gain, second_shift, inner_bias, query_weight, key_weight, value_weight, output_weight, inner_weight,
        outer_weight, query_lengths, passage_lengths, positives,
    )
    outs = pl.pallas_call(
        functools.partial(copy_kernel, len(shapes)),
        out_shape=[jax.ShapeDtypeStruct(shape, kind) for shape, kind in shapes],
        in_specs=[pl.BlockSpec(memory_space=pl.ANY)] * len(shapes),
        out_specs=[pl.BlockSpec(memory_space=pl.ANY)] * len(shapes),
        scratch_shapes=[pltpu.VMEM(shape, kind) for shape, kind in shapes] + [pltpu.SemaphoreType.DMA((2, len(shapes)))],
    )(*outs)
    shape = hidden_in.shape
    return tuple(
        out.reshape(shape) if i < 2 else (out.reshape(-1) if out.shape[0] == 1 else out) for i, out in enumerate(outs)
    )


def local(
    hidden_in,
    query_lengths,
    passage_lengths,
    positives,
    query_weight,
    query_bias,
    key_weight,
    value_weight,
    value_bias,
    output_weight,
    output_bias,
    first_gain,
    first_shift,
    inner_weight,
    inner_bias,
    outer_weight,
    outer_bias,
    second_gain,
    second_shift,
):
    stored = (
        query_weight,
        query_bias,
        key_weight,
        value_weight,
        value_bias,
        output_weight,
        output_bias,
        first_gain,
        first_shift,
        inner_weight,
        inner_bias,
        outer_weight,
        outer_bias,
        second_gain,
        second_shift,
    )
    sizes = (lax.axis_size("tower"), lax.axis_size("batch"), hidden_in.shape, inner_weight.shape)
    if sizes == (2, 16, (MICRO, 1, STREAM, WIDTH), (OWN, FF)) and query_lengths.shape[1] == QS:
        return fast(hidden_in, query_lengths, passage_lengths, positives, stored)
    micro = hidden_in.shape[0]
    width = hidden_in.shape[3]
    cls_scale = width ** (-0.5)
    side = lax.axis_index("tower")
    is_query = side == 0
    slot_count = query_lengths.shape[1]
    passage_count = passage_lengths.shape[1]
    half_count = (slot_count + 1) // 2
    extra_rows = 2 * half_count - slot_count
    owners = lax.axis_size(("tower", "batch"))
    totals = tuple(
        (jnp.zeros((item.shape[0] * owners,) + item.shape[1:], jnp.float32) for item in stored)
    )
    half_totals = tuple(
        (jnp.zeros((item.shape[0] * owners // 2,) + item.shape[1:], jnp.float32) for item in stored)
    )
    shown_list = []
    grad_list = []
    for micro_step in range(micro):
        gathered = (
            lax.all_gather(query_weight, ("tower", "batch"), axis=0, tiled=True),
            lax.all_gather(query_bias, ("tower", "batch"), axis=0, tiled=True),
            lax.all_gather(key_weight, ("tower", "batch"), axis=0, tiled=True),
            lax.all_gather(value_weight, ("tower", "batch"), axis=0, tiled=True),
            lax.all_gather(value_bias, ("tower", "batch"), axis=0, tiled=True),
            lax.all_gather(output_weight, ("tower", "batch"), axis=0, tiled=True),
            lax.all_gather(output_bias, ("tower", "batch"), axis=0, tiled=True),
            lax.all_gather(first_gain, ("tower", "batch"), axis=0, tiled=True),
            lax.all_gather(first_shift, ("tower", "batch"), axis=0, tiled=True),
            lax.all_gather(inner_weight, ("tower", "batch"), axis=0, tiled=True),
            lax.all_gather(inner_bias, ("tower", "batch"), axis=0, tiled=True),
            lax.all_gather(outer_weight, ("tower", "batch"), axis=0, tiled=True),
            lax.all_gather(outer_bias, ("tower", "batch"), axis=0, tiled=True),
            lax.all_gather(second_gain, ("tower", "batch"), axis=0, tiled=True),
            lax.all_gather(second_shift, ("tower", "batch"), axis=0, tiled=True),
        )
        params = cast_params(gathered)
        inputs = hidden_in[micro_step, 0]
        passage_part = jnp.pad(passage_lengths[micro_step], (0, slot_count - passage_count))
        lengths = jnp.where(is_query, query_lengths[micro_step], passage_part)
        labels, valid, starts, live = segments(lengths, inputs.shape[0])
        saved, shown = forward(inputs, labels, valid, params)
        shown_list.append(shown)
        mine = jnp.where(live[:, None], shown[starts], 0.0)
        partner = partner_2(mine, "tower", 0)
        query_cls = jnp.where(is_query, mine, partner)
        passage_cls = jnp.where(is_query, partner, mine)[:passage_count]
        pooled = lax.all_gather(passage_cls, "batch", axis=0, tiled=True)
        padded_queries = jnp.pad(query_cls, ((0, extra_rows), (0, 0)))
        padded_targets = jnp.pad(positives[micro_step], (0, extra_rows))
        my_queries = lax.dynamic_slice_in_dim(padded_queries, side * half_count, half_count, 0)
        my_targets = lax.dynamic_slice_in_dim(padded_targets, side * half_count, half_count, 0)
        logits = product_nt(my_queries, pooled) * cls_scale
        highest = jnp.max(logits, -1, keepdims=True)
        powers = jnp.exp(logits - highest)
        shares = powers / jnp.sum(powers, -1, keepdims=True)
        columns = jnp.arange(pooled.shape[0], dtype=jnp.int32)
        target = (columns[None, :] == my_targets[:, None]).astype(jnp.float32)
        grad_logits = ((shares - target) / micro).astype(jnp.bfloat16)
        own_grad = product(grad_logits, pooled) * cls_scale
        pooled_grad = product_tn(grad_logits, my_queries) * cls_scale
        summed = lax.psum_scatter(pooled_grad, "batch", scatter_dimension=0, tiled=True)
        other_queries, other_passages = (
            partner_2(own_grad.astype(jnp.bfloat16), "tower", 0).astype(own_grad.dtype),
            partner_2(summed.astype(jnp.bfloat16), "tower", 0).astype(summed.dtype),
        )
        query_grad = jnp.concatenate([own_grad, other_queries], 0)[:slot_count]
        passage_grad = jnp.pad(summed + other_passages, ((0, slot_count - passage_count), (0, 0)))
        cotangent = jnp.where(is_query, query_grad, passage_grad)
        input_part, step_grads = backward(inputs, labels, cotangent, starts, live, saved, params)
        grad_list.append(input_part)
        totals = tuple((first + second for first, second in zip(totals, step_grads)))
    keep_all, give_all = split_halves(totals, side)
    came_all = jax.tree.map(
        lambda part, own: part.astype(own.dtype), partner_2(as_sent(give_all), "tower", 0), give_all
    )
    half_totals = tuple((first + second for first, second in zip(keep_all, came_all)))
    shards = lax.psum_scatter(half_totals, "batch", scatter_dimension=0, tiled=True)
    hidden_out = jnp.stack(shown_list)[:, None]
    input_grad = jnp.stack(grad_list)[:, None]
    return (
        hidden_out,
        input_grad,
        shards[0],
        shards[1],
        shards[2],
        shards[3],
        shards[4],
        shards[5],
        shards[6],
        shards[7],
        shards[8],
        shards[9],
        shards[10],
        shards[11],
        shards[12],
        shards[13],
        shards[14],
    )


def solution(mesh):
    placed = (
        P(None, "tower", "batch", None),
        P(None, "batch"),
        P(None, "batch"),
        P(None, "batch"),
        P(("tower", "batch"), None),
        P(("tower", "batch")),
        P(("tower", "batch"), None),
        P(("tower", "batch"), None),
        P(("tower", "batch")),
        P(("tower", "batch"), None),
        P(("tower", "batch")),
        P(("tower", "batch")),
        P(("tower", "batch")),
        P(("tower", "batch"), None),
        P(("tower", "batch")),
        P(("tower", "batch"), None),
        P(("tower", "batch")),
        P(("tower", "batch")),
        P(("tower", "batch")),
    )
    return jax.shard_map(
        local,
        mesh=mesh,
        in_specs=placed,
        out_specs=(
            P(None, "tower", "batch", None),
            P(None, "tower", "batch", None),
            P(("tower", "batch"), None),
            P(("tower", "batch")),
            P(("tower", "batch"), None),
            P(("tower", "batch"), None),
            P(("tower", "batch")),
            P(("tower", "batch"), None),
            P(("tower", "batch")),
            P(("tower", "batch")),
            P(("tower", "batch")),
            P(("tower", "batch"), None),
            P(("tower", "batch")),
            P(("tower", "batch"), None),
            P(("tower", "batch")),
            P(("tower", "batch")),
            P(("tower", "batch")),
        ),
        check_vma=False,
    )
```

```python
import functools

import jax
import jax.numpy as jnp
from jax import lax
from jax.experimental import pallas as pl
from jax.experimental.pallas import tpu as pltpu
from jax.sharding import PartitionSpec as P

HEADS = 12


EPSILON = 1e-12
MASKED = -1e30


def partner_2(x, axis, apart):
    return lax.ppermute(x, axis, [(i, i ^ 1 << apart) for i in range(lax.axis_size(axis))])


def as_sent(x):
    return jax.tree.map(lambda a: a.astype(jnp.bfloat16) if a.dtype == jnp.float32 else a, x)


def product(left, right):
    return jnp.dot(left, right, preferred_element_type=jnp.float32)


def product_tn(left, right):
    return jnp.einsum("ta,tb->ab", left, right, preferred_element_type=jnp.float32)


def product_nt(left, right):
    return jnp.einsum("ra,ba->rb", left, right, preferred_element_type=jnp.float32)


def normalize(values, gains, shifts):
    average = jnp.mean(values, -1, keepdims=True)
    centred = values - average
    inverse = lax.rsqrt(jnp.mean(centred * centred, -1, keepdims=True) + EPSILON)
    normed = centred * inverse
    return (normed * gains + shifts, normed, inverse)


def normalize_back(upstream, normed, inverse, gains):
    scaled = upstream * gains
    inner = (
        scaled
        - jnp.mean(scaled, -1, keepdims=True)
        - normed * jnp.mean(scaled * normed, -1, keepdims=True)
    )
    return (inner * inverse, jnp.sum(upstream * normed, 0), jnp.sum(upstream, 0))


def gelu_slope(values):
    return (
        0.5 * (1.0 + lax.erf(values * 0.7071067811865476))
        + values * jnp.exp(-0.5 * values * values) * 0.3989422804014327
    )


def segments(lengths, token_rows):
    ends = jnp.cumsum(lengths)
    places = jnp.arange(token_rows, dtype=jnp.int32)
    labels = jnp.sum((places[:, None] >= ends[None, :]).astype(jnp.int32), 1)
    starts = jnp.minimum(ends - lengths, token_rows - 1)
    return (labels, places < ends[-1], starts, lengths > 0)


def tail(inputs, attended, params):
    out_mat, out_vec, gain_one, shift_one = (params[5], params[6], params[7], params[8])
    inner_mat, inner_vec, outer_mat, outer_vec, gain_two, shift_two = params[9:15]
    branch = product(attended, out_mat) + out_vec
    hidden_full, normed_one, inverse_one = normalize(
        inputs.astype(jnp.float32) + branch, gain_one, shift_one
    )
    hidden_low = hidden_full.astype(jnp.bfloat16)
    inner = product(hidden_low, inner_mat) + inner_vec
    active = jax.nn.gelu(inner, approximate=False).astype(jnp.bfloat16)
    outer = product(active, outer_mat) + outer_vec
    result, normed_two, inverse_two = normalize(
        hidden_low.astype(jnp.float32) + outer, gain_two, shift_two
    )
    return (result, (normed_one, inverse_one, hidden_low, inner, active, normed_two, inverse_two))


def forward(inputs, labels, valid, params):
    query_mat, query_vec, key_mat, value_mat, value_vec = params[0:5]
    token_rows, width = inputs.shape
    head_size = width // HEADS
    scale = head_size ** (-0.5)
    queries = (product(inputs, query_mat) + query_vec).astype(jnp.bfloat16)
    keys = product(inputs, key_mat).astype(jnp.bfloat16)
    values = (product(inputs, value_mat) + value_vec).astype(jnp.bfloat16)
    block_rows = min(512, token_rows)

    def one_block(first_row):
        allowed = labels[:, None] == labels[None, :]

        def one_head(head_index):
            head_queries = lax.dynamic_slice_in_dim(queries, head_index * head_size, head_size, 1)
            head_keys = lax.dynamic_slice_in_dim(keys, head_index * head_size, head_size, 1)
            head_values = lax.dynamic_slice_in_dim(values, head_index * head_size, head_size, 1)
            scores = jnp.where(allowed, product_nt(head_queries, head_keys) * scale, MASKED)
            highest = jnp.max(scores, -1, keepdims=True)
            powers = jnp.exp(scores - highest)
            totals = jnp.sum(powers, -1, keepdims=True)
            shares = (powers / totals).astype(jnp.bfloat16)
            return (product(shares, head_values), (highest + jnp.log(totals))[:, 0])

        head_out, head_lse = lax.map(one_head, jnp.arange(HEADS, dtype=jnp.int32))
        attended = (
            jnp.transpose(head_out, (1, 0, 2)).reshape(block_rows, width).astype(jnp.bfloat16)
        )
        result, unused = tail(inputs, attended, params)
        shown = jnp.where(valid[:, None], result, 0.0).astype(jnp.bfloat16)
        return (attended, head_lse, shown)

    firsts = jnp.arange(token_rows // block_rows, dtype=jnp.int32) * block_rows
    attended, lse_blocks, shown = lax.map(one_block, firsts)
    attended = attended.reshape(token_rows, width)
    shown = shown.reshape(token_rows, width)
    lse_all = jnp.transpose(lse_blocks, (1, 0, 2)).reshape(HEADS, token_rows)
    return ((queries, keys, values, attended, lse_all), shown)


def backward(inputs, labels, cotangent, starts, live, saved, params):
    queries, keys, values, attended, lse_all = saved
    query_mat, key_mat, value_mat, out_mat = (params[0], params[2], params[3], params[5])
    gain_one, inner_mat, outer_mat, gain_two = (params[7], params[9], params[11], params[13])
    token_rows, width = inputs.shape
    head_size = width // HEADS
    scale = head_size ** (-0.5)
    slot_count = starts.shape[0]
    row_inputs = inputs[starts]
    row_attended = attended[starts]
    unused, kept = tail(row_inputs, row_attended, params)
    normed_one, inverse_one, hidden_low, inner, active, normed_two, inverse_two = kept
    upstream = jnp.where(live[:, None], cotangent, 0.0)
    grad_sum_two, grad_gain_two, grad_shift_two = normalize_back(
        upstream, normed_two, inverse_two, gain_two
    )
    grad_outer = grad_sum_two.astype(jnp.bfloat16)
    grad_outer_mat = product_tn(active, grad_outer)
    grad_outer_vec = jnp.sum(grad_outer.astype(jnp.float32), 0)
    grad_inner = (product_nt(grad_outer, outer_mat) * gelu_slope(inner)).astype(jnp.bfloat16)
    grad_inner_mat = product_tn(hidden_low, grad_inner)
    grad_inner_vec = jnp.sum(grad_inner.astype(jnp.float32), 0)
    grad_hidden = grad_sum_two + product_nt(grad_inner, inner_mat)
    grad_sum_one, grad_gain_one, grad_shift_one = normalize_back(
        grad_hidden, normed_one, inverse_one, gain_one
    )
    grad_branch = grad_sum_one.astype(jnp.bfloat16)
    grad_out_mat = product_tn(row_attended, grad_branch)
    grad_out_vec = jnp.sum(grad_branch.astype(jnp.float32), 0)
    grad_attended = (
        product_nt(grad_branch, out_mat).astype(jnp.bfloat16).reshape(slot_count, HEADS, head_size)
    )
    row_queries = queries[starts].reshape(slot_count, HEADS, head_size)
    keys_split = keys.reshape(token_rows, HEADS, head_size)
    values_split = values.reshape(token_rows, HEADS, head_size)
    allowed = labels[starts][None, :, None] == labels[None, None, :]
    scores = (
        jnp.einsum("rhd,thd->hrt", row_queries, keys_split, preferred_element_type=jnp.float32)
        * scale
    )
    shares = jnp.where(allowed, jnp.exp(scores - lse_all[:, starts][:, :, None]), 0.0)
    shares_low = shares.astype(jnp.bfloat16)
    grad_shares = jnp.einsum(
        "rhd,thd->hrt", grad_attended, values_split, preferred_element_type=jnp.float32
    )
    grad_scores = (
        shares * (grad_shares - jnp.sum(grad_shares * shares, -1, keepdims=True))
    ).astype(jnp.bfloat16)
    grad_queries = (
        jnp.einsum("hrt,thd->rhd", grad_scores, keys_split, preferred_element_type=jnp.float32)
        * scale
    )
    grad_queries = grad_queries.reshape(slot_count, width).astype(jnp.bfloat16)
    grad_keys = (
        jnp.einsum("hrt,rhd->thd", grad_scores, row_queries, preferred_element_type=jnp.float32)
        * scale
    )
    grad_keys = grad_keys.reshape(token_rows, width).astype(jnp.bfloat16)
    grad_values = jnp.einsum(
        "hrt,rhd->thd", shares_low, grad_attended, preferred_element_type=jnp.float32
    )
    grad_values = grad_values.reshape(token_rows, width).astype(jnp.bfloat16)
    grad_inputs = product_nt(grad_keys, key_mat) + product_nt(grad_values, value_mat)
    grad_inputs = grad_inputs.at[starts].add(product_nt(grad_queries, query_mat) + grad_sum_one)
    grads = (
        product_tn(row_inputs, grad_queries),
        jnp.sum(grad_queries.astype(jnp.float32), 0),
        product_tn(inputs, grad_keys),
        product_tn(inputs, grad_values),
        jnp.sum(grad_values.astype(jnp.float32), 0),
        grad_out_mat,
        grad_out_vec,
        grad_gain_one,
        grad_shift_one,
        grad_inner_mat,
        grad_inner_vec,
        grad_outer_mat,
        grad_outer_vec,
        grad_gain_two,
        grad_shift_two,
    )
    return (grad_inputs.astype(jnp.bfloat16), grads)


def cast_params(gathered):
    vector_places = (1, 4, 6, 7, 8, 10, 12, 13, 14)
    return tuple(
        (
            item.astype(jnp.float32) if place in vector_places else item
            for place, item in enumerate(gathered)
        )
    )


def split_halves(grads, side):
    keep_list = []
    give_list = []
    for item in grads:
        half = item.shape[0] // 2
        keep_list.append(lax.dynamic_slice_in_dim(item, side * half, half, 0))
        give_list.append(lax.dynamic_slice_in_dim(item, (1 - side) * half, half, 0))
    return (tuple(keep_list), tuple(give_list))


MESH = pl.DeviceIdType.MESH
BLOCK = 40
QS, PS, STREAM, WIDTH, FF, MICRO = 17, 2, 512, 768, 3072, 2
ROWS = MICRO * STREAM
CLS = 16 * BLOCK
HALF = 1280
PART = (HALF, 1152, 768)
FIRST = (0, 2560, 4864)
CHUNKS = (
    (0, 0, 640, 256, 384), (0, 640, 640, 256, 384), (1, 0, 768, 256, 512), (1, 768, 384, 128, 256), (2, 0, 768, 256, 512),
    (3, 0, 48, 16, 32), (3, 48, 48, 16, 32),
)
SHORT = (0, 1, 5, 6)
SLOTS = 40 * len(CHUNKS)
OWN = 24
FF_OWN = 96
BF, F32 = jnp.bfloat16, jnp.float32
OFF = ()
RATE = (3, 4, 0.5, 2, 1, (4, 4, 4, 4, 4, 4, 4))
START = (0, 0, 1, 2, 3, 4, 5)
LEAD = 2


class Place:
    def __init__(self):
        self.x = lax.axis_index("tower")
        self.batch = lax.axis_index("batch")
        self.core = self.batch % 2
        self.y = (self.batch // 2) % 2
        self.z = self.batch // 4
        self.index = self.x * 16 + self.batch

    def device(self, x=None, y=None, z=None, core=None):
        x = self.x if x is None else x
        y = self.y if y is None else y
        z = self.z if z is None else z
        core = self.core if core is None else core
        return (x, z * 4 + y * 2 + core)

    def chip(self, x=None, y=None, z=None):
        x = self.x if x is None else x
        y = self.y if y is None else y
        z = self.z if z is None else z
        return x * 8 + z * 2 + y

    def layer(self, step):
        if step == 0:
            return self.z
        if step == 1:
            return self.z + 1 - 2 * (self.z % 2)
        if step == 2:
            return (self.z + 2) % 4
        return 3 - self.z

    @property
    def sibling(self):
        return self.device(core=1 - self.core)

    @property
    def over_x(self):
        return self.device(x=1 - self.x)

    @property
    def over_y(self):
        return self.device(y=1 - self.y)


def greet(place):
    barrier = pltpu.get_barrier_semaphore()
    peers = [place.device(z=place.layer(step)) for step in (1, 2, 3)]
    peers += [place.over_x, place.over_y, place.sibling]
    for peer in peers:
        pl.semaphore_signal(barrier, inc=1, device_id=peer, device_id_type=MESH)
    return lambda: pl.semaphore_wait(barrier, len(peers))


class Sender:
    def __init__(self, place, send_sems, recv_sems):
        self.place = place
        self.send_sems = send_sems
        self.recv_sems = recv_sems
        self.used = 0
        self.open = []

    def send(self, src, dst, slot, peer, only=None):
        copy = pltpu.make_async_remote_copy(
            src_ref=src,
            dst_ref=dst,
            send_sem=self.send_sems.at[self.used],
            recv_sem=self.recv_sems.at[slot],
            device_id=peer,
            device_id_type=MESH,
        )
        self.used += 1
        if only is None:
            copy.start()
        else:
            pl.when(only)(copy.start)
        self.open.append((copy, only))

    def arrived(self, dst, slot):
        pltpu.make_async_remote_copy(
            src_ref=dst,
            dst_ref=dst,
            send_sem=self.send_sems.at[0],
            recv_sem=self.recv_sems.at[slot],
            device_id=self.place.sibling,
            device_id_type=MESH,
        ).wait_recv()

    def close(self):
        for copy, only in self.open:
            if only is None:
                copy.wait_send()
            else:
                pl.when(only)(copy.wait_send)
        self.open = []


def tile(index, size, unit):
    return pl.ds(pl.multiple_of(index * unit, unit), size)


def loop(count, body):
    if getattr(body, '__name__', '') in OFF or 'all' in OFF:
        return
    def step(index, carry):
        body(index)
        return carry

    lax.fori_loop(0, count, step, 0)


def shifted(body, by):
    def moved(index):
        body(index + by)
    moved.__name__ = body.__name__
    return moved


def dot(left, right):
    return jnp.dot(left, right, preferred_element_type=F32)


def dot_nt(left, right):
    return lax.dot_general(left, right, (((1,), (1,)), ((), ())), preferred_element_type=F32)


def dot_tn(left, right):
    return lax.dot_general(left, right, (((0,), (0,)), ((), ())), preferred_element_type=F32)


def iota(shape, dim):
    return lax.broadcasted_iota(jnp.int32, shape, dim)


def centre(values):
    average = jnp.mean(values, -1, keepdims=True)
    centred = values - average
    inverse = lax.rsqrt(jnp.mean(centred * centred, -1, keepdims=True) + EPSILON)
    return centred * inverse, inverse


def centre_back(scaled, normed, inverse):
    return inverse * (
        scaled - jnp.mean(scaled, -1, keepdims=True) - normed * jnp.mean(scaled * normed, -1, keepdims=True)
    )


def weight_steps(place, sender, all_wide, all_tall):
    middle = (place.z == 1) | (place.z == 2)

    def view(chunk, core, chip, start=0, stop=None):
        part, offset, size, unused, unused = CHUNKS[chunk]
        size = (size if stop is None else stop) - start
        if part < 3:
            first = pl.multiple_of(FIRST[part] + core * PART[part] + offset + start, 128)
            return all_wide.at[tile(chip, 2 * OWN, 2 * OWN), pl.ds(first, size)]
        first = pl.multiple_of((chip * 2 + core) * FF_OWN + offset + start, 16)
        return all_tall.at[pl.ds(first, size), :]

    def slot(chunk, kind, layer):
        return (chunk * 10 + kind) * 4 + layer

    def along_z(chunk, block, at):
        sender.send(block, block, at, place.device(z=place.layer(1)))
        sender.send(block, block, at, place.device(z=place.layer(2)))
        sender.send(block, block, at, place.device(z=place.layer(3)), only=None if chunk in SHORT else middle)

    def begin(chunk):
        own = view(chunk, place.core, place.chip())
        along_z(chunk, own, slot(chunk, 0, place.z))
        sender.send(own, own, slot(chunk, 1, place.z), place.over_x)
        sender.send(own, own, slot(chunk, 2, place.z), place.over_y)
        sender.send(own, own, slot(chunk, 5, place.z), place.sibling)

    def along(chunk, step):
        layer = place.layer(step)
        block = view(chunk, place.core, place.chip(z=layer))
        sender.arrived(block, slot(chunk, 0, layer))
        if step == 2 and chunk not in SHORT:
            sender.send(block, block, slot(chunk, 0, layer), place.device(z=place.layer(1)), only=middle)
        sender.send(block, block, slot(chunk, 1, layer), place.over_x)
        sender.send(block, block, slot(chunk, 2, layer), place.over_y)
        sender.send(block, block, slot(chunk, 5, layer), place.sibling)

    def across(chunk, step):
        layer = place.layer(step)
        chip_x, chip_y = place.chip(x=1 - place.x, z=layer), place.chip(y=1 - place.y, z=layer)
        short = chunk in SHORT
        first, second = CHUNKS[chunk][3:]
        from_x, from_y = view(chunk, place.core, chip_x), view(chunk, place.core, chip_y)
        sender.arrived(from_x, slot(chunk, 1, layer))
        if step < 2:
            piece = from_x if short else view(chunk, place.core, chip_x, 0, second if step == 0 else first)
            sender.send(piece, piece, slot(chunk, 3, layer), place.over_y)
        sender.send(from_x, from_x, slot(chunk, 6, layer), place.sibling)
        sender.arrived(from_y, slot(chunk, 2, layer))
        if step >= 2:
            piece = from_y if short else view(chunk, place.core, chip_y, 0, first)
            sender.send(piece, piece, slot(chunk, 3, layer), place.over_x)
        if step == 0 and not short:
            piece = view(chunk, place.core, chip_y, second)
            sender.send(piece, piece, slot(chunk, 4, layer), place.over_x)
        sender.send(from_y, from_y, slot(chunk, 7, layer), place.sibling)

    def far(layer):
        return place.chip(x=1 - place.x, y=1 - place.y, z=layer)

    def corner(chunk):
        first, second = CHUNKS[chunk][3:]
        sender.arrived(view(chunk, place.core, far(place.z), 0, second), slot(chunk, 3, place.z))
        sender.arrived(view(chunk, place.core, far(place.z), second), slot(chunk, 4, place.z))
        rest = view(chunk, place.core, far(place.z), first)
        along_z(chunk, rest, slot(chunk, 4, place.z))
        block = view(chunk, place.core, far(place.z))
        sender.send(block, block, slot(chunk, 8, place.z), place.sibling)

    def corner_along(chunk, step):
        layer = place.layer(step)
        rest = view(chunk, place.core, far(layer), CHUNKS[chunk][3])
        sender.arrived(rest, slot(chunk, 4, layer))
        if step == 2:
            sender.send(rest, rest, slot(chunk, 4, layer), place.device(z=place.layer(1)), only=middle)
        sender.send(rest, rest, slot(chunk, 9, layer), place.sibling)

    def corner_third(chunk, step):
        layer = place.layer(step)
        piece = view(chunk, place.core, far(layer), 0, None if chunk in SHORT else CHUNKS[chunk][3])
        sender.arrived(piece, slot(chunk, 3, layer))
        sender.send(piece, piece, slot(chunk, 8, layer), place.sibling)

    def twin(chunk):
        core = 1 - place.core
        for step in range(4):
            layer = place.layer(step)
            sender.arrived(view(chunk, core, place.chip(z=layer)), slot(chunk, 5, layer))
            sender.arrived(view(chunk, core, place.chip(x=1 - place.x, z=layer)), slot(chunk, 6, layer))
            sender.arrived(view(chunk, core, place.chip(y=1 - place.y, z=layer)), slot(chunk, 7, layer))
            if step == 0 or chunk in SHORT:
                sender.arrived(view(chunk, core, far(layer)), slot(chunk, 8, layer))
            else:
                sender.arrived(view(chunk, core, far(layer), 0, CHUNKS[chunk][3]), slot(chunk, 8, layer))
                sender.arrived(view(chunk, core, far(layer), CHUNKS[chunk][3]), slot(chunk, 9, layer))

    def steps():
        usual = (
            (5, twin, (None,)), (4, corner_along, (3,)), (3, corner_along, (1, 2)), (3, corner_third, (3,)),
            (2, corner, (None,)), (2, corner_third, (1, 2)), (2, across, (3,)), (1, across, (0, 1, 2)),
            (1, along, (3,)), (0, along, (1, 2)),
        )
        short = ((3, twin, (None,)), (2, corner_third, (0, 1, 2, 3)), (1, across, (0, 1, 2, 3)), (0, along, (1, 2, 3)))
        count = len(CHUNKS)
        for turn in range(START[-1] + 6):
            for chunk in range(count):
                for late, stage, places in short if chunk in SHORT else usual:
                    if START[chunk] == turn - late:
                        for step in places:
                            if step is None:
                                stage(chunk)
                            else:
                                stage(chunk, step)
                            yield chunk if stage is twin else None
            for chunk in range(count):
                if START[chunk] == turn + LEAD:
                    begin(chunk)

    return begin, steps


def cls_steps(place, sender, base, block_ref, merged, stage, out_ref):
    rows, half = 2 * BLOCK, WIDTH // 2
    mine = tile(place.core, half, half)
    other = tile(1 - place.core, half, half)

    def view(core, y, z):
        return out_ref.at[tile(z * 2 + y, rows, rows), tile(core, half, half)]

    sender.send(block_ref.at[:, other], stage.at[0], base, place.sibling)
    yield
    sender.arrived(stage.at[0], base)
    merged[...] = (block_ref[:, mine].astype(F32) + stage[0].astype(F32)).astype(BF)
    sender.send(merged, stage.at[1], base + 1, place.over_x)
    yield
    sender.arrived(stage.at[1], base + 1)
    own = view(place.core, place.y, place.z)
    own[...] = (merged[...].astype(F32) + stage[1].astype(F32)).astype(BF)
    for step in (3, 2, 1):
        sender.send(own, own, base + 2 + place.z, place.device(z=place.layer(step)))
    for step in range(4):
        layer = place.layer(step)
        block = view(place.core, place.y, layer)
        if step > 0:
            yield
            sender.arrived(block, base + 2 + layer)
        sender.send(block, block, base + 6 + layer, place.over_y)
        sender.send(block, block, base + 10 + layer, place.sibling)
    for step in range(4):
        yield
        layer = place.layer(step)
        block = view(place.core, 1 - place.y, layer)
        sender.arrived(block, base + 6 + layer)
        sender.send(block, block, base + 14 + layer, place.sibling)
    yield
    for step in range(4):
        layer = place.layer(step)
        sender.arrived(view(1 - place.core, place.y, layer), base + 10 + layer)
        sender.arrived(view(1 - place.core, 1 - place.y, layer), base + 14 + layer)


def sum_begin(place, sender, base, part_ref, stage_core, first, last):
    other = tile(1 - place.core, HALF, HALF)
    for chip in range(first, last):
        sender.send(part_ref.at[pl.ds(2 * OWN * chip, 2 * OWN), other], stage_core.at[chip], base + chip, place.sibling)


def sum_steps(place, sender, base, part_ref, work, stage_core, stage_pair, stage_z, final, stage_last, out_ref):
    mine = tile(place.core, HALF, HALF)
    other = tile(1 - place.core, HALF, HALF)
    order = (3, 2, 1, 0)
    blocks = [(dx, dy, step) for step in order for dx, dy in ((1, 1), (1, 0), (0, 1), (0, 0))]

    def x_first(step):
        return step % 2 == 0

    def chip_of(dx, dy, step):
        return place.chip(1 - place.x if dx else place.x, 1 - place.y if dy else place.y, place.layer(step))

    def add(index, landed):
        work[index] = (work[index].astype(F32) + landed.astype(F32)).astype(BF)

    for index, at in enumerate(blocks):
        if index % 4 == 0:
            yield
        dx, dy, step = at
        chip = chip_of(*at)
        sender.arrived(stage_core.at[chip], base + chip)
        work[index] = (part_ref[tile(chip, 2 * OWN, 2 * OWN), mine].astype(F32) + stage_core[chip].astype(F32)).astype(BF)
        if (dx if x_first(step) else dy) == 1:
            peer = place.over_x if x_first(step) else place.over_y
            sender.send(work.at[index], stage_pair.at[index], base + 16 + index, peer)

    def first_add(step):
        for second in (1, 0):
            keep = (0, second) if x_first(step) else (second, 0)
            sent = (1, second) if x_first(step) else (second, 1)
            index, source = blocks.index(keep + (step,)), blocks.index(sent + (step,))
            sender.arrived(stage_pair.at[source], base + 16 + source)
            add(index, stage_pair[source])
            if second:
                peer = place.over_y if x_first(step) else place.over_x
                sender.send(work.at[index], stage_pair.at[index], base + 32 + index, peer)

    def second_add(step):
        index = blocks.index((0, 0, step))
        source = blocks.index(((0, 1) if x_first(step) else (1, 0)) + (step,))
        sender.arrived(stage_pair.at[source], base + 32 + source)
        add(index, stage_pair[source])
        if step:
            sender.send(work.at[index], stage_z.at[step], base + 48 + step, place.device(z=place.layer(step)))

    yield
    first_add(3)
    yield
    first_add(2)
    yield
    second_add(3)
    yield
    first_add(1)
    yield
    second_add(2)
    yield
    first_add(0)
    yield
    second_add(1)
    yield
    second_add(0)
    yield
    total = work[blocks.index((0, 0, 0))].astype(F32)
    for step in (3, 2, 1):
        sender.arrived(stage_z.at[step], base + 48 + step)
        total = total + stage_z[step].astype(F32)
    top, low = total[:OWN], total[OWN:]
    is_first = place.core == 0
    final[...] = jnp.where(is_first, low, top)
    sender.send(final, stage_last, base + 52, place.sibling)
    out_ref[:, mine] = jnp.where(is_first, top, low)
    yield
    sender.arrived(stage_last, base + 52)
    out_ref[:, other] = stage_last[...]


def weave(units, *steps):
    for index, unit in enumerate(units):
        unit()
        for generator, count in steps:
            run(generator, int((index + 1) * count) - int(index * count))


def run_to(steps, chunk):
    for done in steps:
        if done == chunk:
            return


def run(steps, count=None):
    while count is None or count > 0:
        if next(steps, "end") == "end":
            return
        if count is not None:
            count -= 1


def layer_kernel(
    x_ref, bq_ref, bv_ref, bo_ref, g1_in, s1_in, b2_ref, g2_in, s2_in, b1_ref, wq_ref, wk_ref, wv_ref, wo_ref, w1_ref, w2_ref, qlen_ref, plen_ref, pos_ref,
    hidden_ref, igrad_ref, qw_ref, qb_ref, kw_ref, vw_ref, vb_ref, ow_ref, ob_ref, g1_ref, s1_ref, iw_ref, ib_ref,
    tw_ref, tb_ref, g2_ref, s2_ref,
    lines_s, wide, stage, wa, wb, vecs, b1, q_s, k_s, v_s, bias, sel, code,
    block, merged, cls_stage, cls, att_block, att_merged, att_stage, cls_att, n1, columns, h_low, slope, act, n2, d_out, d_branch, sums, sums_b1,
    q_rows, x_rows, att_rows, dq, dkv, part, work, stage_core, stage_pair, stage_z, final, stage_last, summed,
    send_sems, cls_sems, recv_sems,
):
    place = Place()
    sender = Sender(place, send_sems, recv_sems)
    cls_sender = Sender(place, cls_sems, recv_sems)
    is_query = place.x == 0
    core = place.core
    scr = n1.at[pl.ds(0, STREAM), :]
    window = n1.at[pl.ds(0, 256), :]

    all_here = greet(place)

    cut = WIDTH // 2
    lines_s[...] = jnp.zeros_like(lines_s)
    for i, ref in enumerate((bq_ref, bv_ref, bo_ref, g1_in, s1_in, b2_ref, g2_in, s2_in)):
        lines_s[pl.ds(i, 1), pl.ds(0, OWN)] = ref[...].astype(F32).reshape(1, OWN)
    lines_s[pl.ds(16, 1), pl.ds(0, FF_OWN)] = b1_ref[...].astype(F32).reshape(1, FF_OWN)
    long_line = jnp.broadcast_to(lines_s[pl.ds(16, 1), :], (8, 128))
    for i in range(4):
        turned = long_line if i == 0 else pltpu.roll(long_line, 128 - OWN * i, 1)
        lines_s[pl.ds(8 + i, 1), :] = turned[:1, :]
    vec_cols = lines_s[...].T[:OWN, :].astype(BF)
    filled = (
        (wq_ref, 0, WIDTH, 0), (wv_ref, 0, cut, 768), (wk_ref, 0, WIDTH, 1280), (wv_ref, cut, cut, 2048),
        (wo_ref, 0, WIDTH, 2560), (w1_ref, 0, FF, 3328),
    )
    for at in (1152, 2432):
        wide[:, pl.ds(at, 128)] = jnp.zeros((32, 128), BF)
    for ref, start, size, at in filled:
        wide[pl.ds(0, OWN), pl.ds(at, size)] = ref[:, pl.ds(start, size)]
        wide[pl.ds(OWN, 8), pl.ds(at, size)] = jnp.zeros((8, size), BF)
    wide[pl.ds(0, OWN), pl.ds(1152, 128)] = vec_cols
    all_here()

    begin, weight_parts = weight_steps(place, sender, wa, wb)
    offsets = (0, HALF, HALF + PART[1])
    for chunk in range(3):
        first = pl.multiple_of(FIRST[chunk] + (1 - core) * PART[chunk], 128)
        landing = stage.at[:, pl.ds(offsets[chunk], PART[chunk])]
        sender.send(wide.at[:, pl.ds(first, PART[chunk])], landing, SLOTS + chunk, place.sibling)
    wb[tile(place.index, FF_OWN, FF_OWN), :] = w2_ref[...]

    def assemble(chunk):
        sender.arrived(stage.at[:, pl.ds(offsets[chunk], PART[chunk])], SLOTS + chunk)
        first = pl.multiple_of(FIRST[chunk] + core * PART[chunk], 128)
        mine = wide[pl.ds(0, OWN), pl.ds(first, PART[chunk])].astype(F32)
        other = stage[pl.ds(0, OWN), pl.ds(offsets[chunk], PART[chunk])].astype(F32)
        top, low = jnp.where(core == 0, mine, other), jnp.where(core == 0, other, mine)
        wa[tile(place.chip(), 2 * OWN, 2 * OWN), pl.ds(first, PART[chunk])] = jnp.concatenate([top, low], 0).astype(BF)

    assemble(0)
    for chunk in range(len(CHUNKS)):
        if START[chunk] == 0:
            begin(chunk)
    assemble(1)
    assemble(2)
    for chunk in range(len(CHUNKS)):
        if 0 < START[chunk] < LEAD:
            begin(chunk)

    ends, starts = [], []
    for m in range(MICRO):
        end = jnp.int32(0)
        ends.append([])
        starts.append([])
        for i in range(QS):
            length = jnp.where(is_query, qlen_ref[m, i], plen_ref[m, i] if i < PS else 0)
            starts[m].append(end)
            end = end + length
            ends[m].append(end)
    def cls_places(rows, offset):
        at = iota((rows, 128), 0)
        found = jnp.full((rows, 128), -1, jnp.int32)
        label = jnp.full((rows, 128), -1, jnp.int32)
        for m in range(MICRO):
            for i in range(QS):
                row = jnp.where(is_query, QS * m + i, MICRO * QS + PS * m + i if i < PS else -1000) + offset
                found = jnp.where(at == row, m * STREAM + starts[m][i], found)
                label = jnp.where(at == row, m * 64 + i, label)
        return found[:, :1], label[:, :1]

    found, label = cls_places(BLOCK, 0)
    sel[...] = (found == iota((BLOCK, ROWS), 1)).astype(BF)
    ours = label >= 0
    low_lanes = iota((BLOCK, 128), 1) < 64
    coded = jnp.zeros((BLOCK, 128), jnp.int32)
    at_row, at_lane = iota((BLOCK, 128), 0), iota((BLOCK, 128), 1)
    for m in range(MICRO):
        for i in range(QS):
            here = (at_row == jnp.where(is_query, -1000, BLOCK - MICRO + m)) & (at_lane == i)
            coded = jnp.where(here, pos_ref[m, i], coded)
    coded = coded.astype(F32)

    def both(rows):
        return jnp.concatenate([jnp.where(low_lanes, rows, 0.0), jnp.where(low_lanes, 0.0, rows)], 0).astype(BF)

    def for_chip(rows):
        nothing = jnp.zeros_like(rows)
        return jnp.concatenate([jnp.where(core == 0, rows, nothing), jnp.where(core == 0, nothing, rows)], 0).astype(BF)

    x_rows[...] = dot(sel[...], x_ref[...])
    block[...] = for_chip(x_rows[...])
    block[:, pl.ds(0, 128)] = for_chip(x_rows[:, pl.ds(0, 128)] + coded)
    x_parts = cls_steps(place, cls_sender, SLOTS + 3, block, merged, cls_stage, cls)
    run(x_parts, 1)
    weights = weight_parts()

    row_of_key = iota((8, STREAM), 1)
    row_of_query = iota((STREAM, 128), 0)
    for m in range(MICRO):
        key_label = jnp.zeros((8, STREAM), jnp.int32)
        query_label = jnp.zeros((STREAM, 128), jnp.int32)
        for end in ends[m]:
            key_label += (row_of_key >= end).astype(jnp.int32)
            query_label += (row_of_query >= end).astype(jnp.int32)
        code[:, pl.ds(m * STREAM, STREAM)] = key_label + m * 64
        same = query_label[:, :1] == key_label[:1, :]
        bias[pl.ds(m * STREAM, STREAM), :] = jnp.where(same, 0.0, MASKED).astype(BF)

    seen = (label == code[pl.ds(0, 1), :]).astype(F32)
    seen2 = jnp.concatenate([seen, seen], 0) > 0.5
    for count in RATE[5]:
        run(x_parts, 1)
        run(weights, count)
    run_to(weights, 1)

    vecs[...] = wa[:, pl.ds(1152, 128)].astype(F32).T[:16, :]
    low_at, out_at = iota((FF_OWN, 384), 0), iota((FF_OWN, 384), 1)
    spread = jnp.zeros((FF_OWN, 384), jnp.bool_)
    row8, lane8 = iota((8, 384), 0), iota((8, 384), 1)
    pick = jnp.zeros((8, 384), jnp.bool_)
    for a in range(4):
        pick |= (lane8 >= 96 * a + 24 * row8) & (lane8 < 96 * a + 24 * row8 + 24) & (row8 < 4)
        for j in range(4):
            spread |= (low_at >= 24 * a) & (low_at < 24 * a + 24) & (out_at - low_at == 72 * a + 24 * j)
    spread = spread.astype(BF)
    for t in range(8):
        found_b1 = dot_tn(wa[pl.ds(FF_OWN * t, FF_OWN), pl.ds(1152, 128)], spread)
        b1[:, pl.ds(384 * t, 384)] = jnp.sum(jnp.where(pick, found_b1[8:16], 0.0), 0, keepdims=True)

    def vec(i):
        return vecs[pl.ds(i, 1), :]

    def project_q(i):
        rows = tile(i, 512, 512)
        xb = x_ref[rows, :]
        q_s[rows, :] = ((dot(xb, wa[:, pl.ds(0, WIDTH)]) + vec(0)).astype(BF).astype(F32) * 0.125).astype(BF)

    def project_k(i):
        rows = tile(i, 512, 512)
        k_s[rows, :] = dot(x_ref[rows, :], wa[:, pl.ds(HALF, WIDTH)]).astype(BF)

    def project_v(i):
        rows = tile(i, 512, 512)
        xb = x_ref[rows, :]
        v_s[rows, pl.ds(0, cut)] = (dot(xb, wa[:, pl.ds(WIDTH, cut)]) + vecs[pl.ds(1, 1), pl.ds(0, cut)]).astype(BF)
        v_s[rows, pl.ds(cut, cut)] = (
            dot(xb, wa[:, pl.ds(HALF + WIDTH, cut)]) + vecs[pl.ds(1, 1), pl.ds(cut, cut)]
        ).astype(BF)

    run(weights, 1)
    weave([functools.partial(loop, 1, shifted(f, i)) for f in (project_q, project_k, project_v) for i in range(2)], (weights, RATE[3]), (x_parts, 0.5))

    q_rows[...] = dot(sel[...], q_s[...])

    def own_shares(pair):
        q2 = both(q_rows[:, pl.ds(128 * pair, 128)])
        scores = jnp.where(seen2, dot_nt(q2, k_s[:, pl.ds(128 * pair, 128)]), MASKED)
        powers = jnp.where(seen2, jnp.exp(scores - jnp.max(scores, -1, keepdims=True)), 0.0)
        total = jnp.sum(powers, -1, keepdims=True)
        return q2, powers * (1.0 / jnp.where(total > 0, total, 1.0))

    def own_attend(pair):
        cols = pl.ds(128 * pair, 128)
        unused, shares = own_shares(pair)
        out = dot(shares.astype(BF), v_s[:, cols])
        att_rows[:, cols] = jnp.where(low_lanes, out[:BLOCK], out[BLOCK:])

    weave([functools.partial(own_attend, pair) for pair in range(6)], (weights, RATE[4]), (x_parts, 0.5))
    run(x_parts)

    att_block[...] = for_chip(jnp.where(ours, att_rows[...], 0.0))
    cls_parts = cls_steps(place, sender, SLOTS + 21, att_block, att_merged, att_stage, cls_att)
    run(cls_parts, 1)

    def attend(pair, m):
        cols = pl.ds(128 * pair, 128)
        keys = pl.ds(m * STREAM, STREAM)
        k2, v2 = k_s[keys, cols], v_s[keys, cols].astype(F32)
        low_keys = iota((STREAM, 128), 1) < 64
        values = jnp.concatenate([jnp.where(low_keys, v2, 1.0), jnp.where(low_keys, 1.0, v2)], 1).astype(BF)
        low = iota((256, 128), 1) < 64
        for i in range(2):
            rows = pl.ds(m * STREAM + 256 * i, 256)
            q2 = q_s[rows, cols].astype(F32)
            heads = jnp.concatenate([jnp.where(low, q2, 0.0), jnp.where(low, 0.0, q2)], 0).astype(BF)
            scores = dot_nt(heads, k2)
            masked = bias[rows, :].astype(F32)
            powers = []
            for head in range(2):
                part_scores = scores[256 * head : 256 * head + 256] + masked
                powers.append(jnp.exp(part_scores - jnp.max(part_scores, -1, keepdims=True)).astype(BF))
            out = dot(jnp.concatenate(powers, 0), values)
            first, second = out[:256, :128], out[256:, 128:]
            sums_of = pltpu.roll(jnp.where(low, second, first), 64, 1)
            igrad_ref[rows, cols] = (jnp.where(low, first, second) * (1.0 / sums_of)).astype(BF)

    weave(
        [functools.partial(attend, pair, m) for pair in range(6) for m in range(MICRO)], (cls_parts, 1), (weights, RATE[0])
    )
    run(cls_parts)

    def cls_first(i):
        rows = tile(i, CLS, CLS)
        at = iota((CLS, 1), 0) + i * CLS
        group = jnp.zeros((CLS, 1), jnp.int32)
        for b in range(1, 16):
            group += (at >= BLOCK * b).astype(jnp.int32)
        xin = jnp.where(at - BLOCK * group < BLOCK - MICRO, cls[rows, :].astype(F32), 0.0)
        normed, inverse = centre(xin + (dot(cls_att[rows, :], wa[:, pl.ds(2560, WIDTH)]) + vec(2)))
        n1[rows, :] = normed
        columns[rows, pl.ds(0, 1)] = inverse
        h_low[rows, :] = (normed * vec(3) + vec(4)).astype(BF)

    run_to(weights, 2)
    loop(1, cls_first)
    run(weights, 1)

    at = iota((CLS, 1), 0)
    at_col = iota((1, CLS), 1)

    def kinds(index):
        group = jnp.zeros(index.shape, jnp.int32)
        for b in range(1, 16):
            group += (index >= BLOCK * b).astype(jnp.int32)
        inner = index - BLOCK * group
        query_m = (inner >= QS).astype(jnp.int32)
        is_q = inner < MICRO * QS
        passage_m = (inner >= MICRO * QS + PS).astype(jnp.int32)
        is_p = (inner >= MICRO * QS) & (inner < MICRO * (QS + PS))
        return group, inner, is_q, query_m, is_p, passage_m

    group, inner, is_q, query_m, unused, unused = kinds(at)
    source = (group * BLOCK + (BLOCK - MICRO) + query_m == at_col).astype(BF)
    codes = dot(source, cls[:, pl.ds(0, 128)])
    wanted = jnp.sum(jnp.where(iota((CLS, 128), 1) == inner - QS * query_m, codes, 0.0), 1, keepdims=True)
    wanted = wanted.astype(jnp.int32)
    target = 2 * wanted - (wanted & 1) + PS * query_m
    columns[:, pl.ds(2, 1)] = target.astype(F32)
    cls_sender.close()
    y_low = cls
    hid_blk = y_low.at[pl.ds(0, STREAM), :]

    def cls_inner(i):
        rows = pl.ds(0, CLS)
        cols = tile(i, 512, 512)
        wcols = pl.ds(pl.multiple_of(3328 + i * 512, 128), 512)
        u = dot(h_low[rows, :], wa[:, wcols]) + b1[:, cols]
        phi = 0.5 * (1.0 + lax.erf(u * 0.7071067811865476))
        act[rows, cols] = (u * phi).astype(BF)
        slope[rows, cols] = (phi + u * jnp.exp(-0.5 * u * u) * 0.3989422804014327).astype(BF)

    weave([functools.partial(loop, 1, shifted(cls_inner, i)) for i in range(3)], (weights, RATE[1]))
    run_to(weights, 4)
    weave([functools.partial(loop, 1, shifted(cls_inner, i)) for i in range(3, 6)], (weights, RATE[1]))
    run_to(weights, 6)

    def cls_second(i):
        rows = tile(i, CLS, CLS)
        r = h_low[rows, :].astype(F32) + (dot(act[rows, :], wb[...]) + vec(5))
        normed, inverse = centre(r)
        n2[rows, :] = normed
        columns[rows, pl.ds(1, 1)] = inverse
        y_low[rows, :] = (normed * vec(6) + vec(7)).astype(BF)

    loop(1, cls_second)

    unused, unused, is_q, query_m, unused, unused = kinds(iota((CLS, 1), 0))
    lane = iota((1, 128), 1)
    paired = is_q & (lane < 16 * MICRO * PS) & (((lane >> 1) & 1) == query_m)
    hit = paired & (columns[:, pl.ds(2, 1)] == lane.astype(F32))
    passage = iota((128, CLS), 0)
    chosen = BLOCK * (passage >> 2) + MICRO * QS + (passage & 3) == iota((128, CLS), 1)
    chosen = (chosen & (passage < 16 * MICRO * PS)).astype(BF)
    y_all = y_low[...]
    y_passages = dot(chosen, y_all).astype(BF)
    logits = jnp.where(paired, dot_nt(y_all, y_passages) * WIDTH ** -0.5, MASKED)
    powers = jnp.where(paired, jnp.exp(logits - jnp.max(logits, -1, keepdims=True)), 0.0)
    total = jnp.sum(powers, -1, keepdims=True)
    shares = powers * (1.0 / jnp.where(is_q, total, 1.0))
    d_logits = ((shares - hit.astype(F32)) * (1.0 / MICRO)).astype(BF)
    d_passages = dot_tn(d_logits, y_all)
    d_high = d_passages.astype(BF)
    d_rest = (d_passages - d_high.astype(F32)).astype(BF)
    d_y = (dot(d_logits, y_passages) + dot_tn(chosen, d_high) + dot_tn(chosen, d_rest)) * WIDTH ** -0.5
    normed = n2[...]
    sums[pl.ds(0, 1), :] = jnp.sum(d_y * normed, 0, keepdims=True)
    sums[pl.ds(1, 1), :] = jnp.sum(d_y, 0, keepdims=True)
    d_sum = centre_back(d_y * vec(6), normed, columns[:, pl.ds(1, 1)])
    n2[...] = d_sum
    d_out[...] = d_sum.astype(BF)
    sums[pl.ds(2, 1), :] = jnp.sum(d_out[...].astype(F32), 0, keepdims=True)

    def cls_inner_back(i):
        cols = tile(i, 512, 512)
        d_act = dot_nt(d_out[...], wb[cols, :])
        d_u = (d_act * slope[:, cols].astype(F32)).astype(BF)
        slope[:, cols] = d_u
        sums_b1[:, cols] = jnp.sum(d_u.astype(F32), 0, keepdims=True)

    loop(6, cls_inner_back)

    def cls_first_back(i):
        rows = tile(i, CLS, CLS)
        d_hidden = n2[rows, :] + dot_nt(slope[rows, :], wa[:, pl.ds(3328, FF)])
        normed = n1[rows, :]
        gains = jnp.sum(d_hidden * normed, 0, keepdims=True)
        shifts = jnp.sum(d_hidden, 0, keepdims=True)
        d_sum = centre_back(d_hidden * vec(3), normed, columns[rows, pl.ds(0, 1)])
        n2[rows, :] = d_sum
        d_low = d_sum.astype(BF)
        d_branch[rows, :] = d_low
        totals = (gains, shifts, jnp.sum(d_low.astype(F32), 0, keepdims=True))
        for place_in, value in enumerate(totals):
            line = pl.ds(3 + place_in, 1)
            sums[line, :] = jnp.where(i == 0, value, sums[line, :] + value)

    loop(1, cls_first_back)

    own_sum = jnp.where(ours, n2[tile(place.batch, BLOCK, BLOCK), :], 0.0)
    d_att = dot_nt(own_sum.astype(BF), wa[:, pl.ds(2560, WIDTH)]).astype(BF).astype(F32)
    def own_back(pair):
        cols = pl.ds(128 * pair, 128)
        d_a2 = both(d_att[:, 128 * pair : 128 * pair + 128])
        k2, v2 = k_s[:, cols], v_s[:, cols]
        q2, shares = own_shares(pair)
        d_shares = dot_nt(d_a2, v2)
        d_scores = (shares * (d_shares - jnp.sum(d_shares * shares, -1, keepdims=True))).astype(BF)
        d_q2 = dot(d_scores, k2)
        dq[:, cols] = (jnp.where(low_lanes, d_q2[:BLOCK], d_q2[BLOCK:]) * 0.125).astype(BF)
        dkv[:, cols] = dot_tn(d_scores, q2).astype(BF)
        dkv[:, pl.ds(WIDTH + 128 * pair, 128)] = dot_tn(shares.astype(BF), d_a2).astype(BF)

    for pair in range(6):
        own_back(pair)

    part[:, pl.ds(0, WIDTH)] = dot_tn(x_rows[...].astype(BF), dq[...]).astype(BF)

    def project_back(i):
        out = dot_tn(x_ref[:, tile(i, 256, 256)], dkv[...])
        part[tile(i, 256, 256), pl.ds(WIDTH, 2 * WIDTH)] = out.astype(BF)

    line = iota((128, WIDTH), 0)
    q_line = jnp.sum(dq[...].astype(F32), 0, keepdims=True)
    v_line = jnp.sum(dkv[:, pl.ds(WIDTH, WIDTH)].astype(F32), 0, keepdims=True)
    lines = jnp.where(line == 0, q_line, jnp.where(line == 1, v_line, 0.0))
    part[:, pl.ds(3 * WIDTH, 128)] = lines.T.astype(BF)
    part[:, pl.ds(3 * WIDTH + 128, 128)] = jnp.zeros((WIDTH, 128), BF)
    for i, (first, last) in enumerate(((0, 5), (5, 10), (10, 16))):
        loop(1, shifted(project_back, i))
        sum_begin(place, sender, SLOTS + 39, part, stage_core, first, last)

    steps = sum_steps(place, sender, SLOTS + 39, part, work, stage_core, stage_pair, stage_z, final, stage_last, summed)
    run(steps, 2)

    def rows_first(i):
        rows = pl.ds(STREAM * i, STREAM)
        branch = dot(igrad_ref[rows, :], wa[:, pl.ds(2560, WIDTH)]) + vec(2)
        normed, unused = centre(x_ref[rows, :].astype(F32) + branch)
        low = (normed * vec(3) + vec(4)).astype(BF)
        hid_blk[...] = low
        scr[...] = low.astype(F32) + vec(5)

    def rows_inner(j):
        cols = tile(j, 512, 512)
        u = dot(hid_blk[...], wa[:, pl.ds(pl.multiple_of(3328 + j * 512, 128), 512)]) + b1[:, cols]
        active = (u * (0.5 * (1.0 + lax.erf(u * 0.7071067811865476)))).astype(BF)
        scr[...] += dot(active, wb[cols, :])

    def rows_second(i):
        normed, unused = centre(scr[...])
        valid = iota((STREAM, 1), 0) < ends[i][QS - 1]
        hidden_ref[pl.ds(STREAM * i, STREAM), :] = jnp.where(valid, normed * vec(6) + vec(7), 0.0).astype(BF)

    units = []
    for i in range(MICRO):
        units.append(functools.partial(rows_first, i))
        units += [functools.partial(loop, 1, shifted(rows_inner, j)) for j in range(6)]
        units.append(functools.partial(rows_second, i))
    weave(units, (steps, RATE[2]))

    back_rows = dot_nt(dq[...], wa[:, pl.ds(0, WIDTH)]) + own_sum
    q_s[:, pl.ds(0, 128)] = jnp.concatenate([sel[...].astype(F32), jnp.zeros((128 - BLOCK, ROWS), F32)], 0).T.astype(BF)
    back_low = jnp.concatenate([back_rows, jnp.zeros((128 - BLOCK, WIDTH), F32)], 0)
    back_rest = (back_low - back_low.astype(BF).astype(F32)).astype(BF)
    back_low = back_low.astype(BF)

    def input_back(i):
        rows = tile(i, 256, 256)
        total = dot_nt(dkv[rows, pl.ds(0, WIDTH)], wa[:, pl.ds(HALF, WIDTH)])
        total += dot_nt(dkv[rows, pl.ds(WIDTH, cut)], wa[:, pl.ds(WIDTH, cut)])
        total += dot_nt(dkv[rows, pl.ds(WIDTH + cut, cut)], wa[:, pl.ds(HALF + WIDTH, cut)])
        hit_rows = q_s[rows, pl.ds(0, 128)]
        total += dot(hit_rows, back_low) + dot(hit_rows, back_rest)
        igrad_ref[rows, :] = total.astype(BF)

    weave([functools.partial(loop, 2, shifted(input_back, i)) for i in (0, 2)], (steps, 1))

    tall_first = jnp.minimum(place.index * FF_OWN // 128, (FF - 256) // 128) * 128
    tall_at = place.index * FF_OWN - tall_first
    own_first = jnp.minimum(place.index * OWN // 128, (WIDTH - 256) // 128) * 128
    own_at = place.index * OWN - own_first

    window[...] = dot_tn(act[:, pl.ds(pl.multiple_of(tall_first, 128), 256)], d_out[...])
    tw_ref[...] = window[pl.ds(pl.multiple_of(tall_at, 8), FF_OWN), :]
    own_cols = pl.ds(pl.multiple_of(own_first, 128), 256)
    own_lines = pl.ds(pl.multiple_of(own_at, 8), OWN)
    window[...] = dot_tn(cls_att[:, own_cols], d_branch[...])
    ow_ref[...] = window[own_lines, :]
    for j in range(4):
        window[...] = dot_tn(h_low[:, own_cols], slope[:, pl.ds(WIDTH * j, WIDTH)])
        iw_ref[:, pl.ds(WIDTH * j, WIDTH)] = window[own_lines, :]

    def own_lanes(line, first, shift, size):
        window = jnp.broadcast_to(line[:, pl.ds(pl.multiple_of(first, 128), 256)], (8, 256))
        return pltpu.roll(window, 256 - shift, 1)[:1, :size]

    for ref, i in ((g2_ref, 0), (s2_ref, 1), (tb_ref, 2), (g1_ref, 3), (s1_ref, 4), (ob_ref, 5)):
        ref[...] = own_lanes(sums.at[pl.ds(i, 1), :], own_first, own_at, OWN)
    ib_ref[...] = own_lanes(sums_b1, tall_first, tall_at, FF_OWN)

    run(steps)
    qw_ref[...] = summed[:, pl.ds(0, WIDTH)]
    kw_ref[...] = summed[:, pl.ds(WIDTH, WIDTH)]
    vw_ref[...] = summed[:, pl.ds(2 * WIDTH, WIDTH)]
    lines = jnp.concatenate([summed[:, pl.ds(3 * WIDTH, 128)], jnp.zeros((128 - OWN, 128), F32)], 0).T
    qb_ref[...] = lines[0:1, :OWN]
    vb_ref[...] = lines[1:2, :OWN]
    sender.close()


def copy_kernel(count, *refs):
    ins, outs, held, sems = refs[:count], refs[count : 2 * count], refs[2 * count : 3 * count], refs[-1]
    first = [pltpu.make_async_copy(ins[i], held[i], sems.at[0, i]) for i in range(count)]
    second = [pltpu.make_async_copy(held[i], outs[i], sems.at[1, i]) for i in range(count)]
    for copy in first:
        copy.start()
    for i in range(count):
        first[i].wait()
        second[i].start()
    for copy in second:
        copy.wait()


def fast(hidden_in, query_lengths, passage_lengths, positives, stored):
    (query_weight, query_bias, key_weight, value_weight, value_bias, output_weight, output_bias, first_gain,
     first_shift, inner_weight, inner_bias, outer_weight, outer_bias, second_gain, second_shift) = stored
    shapes = [
        ((ROWS, WIDTH), BF), ((ROWS, WIDTH), BF), ((OWN, WIDTH), F32), ((1, OWN), F32), ((OWN, WIDTH), F32),
        ((OWN, WIDTH), F32), ((1, OWN), F32), ((OWN, WIDTH), F32), ((1, OWN), F32), ((1, OWN), F32), ((1, OWN), F32),
        ((OWN, FF), F32), ((1, FF_OWN), F32), ((FF_OWN, WIDTH), F32), ((1, OWN), F32), ((1, OWN), F32), ((1, OWN), F32),
    ]
    scratch = [
        pltpu.VMEM((128, 128), F32), pltpu.VMEM((32, 6400), BF), pltpu.VMEM((32, 3200), BF), pltpu.VMEM((WIDTH, 6400), BF), pltpu.VMEM((FF, WIDTH), BF),
        pltpu.VMEM((16, WIDTH), F32), pltpu.VMEM((1, FF), F32),
        pltpu.VMEM((ROWS, WIDTH), BF), pltpu.VMEM((ROWS, WIDTH), BF), pltpu.VMEM((ROWS, WIDTH), BF),
        pltpu.VMEM((ROWS, STREAM), BF), pltpu.VMEM((BLOCK, ROWS), BF), pltpu.VMEM((8, ROWS), jnp.int32),
        pltpu.VMEM((2 * BLOCK, WIDTH), BF), pltpu.VMEM((2 * BLOCK, WIDTH // 2), BF),
        pltpu.VMEM((2, 2 * BLOCK, WIDTH // 2), BF), pltpu.VMEM((CLS, WIDTH), BF),
        pltpu.VMEM((2 * BLOCK, WIDTH), BF), pltpu.VMEM((2 * BLOCK, WIDTH // 2), BF),
        pltpu.VMEM((2, 2 * BLOCK, WIDTH // 2), BF), pltpu.VMEM((CLS, WIDTH), BF),
        pltpu.VMEM((CLS, WIDTH), F32), pltpu.VMEM((CLS, 128), F32), pltpu.VMEM((CLS, WIDTH), BF),
        pltpu.VMEM((CLS, FF), BF), pltpu.VMEM((CLS, FF), BF),
        pltpu.VMEM((CLS, WIDTH), F32), pltpu.VMEM((CLS, WIDTH), BF), pltpu.VMEM((CLS, WIDTH), BF),
        pltpu.VMEM((8, WIDTH), F32), pltpu.VMEM((1, FF), F32),
        pltpu.VMEM((BLOCK, WIDTH), F32), pltpu.VMEM((BLOCK, WIDTH), F32), pltpu.VMEM((BLOCK, WIDTH), F32),
        pltpu.VMEM((BLOCK, WIDTH), BF), pltpu.VMEM((ROWS, 2 * WIDTH), BF),
        pltpu.VMEM((WIDTH, 2 * HALF), BF),
        pltpu.VMEM((16, 2 * OWN, HALF), BF), pltpu.VMEM((16, 2 * OWN, HALF), BF), pltpu.VMEM((16, 2 * OWN, HALF), BF),
        pltpu.VMEM((4, 2 * OWN, HALF), BF), pltpu.VMEM((OWN, HALF), F32), pltpu.VMEM((OWN, HALF), F32),
        pltpu.VMEM((OWN, 2 * HALF), F32),
        pltpu.SemaphoreType.DMA((380,)), pltpu.SemaphoreType.DMA((20,)), pltpu.SemaphoreType.DMA((SLOTS + 92,)),
    ]
    vmem = pl.BlockSpec(memory_space=pltpu.VMEM)
    smem = pl.BlockSpec(memory_space=pltpu.SMEM)
    outs = pl.pallas_call(
        layer_kernel,
        out_shape=[jax.ShapeDtypeStruct(shape, kind) for shape, kind in shapes],
        in_specs=[vmem] * 16 + [smem] * 3,
        out_specs=[vmem] * len(shapes),
        scratch_shapes=scratch,
        compiler_params=pltpu.CompilerParams(collective_id=0, has_side_effects=True, vmem_limit_bytes=63 * 2**20),
    )(
        hidden_in.reshape(ROWS, WIDTH), query_bias, value_bias, output_bias, first_gain, first_shift, outer_bias,
        second_gain, second_shift, inner_bias, query_weight, key_weight, value_weight, output_weight, inner_weight,
        outer_weight, query_lengths, passage_lengths, positives,
    )
    outs = pl.pallas_call(
        functools.partial(copy_kernel, len(shapes)),
        out_shape=[jax.ShapeDtypeStruct(shape, kind) for shape, kind in shapes],
        in_specs=[pl.BlockSpec(memory_space=pl.ANY)] * len(shapes),
        out_specs=[pl.BlockSpec(memory_space=pl.ANY)] * len(shapes),
        scratch_shapes=[pltpu.VMEM(shape, kind) for shape, kind in shapes] + [pltpu.SemaphoreType.DMA((2, len(shapes)))],
    )(*outs)
    shape = hidden_in.shape
    return tuple(
        out.reshape(shape) if i < 2 else (out.reshape(-1) if out.shape[0] == 1 else out) for i, out in enumerate(outs)
    )


def local(
    hidden_in,
    query_lengths,
    passage_lengths,
    positives,
    query_weight,
    query_bias,
    key_weight,
    value_weight,
    value_bias,
    output_weight,
    output_bias,
    first_gain,
    first_shift,
    inner_weight,
    inner_bias,
    outer_weight,
    outer_bias,
    second_gain,
    second_shift,
):
    stored = (
        query_weight,
        query_bias,
        key_weight,
        value_weight,
        value_bias,
        output_weight,
        output_bias,
        first_gain,
        first_shift,
        inner_weight,
        inner_bias,
        outer_weight,
        outer_bias,
        second_gain,
        second_shift,
    )
    sizes = (lax.axis_size("tower"), lax.axis_size("batch"), hidden_in.shape, inner_weight.shape)
    if sizes == (2, 16, (MICRO, 1, STREAM, WIDTH), (OWN, FF)) and query_lengths.shape[1] == QS:
        return fast(hidden_in, query_lengths, passage_lengths, positives, stored)
    micro = hidden_in.shape[0]
    width = hidden_in.shape[3]
    cls_scale = width ** (-0.5)
    side = lax.axis_index("tower")
    is_query = side == 0
    slot_count = query_lengths.shape[1]
    passage_count = passage_lengths.shape[1]
    half_count = (slot_count + 1) // 2
    extra_rows = 2 * half_count - slot_count
    owners = lax.axis_size(("tower", "batch"))
    totals = tuple(
        (jnp.zeros((item.shape[0] * owners,) + item.shape[1:], jnp.float32) for item in stored)
    )
    half_totals = tuple(
        (jnp.zeros((item.shape[0] * owners // 2,) + item.shape[1:], jnp.float32) for item in stored)
    )
    shown_list = []
    grad_list = []
    for micro_step in range(micro):
        gathered = (
            lax.all_gather(query_weight, ("tower", "batch"), axis=0, tiled=True),
            lax.all_gather(query_bias, ("tower", "batch"), axis=0, tiled=True),
            lax.all_gather(key_weight, ("tower", "batch"), axis=0, tiled=True),
            lax.all_gather(value_weight, ("tower", "batch"), axis=0, tiled=True),
            lax.all_gather(value_bias, ("tower", "batch"), axis=0, tiled=True),
            lax.all_gather(output_weight, ("tower", "batch"), axis=0, tiled=True),
            lax.all_gather(output_bias, ("tower", "batch"), axis=0, tiled=True),
            lax.all_gather(first_gain, ("tower", "batch"), axis=0, tiled=True),
            lax.all_gather(first_shift, ("tower", "batch"), axis=0, tiled=True),
            lax.all_gather(inner_weight, ("tower", "batch"), axis=0, tiled=True),
            lax.all_gather(inner_bias, ("tower", "batch"), axis=0, tiled=True),
            lax.all_gather(outer_weight, ("tower", "batch"), axis=0, tiled=True),
            lax.all_gather(outer_bias, ("tower", "batch"), axis=0, tiled=True),
            lax.all_gather(second_gain, ("tower", "batch"), axis=0, tiled=True),
            lax.all_gather(second_shift, ("tower", "batch"), axis=0, tiled=True),
        )
        params = cast_params(gathered)
        inputs = hidden_in[micro_step, 0]
        passage_part = jnp.pad(passage_lengths[micro_step], (0, slot_count - passage_count))
        lengths = jnp.where(is_query, query_lengths[micro_step], passage_part)
        labels, valid, starts, live = segments(lengths, inputs.shape[0])
        saved, shown = forward(inputs, labels, valid, params)
        shown_list.append(shown)
        mine = jnp.where(live[:, None], shown[starts], 0.0)
        partner = partner_2(mine, "tower", 0)
        query_cls = jnp.where(is_query, mine, partner)
        passage_cls = jnp.where(is_query, partner, mine)[:passage_count]
        pooled = lax.all_gather(passage_cls, "batch", axis=0, tiled=True)
        padded_queries = jnp.pad(query_cls, ((0, extra_rows), (0, 0)))
        padded_targets = jnp.pad(positives[micro_step], (0, extra_rows))
        my_queries = lax.dynamic_slice_in_dim(padded_queries, side * half_count, half_count, 0)
        my_targets = lax.dynamic_slice_in_dim(padded_targets, side * half_count, half_count, 0)
        logits = product_nt(my_queries, pooled) * cls_scale
        highest = jnp.max(logits, -1, keepdims=True)
        powers = jnp.exp(logits - highest)
        shares = powers / jnp.sum(powers, -1, keepdims=True)
        columns = jnp.arange(pooled.shape[0], dtype=jnp.int32)
        target = (columns[None, :] == my_targets[:, None]).astype(jnp.float32)
        grad_logits = ((shares - target) / micro).astype(jnp.bfloat16)
        own_grad = product(grad_logits, pooled) * cls_scale
        pooled_grad = product_tn(grad_logits, my_queries) * cls_scale
        summed = lax.psum_scatter(pooled_grad, "batch", scatter_dimension=0, tiled=True)
        other_queries, other_passages = (
            partner_2(own_grad.astype(jnp.bfloat16), "tower", 0).astype(own_grad.dtype),
            partner_2(summed.astype(jnp.bfloat16), "tower", 0).astype(summed.dtype),
        )
        query_grad = jnp.concatenate([own_grad, other_queries], 0)[:slot_count]
        passage_grad = jnp.pad(summed + other_passages, ((0, slot_count - passage_count), (0, 0)))
        cotangent = jnp.where(is_query, query_grad, passage_grad)
        input_part, step_grads = backward(inputs, labels, cotangent, starts, live, saved, params)
        grad_list.append(input_part)
        totals = tuple((first + second for first, second in zip(totals, step_grads)))
    keep_all, give_all = split_halves(totals, side)
    came_all = jax.tree.map(
        lambda part, own: part.astype(own.dtype), partner_2(as_sent(give_all), "tower", 0), give_all
    )
    half_totals = tuple((first + second for first, second in zip(keep_all, came_all)))
    shards = lax.psum_scatter(half_totals, "batch", scatter_dimension=0, tiled=True)
    hidden_out = jnp.stack(shown_list)[:, None]
    input_grad = jnp.stack(grad_list)[:, None]
    return (
        hidden_out,
        input_grad,
        shards[0],
        shards[1],
        shards[2],
        shards[3],
        shards[4],
        shards[5],
        shards[6],
        shards[7],
        shards[8],
        shards[9],
        shards[10],
        shards[11],
        shards[12],
        shards[13],
        shards[14],
    )


def solution(mesh):
    placed = (
        P(None, "tower", "batch", None),
        P(None, "batch"),
        P(None, "batch"),
        P(None, "batch"),
        P(("tower", "batch"), None),
        P(("tower", "batch")),
        P(("tower", "batch"), None),
        P(("tower", "batch"), None),
        P(("tower", "batch")),
        P(("tower", "batch"), None),
        P(("tower", "batch")),
        P(("tower", "batch")),
        P(("tower", "batch")),
        P(("tower", "batch"), None),
        P(("tower", "batch")),
        P(("tower", "batch"), None),
        P(("tower", "batch")),
        P(("tower", "batch")),
        P(("tower", "batch")),
    )
    return jax.shard_map(
        local,
        mesh=mesh,
        in_specs=placed,
        out_specs=(
            P(None, "tower", "batch", None),
            P(None, "tower", "batch", None),
            P(("tower", "batch"), None),
            P(("tower", "batch")),
            P(("tower", "batch"), None),
            P(("tower", "batch"), None),
            P(("tower", "batch")),
            P(("tower", "batch"), None),
            P(("tower", "batch")),
            P(("tower", "batch")),
            P(("tower", "batch")),
            P(("tower", "batch"), None),
            P(("tower", "batch")),
            P(("tower", "batch"), None),
            P(("tower", "batch")),
            P(("tower", "batch")),
            P(("tower", "batch")),
        ),
        check_vma=False,
    )
```

```python
import functools

import jax
import jax.numpy as jnp
from jax import lax
from jax.experimental import pallas as pl
from jax.experimental.pallas import tpu as pltpu
from jax.sharding import PartitionSpec as P

HEADS = 12


EPSILON = 1e-12
MASKED = -1e30


def partner_2(x, axis, apart):
    return lax.ppermute(x, axis, [(i, i ^ 1 << apart) for i in range(lax.axis_size(axis))])


def as_sent(x):
    return jax.tree.map(lambda a: a.astype(jnp.bfloat16) if a.dtype == jnp.float32 else a, x)


def product(left, right):
    return jnp.dot(left, right, preferred_element_type=jnp.float32)


def product_tn(left, right):
    return jnp.einsum("ta,tb->ab", left, right, preferred_element_type=jnp.float32)


def product_nt(left, right):
    return jnp.einsum("ra,ba->rb", left, right, preferred_element_type=jnp.float32)


def normalize(values, gains, shifts):
    average = jnp.mean(values, -1, keepdims=True)
    centred = values - average
    inverse = lax.rsqrt(jnp.mean(centred * centred, -1, keepdims=True) + EPSILON)
    normed = centred * inverse
    return (normed * gains + shifts, normed, inverse)


def normalize_back(upstream, normed, inverse, gains):
    scaled = upstream * gains
    inner = (
        scaled
        - jnp.mean(scaled, -1, keepdims=True)
        - normed * jnp.mean(scaled * normed, -1, keepdims=True)
    )
    return (inner * inverse, jnp.sum(upstream * normed, 0), jnp.sum(upstream, 0))


def gelu_slope(values):
    return (
        0.5 * (1.0 + lax.erf(values * 0.7071067811865476))
        + values * jnp.exp(-0.5 * values * values) * 0.3989422804014327
    )


def segments(lengths, token_rows):
    ends = jnp.cumsum(lengths)
    places = jnp.arange(token_rows, dtype=jnp.int32)
    labels = jnp.sum((places[:, None] >= ends[None, :]).astype(jnp.int32), 1)
    starts = jnp.minimum(ends - lengths, token_rows - 1)
    return (labels, places < ends[-1], starts, lengths > 0)


def tail(inputs, attended, params):
    out_mat, out_vec, gain_one, shift_one = (params[5], params[6], params[7], params[8])
    inner_mat, inner_vec, outer_mat, outer_vec, gain_two, shift_two = params[9:15]
    branch = product(attended, out_mat) + out_vec
    hidden_full, normed_one, inverse_one = normalize(
        inputs.astype(jnp.float32) + branch, gain_one, shift_one
    )
    hidden_low = hidden_full.astype(jnp.bfloat16)
    inner = product(hidden_low, inner_mat) + inner_vec
    active = jax.nn.gelu(inner, approximate=False).astype(jnp.bfloat16)
    outer = product(active, outer_mat) + outer_vec
    result, normed_two, inverse_two = normalize(
        hidden_low.astype(jnp.float32) + outer, gain_two, shift_two
    )
    return (result, (normed_one, inverse_one, hidden_low, inner, active, normed_two, inverse_two))


def forward(inputs, labels, valid, params):
    query_mat, query_vec, key_mat, value_mat, value_vec = params[0:5]
    token_rows, width = inputs.shape
    head_size = width // HEADS
    scale = head_size ** (-0.5)
    queries = (product(inputs, query_mat) + query_vec).astype(jnp.bfloat16)
    keys = product(inputs, key_mat).astype(jnp.bfloat16)
    values = (product(inputs, value_mat) + value_vec).astype(jnp.bfloat16)
    block_rows = min(512, token_rows)

    def one_block(first_row):
        allowed = labels[:, None] == labels[None, :]

        def one_head(head_index):
            head_queries = lax.dynamic_slice_in_dim(queries, head_index * head_size, head_size, 1)
            head_keys = lax.dynamic_slice_in_dim(keys, head_index * head_size, head_size, 1)
            head_values = lax.dynamic_slice_in_dim(values, head_index * head_size, head_size, 1)
            scores = jnp.where(allowed, product_nt(head_queries, head_keys) * scale, MASKED)
            highest = jnp.max(scores, -1, keepdims=True)
            powers = jnp.exp(scores - highest)
            totals = jnp.sum(powers, -1, keepdims=True)
            shares = (powers / totals).astype(jnp.bfloat16)
            return (product(shares, head_values), (highest + jnp.log(totals))[:, 0])

        head_out, head_lse = lax.map(one_head, jnp.arange(HEADS, dtype=jnp.int32))
        attended = (
            jnp.transpose(head_out, (1, 0, 2)).reshape(block_rows, width).astype(jnp.bfloat16)
        )
        result, unused = tail(inputs, attended, params)
        shown = jnp.where(valid[:, None], result, 0.0).astype(jnp.bfloat16)
        return (attended, head_lse, shown)

    firsts = jnp.arange(token_rows // block_rows, dtype=jnp.int32) * block_rows
    attended, lse_blocks, shown = lax.map(one_block, firsts)
    attended = attended.reshape(token_rows, width)
    shown = shown.reshape(token_rows, width)
    lse_all = jnp.transpose(lse_blocks, (1, 0, 2)).reshape(HEADS, token_rows)
    return ((queries, keys, values, attended, lse_all), shown)


def backward(inputs, labels, cotangent, starts, live, saved, params):
    queries, keys, values, attended, lse_all = saved
    query_mat, key_mat, value_mat, out_mat = (params[0], params[2], params[3], params[5])
    gain_one, inner_mat, outer_mat, gain_two = (params[7], params[9], params[11], params[13])
    token_rows, width = inputs.shape
    head_size = width // HEADS
    scale = head_size ** (-0.5)
    slot_count = starts.shape[0]
    row_inputs = inputs[starts]
    row_attended = attended[starts]
    unused, kept = tail(row_inputs, row_attended, params)
    normed_one, inverse_one, hidden_low, inner, active, normed_two, inverse_two = kept
    upstream = jnp.where(live[:, None], cotangent, 0.0)
    grad_sum_two, grad_gain_two, grad_shift_two = normalize_back(
        upstream, normed_two, inverse_two, gain_two
    )
    grad_outer = grad_sum_two.astype(jnp.bfloat16)
    grad_outer_mat = product_tn(active, grad_outer)
    grad_outer_vec = jnp.sum(grad_outer.astype(jnp.float32), 0)
    grad_inner = (product_nt(grad_outer, outer_mat) * gelu_slope(inner)).astype(jnp.bfloat16)
    grad_inner_mat = product_tn(hidden_low, grad_inner)
    grad_inner_vec = jnp.sum(grad_inner.astype(jnp.float32), 0)
    grad_hidden = grad_sum_two + product_nt(grad_inner, inner_mat)
    grad_sum_one, grad_gain_one, grad_shift_one = normalize_back(
        grad_hidden, normed_one, inverse_one, gain_one
    )
    grad_branch = grad_sum_one.astype(jnp.bfloat16)
    grad_out_mat = product_tn(row_attended, grad_branch)
    grad_out_vec = jnp.sum(grad_branch.astype(jnp.float32), 0)
    grad_attended = (
        product_nt(grad_branch, out_mat).astype(jnp.bfloat16).reshape(slot_count, HEADS, head_size)
    )
    row_queries = queries[starts].reshape(slot_count, HEADS, head_size)
    keys_split = keys.reshape(token_rows, HEADS, head_size)
    values_split = values.reshape(token_rows, HEADS, head_size)
    allowed = labels[starts][None, :, None] == labels[None, None, :]
    scores = (
        jnp.einsum("rhd,thd->hrt", row_queries, keys_split, preferred_element_type=jnp.float32)
        * scale
    )
    shares = jnp.where(allowed, jnp.exp(scores - lse_all[:, starts][:, :, None]), 0.0)
    shares_low = shares.astype(jnp.bfloat16)
    grad_shares = jnp.einsum(
        "rhd,thd->hrt", grad_attended, values_split, preferred_element_type=jnp.float32
    )
    grad_scores = (
        shares * (grad_shares - jnp.sum(grad_shares * shares, -1, keepdims=True))
    ).astype(jnp.bfloat16)
    grad_queries = (
        jnp.einsum("hrt,thd->rhd", grad_scores, keys_split, preferred_element_type=jnp.float32)
        * scale
    )
    grad_queries = grad_queries.reshape(slot_count, width).astype(jnp.bfloat16)
    grad_keys = (
        jnp.einsum("hrt,rhd->thd", grad_scores, row_queries, preferred_element_type=jnp.float32)
        * scale
    )
    grad_keys = grad_keys.reshape(token_rows, width).astype(jnp.bfloat16)
    grad_values = jnp.einsum(
        "hrt,rhd->thd", shares_low, grad_attended, preferred_element_type=jnp.float32
    )
    grad_values = grad_values.reshape(token_rows, width).astype(jnp.bfloat16)
    grad_inputs = product_nt(grad_keys, key_mat) + product_nt(grad_values, value_mat)
    grad_inputs = grad_inputs.at[starts].add(product_nt(grad_queries, query_mat) + grad_sum_one)
    grads = (
        product_tn(row_inputs, grad_queries),
        jnp.sum(grad_queries.astype(jnp.float32), 0),
        product_tn(inputs, grad_keys),
        product_tn(inputs, grad_values),
        jnp.sum(grad_values.astype(jnp.float32), 0),
        grad_out_mat,
        grad_out_vec,
        grad_gain_one,
        grad_shift_one,
        grad_inner_mat,
        grad_inner_vec,
        grad_outer_mat,
        grad_outer_vec,
        grad_gain_two,
        grad_shift_two,
    )
    return (grad_inputs.astype(jnp.bfloat16), grads)


def cast_params(gathered):
    vector_places = (1, 4, 6, 7, 8, 10, 12, 13, 14)
    return tuple(
        (
            item.astype(jnp.float32) if place in vector_places else item
            for place, item in enumerate(gathered)
        )
    )


def split_halves(grads, side):
    keep_list = []
    give_list = []
    for item in grads:
        half = item.shape[0] // 2
        keep_list.append(lax.dynamic_slice_in_dim(item, side * half, half, 0))
        give_list.append(lax.dynamic_slice_in_dim(item, (1 - side) * half, half, 0))
    return (tuple(keep_list), tuple(give_list))


MESH = pl.DeviceIdType.MESH
BLOCK = 40
QS, PS, STREAM, WIDTH, FF, MICRO = 17, 2, 512, 768, 3072, 2
ROWS = MICRO * STREAM
CLS = 16 * BLOCK
HALF = 1280
PART = (HALF, 1152, 768)
FIRST = (0, 2560, 4864)
CHUNKS = (
    (0, 0, 640, 256, 384), (0, 640, 640, 256, 384), (1, 0, 768, 256, 512), (1, 768, 384, 128, 256), (2, 0, 768, 256, 512),
    (3, 0, 48, 16, 32), (3, 48, 48, 16, 32),
)
SHORT = (0, 1, 6)
SLOTS = 40 * len(CHUNKS)
OWN = 24
PIECE = 256
FF_OWN = 96
BF, F32 = jnp.bfloat16, jnp.float32
OFF = ()
RATE = (3, 4, 0.5, 1.5, 1, (6, 6, 6, 6, 6))
START = (0, 0, 1, 2, 3, 4, 5)
LEAD = 2


class Place:
    def __init__(self):
        self.x = lax.axis_index("tower")
        self.batch = lax.axis_index("batch")
        self.core = self.batch % 2
        self.y = (self.batch // 2) % 2
        self.z = self.batch // 4
        self.index = self.x * 16 + self.batch

    def device(self, x=None, y=None, z=None, core=None):
        x = self.x if x is None else x
        y = self.y if y is None else y
        z = self.z if z is None else z
        core = self.core if core is None else core
        return (x, z * 4 + y * 2 + core)

    def chip(self, x=None, y=None, z=None):
        x = self.x if x is None else x
        y = self.y if y is None else y
        z = self.z if z is None else z
        return x * 8 + z * 2 + y

    def layer(self, step):
        if step == 0:
            return self.z
        if step == 1:
            return self.z + 1 - 2 * (self.z % 2)
        if step == 2:
            return (self.z + 2) % 4
        return 3 - self.z

    @property
    def sibling(self):
        return self.device(core=1 - self.core)

    @property
    def over_x(self):
        return self.device(x=1 - self.x)

    @property
    def over_y(self):
        return self.device(y=1 - self.y)


def greet(place):
    barrier = pltpu.get_barrier_semaphore()
    peers = [place.device(z=place.layer(step)) for step in (1, 2, 3)]
    peers += [place.over_x, place.over_y, place.sibling]
    for peer in peers:
        pl.semaphore_signal(barrier, inc=1, device_id=peer, device_id_type=MESH)
    return lambda: pl.semaphore_wait(barrier, len(peers))


class Sender:
    def __init__(self, place, send_sems, recv_sems):
        self.place = place
        self.send_sems = send_sems
        self.recv_sems = recv_sems
        self.used = 0
        self.open = []

    def send(self, src, dst, slot, peer, only=None):
        copy = pltpu.make_async_remote_copy(
            src_ref=src,
            dst_ref=dst,
            send_sem=self.send_sems.at[self.used],
            recv_sem=self.recv_sems.at[slot],
            device_id=peer,
            device_id_type=MESH,
        )
        self.used += 1
        if only is None:
            copy.start()
        else:
            pl.when(only)(copy.start)
        self.open.append((copy, only))

    def arrived(self, dst, slot):
        pltpu.make_async_remote_copy(
            src_ref=dst,
            dst_ref=dst,
            send_sem=self.send_sems.at[0],
            recv_sem=self.recv_sems.at[slot],
            device_id=self.place.sibling,
            device_id_type=MESH,
        ).wait_recv()

    def close(self):
        for copy, only in self.open:
            if only is None:
                copy.wait_send()
            else:
                pl.when(only)(copy.wait_send)
        self.open = []


def tile(index, size, unit):
    return pl.ds(pl.multiple_of(index * unit, unit), size)


def loop(count, body):
    if getattr(body, '__name__', '') in OFF or 'all' in OFF:
        return
    def step(index, carry):
        body(index)
        return carry

    lax.fori_loop(0, count, step, 0)


def shifted(body, by):
    def moved(index):
        body(index + by)
    moved.__name__ = body.__name__
    return moved


def dot(left, right):
    return jnp.dot(left, right, preferred_element_type=F32)


def dot_nt(left, right):
    return lax.dot_general(left, right, (((1,), (1,)), ((), ())), preferred_element_type=F32)


def dot_tn(left, right):
    return lax.dot_general(left, right, (((0,), (0,)), ((), ())), preferred_element_type=F32)


def iota(shape, dim):
    return lax.broadcasted_iota(jnp.int32, shape, dim)


def centre(values):
    average = jnp.mean(values, -1, keepdims=True)
    centred = values - average
    inverse = lax.rsqrt(jnp.mean(centred * centred, -1, keepdims=True) + EPSILON)
    return centred * inverse, inverse


def centre_back(scaled, normed, inverse):
    return inverse * (
        scaled - jnp.mean(scaled, -1, keepdims=True) - normed * jnp.mean(scaled * normed, -1, keepdims=True)
    )


def weight_steps(place, sender, all_wide, all_tall):
    middle = (place.z == 1) | (place.z == 2)

    def view(chunk, core, chip, start=0, stop=None):
        part, offset, size, unused, unused = CHUNKS[chunk]
        size = (size if stop is None else stop) - start
        if part < 3:
            first = pl.multiple_of(FIRST[part] + core * PART[part] + offset + start, 128)
            return all_wide.at[tile(chip, 2 * OWN, 2 * OWN), pl.ds(first, size)]
        first = pl.multiple_of((chip * 2 + core) * FF_OWN + offset + start, 16)
        return all_tall.at[pl.ds(first, size), :]

    def slot(chunk, kind, layer):
        return (chunk * 10 + kind) * 4 + layer

    def along_z(chunk, block, at):
        sender.send(block, block, at, place.device(z=place.layer(1)))
        sender.send(block, block, at, place.device(z=place.layer(2)))
        sender.send(block, block, at, place.device(z=place.layer(3)), only=None if chunk in SHORT else middle)

    def begin(chunk):
        own = view(chunk, place.core, place.chip())
        along_z(chunk, own, slot(chunk, 0, place.z))
        sender.send(own, own, slot(chunk, 1, place.z), place.over_x)
        sender.send(own, own, slot(chunk, 2, place.z), place.over_y)
        sender.send(own, own, slot(chunk, 5, place.z), place.sibling)

    def along(chunk, step):
        layer = place.layer(step)
        block = view(chunk, place.core, place.chip(z=layer))
        sender.arrived(block, slot(chunk, 0, layer))
        if step == 2 and chunk not in SHORT:
            sender.send(block, block, slot(chunk, 0, layer), place.device(z=place.layer(1)), only=middle)
        sender.send(block, block, slot(chunk, 1, layer), place.over_x)
        sender.send(block, block, slot(chunk, 2, layer), place.over_y)
        sender.send(block, block, slot(chunk, 5, layer), place.sibling)

    def across(chunk, step):
        layer = place.layer(step)
        chip_x, chip_y = place.chip(x=1 - place.x, z=layer), place.chip(y=1 - place.y, z=layer)
        short = chunk in SHORT
        first, second = CHUNKS[chunk][3:]
        from_x, from_y = view(chunk, place.core, chip_x), view(chunk, place.core, chip_y)
        sender.arrived(from_x, slot(chunk, 1, layer))
        if step < (2 if short else 1):
            piece = from_x if short else view(chunk, place.core, chip_x, 0, second if step == 0 else first)
            sender.send(piece, piece, slot(chunk, 3, layer), place.over_y)
        sender.send(from_x, from_x, slot(chunk, 6, layer), place.sibling)
        sender.arrived(from_y, slot(chunk, 2, layer))
        if step >= (2 if short else 1):
            piece = from_y if short else view(chunk, place.core, chip_y, 0, first)
            sender.send(piece, piece, slot(chunk, 3, layer), place.over_x)
        if step == 0 and not short:
            piece = view(chunk, place.core, chip_y, second)
            sender.send(piece, piece, slot(chunk, 4, layer), place.over_x)
        sender.send(from_y, from_y, slot(chunk, 7, layer), place.sibling)

    def far(layer):
        return place.chip(x=1 - place.x, y=1 - place.y, z=layer)

    def corner(chunk):
        first, second = CHUNKS[chunk][3:]
        sender.arrived(view(chunk, place.core, far(place.z), 0, second), slot(chunk, 3, place.z))
        sender.arrived(view(chunk, place.core, far(place.z), second), slot(chunk, 4, place.z))
        rest = view(chunk, place.core, far(place.z), first)
        along_z(chunk, rest, slot(chunk, 4, place.z))
        block = view(chunk, place.core, far(place.z))
        sender.send(block, block, slot(chunk, 8, place.z), place.sibling)

    def corner_along(chunk, step):
        layer = place.layer(step)
        rest = view(chunk, place.core, far(layer), CHUNKS[chunk][3])
        sender.arrived(rest, slot(chunk, 4, layer))
        if step == 2:
            sender.send(rest, rest, slot(chunk, 4, layer), place.device(z=place.layer(1)), only=middle)
        sender.send(rest, rest, slot(chunk, 9, layer), place.sibling)

    def corner_third(chunk, step):
        layer = place.layer(step)
        piece = view(chunk, place.core, far(layer), 0, None if chunk in SHORT else CHUNKS[chunk][3])
        sender.arrived(piece, slot(chunk, 3, layer))
        sender.send(piece, piece, slot(chunk, 8, layer), place.sibling)

    def twin(chunk):
        core = 1 - place.core
        for step in range(4):
            layer = place.layer(step)
            sender.arrived(view(chunk, core, place.chip(z=layer)), slot(chunk, 5, layer))
            sender.arrived(view(chunk, core, place.chip(x=1 - place.x, z=layer)), slot(chunk, 6, layer))
            sender.arrived(view(chunk, core, place.chip(y=1 - place.y, z=layer)), slot(chunk, 7, layer))
            if step == 0 or chunk in SHORT:
                sender.arrived(view(chunk, core, far(layer)), slot(chunk, 8, layer))
            else:
                sender.arrived(view(chunk, core, far(layer), 0, CHUNKS[chunk][3]), slot(chunk, 8, layer))
                sender.arrived(view(chunk, core, far(layer), CHUNKS[chunk][3]), slot(chunk, 9, layer))

    def steps():
        usual = (
            (5, twin, (None,)), (4, corner_along, (3,)), (3, corner_along, (1, 2)), (3, corner_third, (3,)),
            (2, corner, (None,)), (2, corner_third, (1, 2)), (2, across, (3,)), (1, across, (0, 1, 2)),
            (1, along, (3,)), (0, along, (1, 2)),
        )
        short = ((3, twin, (None,)), (2, corner_third, (0, 1, 2, 3)), (1, across, (0, 1, 2, 3)), (0, along, (1, 2, 3)))
        count = len(CHUNKS)
        for turn in range(START[-1] + 6):
            for chunk in range(count):
                for late, stage, places in short if chunk in SHORT else usual:
                    if START[chunk] == turn - late:
                        for step in places:
                            if step is None:
                                stage(chunk)
                            else:
                                stage(chunk, step)
                            yield chunk if stage is twin else None
            for chunk in range(count):
                if START[chunk] == turn + LEAD:
                    begin(chunk)

    return begin, steps


def cls_steps(place, sender, base, block_ref, merged, stage, out_ref):
    rows, half = 2 * BLOCK, WIDTH // 2
    mine = tile(place.core, half, half)
    other = tile(1 - place.core, half, half)

    def view(core, y, z):
        return out_ref.at[tile(z * 2 + y, rows, rows), tile(core, half, half)]

    sender.send(block_ref.at[:, other], stage.at[0], base, place.sibling)
    yield
    sender.arrived(stage.at[0], base)
    merged[...] = (block_ref[:, mine].astype(F32) + stage[0].astype(F32)).astype(BF)
    sender.send(merged, stage.at[1], base + 1, place.over_x)
    yield
    sender.arrived(stage.at[1], base + 1)
    own = view(place.core, place.y, place.z)
    own[...] = (merged[...].astype(F32) + stage[1].astype(F32)).astype(BF)
    middle = (place.z == 1) | (place.z == 2)
    sender.send(own, own, base + 2 + place.z, place.device(z=place.layer(2)))
    sender.send(own, own, base + 2 + place.z, place.device(z=place.layer(3)), only=middle)
    sender.send(own, own, base + 2 + place.z, place.device(z=place.layer(1)))
    for step in (0, 2, 1, 3):
        layer = place.layer(step)
        block = view(place.core, place.y, layer)
        if step > 0:
            yield
            sender.arrived(block, base + 2 + layer)
        if step == 2:
            sender.send(block, block, base + 2 + layer, place.device(z=place.layer(1)), only=middle)
        sender.send(block, block, base + 6 + layer, place.over_y)
        sender.send(block, block, base + 10 + layer, place.sibling)
    for step in (0, 2, 1, 3):
        yield
        layer = place.layer(step)
        block = view(place.core, 1 - place.y, layer)
        sender.arrived(block, base + 6 + layer)
        sender.send(block, block, base + 14 + layer, place.sibling)
    yield
    for step in range(4):
        layer = place.layer(step)
        sender.arrived(view(1 - place.core, place.y, layer), base + 10 + layer)
        sender.arrived(view(1 - place.core, 1 - place.y, layer), base + 14 + layer)


def sum_begin(place, sender, base, part_ref, stage_core, first, last):
    other = tile(1 - place.core, HALF, HALF)
    for chip in range(first, last):
        sender.send(part_ref.at[pl.ds(2 * OWN * chip, 2 * OWN), other], stage_core.at[chip], base + chip, place.sibling)


def sum_steps(place, sender, base, part_ref, work, stage_core, stage_pair, stage_z, final, stage_last, out_ref):
    mine = tile(place.core, HALF, HALF)
    other = tile(1 - place.core, HALF, HALF)
    order = (3, 2, 1, 0)
    blocks = [(dx, dy, step) for step in order for dx, dy in ((1, 1), (1, 0), (0, 1), (0, 0))]

    def x_first(step):
        return step % 2 == 0

    def chip_of(dx, dy, step):
        return place.chip(1 - place.x if dx else place.x, 1 - place.y if dy else place.y, place.layer(step))

    def add(index, landed):
        work[index] = (work[index].astype(F32) + landed.astype(F32)).astype(BF)

    for index, at in enumerate(blocks):
        if index % 4 == 0:
            yield
        dx, dy, step = at
        chip = chip_of(*at)
        sender.arrived(stage_core.at[chip], base + chip)
        work[index] = (part_ref[tile(chip, 2 * OWN, 2 * OWN), mine].astype(F32) + stage_core[chip].astype(F32)).astype(BF)
        if (dx if x_first(step) else dy) == 1:
            peer = place.over_x if x_first(step) else place.over_y
            sender.send(work.at[index], stage_pair.at[index], base + 16 + index, peer)

    def first_add(step):
        for second in (1, 0):
            keep = (0, second) if x_first(step) else (second, 0)
            sent = (1, second) if x_first(step) else (second, 1)
            index, source = blocks.index(keep + (step,)), blocks.index(sent + (step,))
            sender.arrived(stage_pair.at[source], base + 16 + source)
            add(index, stage_pair[source])
            if second:
                peer = place.over_y if x_first(step) else place.over_x
                sender.send(work.at[index], stage_pair.at[index], base + 32 + index, peer)

    def second_add(step):
        index = blocks.index((0, 0, step))
        source = blocks.index(((0, 1) if x_first(step) else (1, 0)) + (step,))
        sender.arrived(stage_pair.at[source], base + 32 + source)
        add(index, stage_pair[source])
        if step:
            sender.send(work.at[index], stage_z.at[step], base + 48 + step, place.device(z=place.layer(step)))

    yield
    first_add(3)
    yield
    first_add(2)
    yield
    second_add(3)
    yield
    first_add(1)
    yield
    second_add(2)
    yield
    first_add(0)
    yield
    second_add(1)
    yield
    second_add(0)
    yield
    total = work[blocks.index((0, 0, 0))].astype(F32)
    for step in (3, 2, 1):
        sender.arrived(stage_z.at[step], base + 48 + step)
        total = total + stage_z[step].astype(F32)
    top, low = total[:OWN], total[OWN:]
    is_first = place.core == 0
    final[...] = jnp.where(is_first, low, top)
    sender.send(final, stage_last, base + 52, place.sibling)
    out_ref[:, mine] = jnp.where(is_first, top, low)
    yield
    sender.arrived(stage_last, base + 52)
    out_ref[:, other] = stage_last[...]


def weave(units, *steps):
    for index, unit in enumerate(units):
        unit()
        for generator, count in steps:
            run(generator, int((index + 1) * count) - int(index * count))


def run_to(steps, chunk):
    for done in steps:
        if done == chunk:
            return


def run(steps, count=None):
    while count is None or count > 0:
        if next(steps, "end") == "end":
            return
        if count is not None:
            count -= 1


def layer_kernel(
    x_ref, bq_ref, bv_ref, bo_ref, g1_in, s1_in, b2_ref, g2_in, s2_in, b1_ref, wq_ref, wk_ref, wv_ref, wo_ref, w1_ref, w2_ref, qlen_ref, plen_ref, pos_ref,
    hidden_out, igrad_out, qw_ref, qb_ref, kw_ref, vw_ref, vb_ref, ow_ref, ob_ref, g1_ref, s1_ref, iw_ref, ib_ref,
    tw_ref, tb_ref, g2_ref, s2_ref,
    hidden_ref, igrad_ref, lines_s, wide, stage, wa, wb, vecs, b1, q_s, k_s, v_s, bias, sel, code,
    block, merged, cls_stage, cls, att_block, att_merged, att_stage, cls_att, n1, columns, h_low, slope, act, n2, d_out, d_branch, sums, sums_b1,
    q_rows, x_rows, att_rows, dq, dkv, part, work, stage_core, stage_pair, stage_z, final, stage_last, summed,
    send_sems, cls_sems, recv_sems, out_sems,
):
    place = Place()
    sender = Sender(place, send_sems, recv_sems)
    cls_sender = Sender(place, cls_sems, recv_sems)
    is_query = place.x == 0
    core = place.core
    scr = n1.at[pl.ds(0, STREAM), :]
    window = n1.at[pl.ds(0, 256), :]

    all_here = greet(place)

    cut = WIDTH // 2
    lines_s[...] = jnp.zeros_like(lines_s)
    for i, ref in enumerate((bq_ref, bv_ref, bo_ref, g1_in, s1_in, b2_ref, g2_in, s2_in)):
        lines_s[pl.ds(i, 1), pl.ds(0, OWN)] = ref[...].astype(F32).reshape(1, OWN)
    lines_s[pl.ds(16, 1), pl.ds(0, FF_OWN)] = b1_ref[...].astype(F32).reshape(1, FF_OWN)
    long_line = jnp.broadcast_to(lines_s[pl.ds(16, 1), :], (8, 128))
    for i in range(4):
        turned = long_line if i == 0 else pltpu.roll(long_line, 128 - OWN * i, 1)
        lines_s[pl.ds(8 + i, 1), :] = turned[:1, :]
    vec_cols = lines_s[...].T[:OWN, :].astype(BF)
    filled = (
        (wq_ref, 0, WIDTH, 0), (wv_ref, 0, cut, 768), (wk_ref, 0, WIDTH, 1280), (wv_ref, cut, cut, 2048),
        (wo_ref, 0, WIDTH, 2560), (w1_ref, 0, FF, 3328),
    )
    for at in (1152, 2432):
        wide[:, pl.ds(at, 128)] = jnp.zeros((32, 128), BF)
    for ref, start, size, at in filled:
        wide[pl.ds(0, OWN), pl.ds(at, size)] = ref[:, pl.ds(start, size)]
        wide[pl.ds(OWN, 8), pl.ds(at, size)] = jnp.zeros((8, size), BF)
    wide[pl.ds(0, OWN), pl.ds(1152, 128)] = vec_cols
    all_here()

    begin, weight_parts = weight_steps(place, sender, wa, wb)
    offsets = (0, HALF, HALF + PART[1])
    for chunk in range(3):
        first = pl.multiple_of(FIRST[chunk] + (1 - core) * PART[chunk], 128)
        landing = stage.at[:, pl.ds(offsets[chunk], PART[chunk])]
        sender.send(wide.at[:, pl.ds(first, PART[chunk])], landing, SLOTS + chunk, place.sibling)
    wb[tile(place.index, FF_OWN, FF_OWN), :] = w2_ref[...]

    def assemble(chunk):
        sender.arrived(stage.at[:, pl.ds(offsets[chunk], PART[chunk])], SLOTS + chunk)
        first = pl.multiple_of(FIRST[chunk] + core * PART[chunk], 128)
        mine = wide[pl.ds(0, OWN), pl.ds(first, PART[chunk])].astype(F32)
        other = stage[pl.ds(0, OWN), pl.ds(offsets[chunk], PART[chunk])].astype(F32)
        top, low = jnp.where(core == 0, mine, other), jnp.where(core == 0, other, mine)
        wa[tile(place.chip(), 2 * OWN, 2 * OWN), pl.ds(first, PART[chunk])] = jnp.concatenate([top, low], 0).astype(BF)

    assemble(0)
    for chunk in range(len(CHUNKS)):
        if START[chunk] == 0:
            begin(chunk)
    assemble(1)
    assemble(2)
    for chunk in range(len(CHUNKS)):
        if 0 < START[chunk] < LEAD:
            begin(chunk)

    ends, starts = [], []
    for m in range(MICRO):
        end = jnp.int32(0)
        ends.append([])
        starts.append([])
        for i in range(QS):
            length = jnp.where(is_query, qlen_ref[m, i], plen_ref[m, i] if i < PS else 0)
            starts[m].append(end)
            end = end + length
            ends[m].append(end)
    def cls_places(rows, offset):
        at = iota((rows, 128), 0)
        found = jnp.full((rows, 128), -1, jnp.int32)
        label = jnp.full((rows, 128), -1, jnp.int32)
        for m in range(MICRO):
            for i in range(QS):
                row = jnp.where(is_query, QS * m + i, MICRO * QS + PS * m + i if i < PS else -1000) + offset
                found = jnp.where(at == row, m * STREAM + starts[m][i], found)
                label = jnp.where(at == row, m * 64 + i, label)
        return found[:, :1], label[:, :1]

    found, label = cls_places(BLOCK, 0)
    sel[...] = (found == iota((BLOCK, ROWS), 1)).astype(BF)
    ours = label >= 0
    low_lanes = iota((BLOCK, 128), 1) < 64
    coded = jnp.zeros((BLOCK, 128), jnp.int32)
    at_row, at_lane = iota((BLOCK, 128), 0), iota((BLOCK, 128), 1)
    for m in range(MICRO):
        for i in range(QS):
            here = (at_row == jnp.where(is_query, -1000, BLOCK - MICRO + m)) & (at_lane == i)
            coded = jnp.where(here, pos_ref[m, i], coded)
    coded = coded.astype(F32)

    def both(rows):
        return jnp.concatenate([jnp.where(low_lanes, rows, 0.0), jnp.where(low_lanes, 0.0, rows)], 0).astype(BF)

    def for_chip(rows):
        nothing = jnp.zeros_like(rows)
        return jnp.concatenate([jnp.where(core == 0, rows, nothing), jnp.where(core == 0, nothing, rows)], 0).astype(BF)

    x_rows[...] = dot(sel[...], x_ref[...])
    block[...] = for_chip(x_rows[...])
    block[:, pl.ds(0, 128)] = for_chip(x_rows[:, pl.ds(0, 128)] + coded)
    x_parts = cls_steps(place, cls_sender, SLOTS + 3, block, merged, cls_stage, cls)
    run(x_parts, 1)
    weights = weight_parts()

    row_of_key = iota((8, STREAM), 1)
    row_of_query = iota((STREAM, 128), 0)
    for m in range(MICRO):
        key_label = jnp.zeros((8, STREAM), jnp.int32)
        query_label = jnp.zeros((STREAM, 128), jnp.int32)
        for end in ends[m]:
            key_label += (row_of_key >= end).astype(jnp.int32)
            query_label += (row_of_query >= end).astype(jnp.int32)
        code[:, pl.ds(m * STREAM, STREAM)] = key_label + m * 64
        same = query_label[:, :1] == key_label[:1, :]
        bias[pl.ds(m * STREAM, STREAM), :] = jnp.where(same, 0.0, MASKED).astype(BF)

    seen = (label == code[pl.ds(0, 1), :]).astype(F32)
    seen2 = jnp.concatenate([seen, seen], 0) > 0.5
    for count in RATE[5]:
        run(x_parts, 1)
        run(weights, count)
    run_to(weights, 1)

    vecs[...] = wa[:, pl.ds(1152, 128)].astype(F32).T[:16, :]
    low_at, out_at = iota((FF_OWN, 384), 0), iota((FF_OWN, 384), 1)
    spread = jnp.zeros((FF_OWN, 384), jnp.bool_)
    row8, lane8 = iota((8, 384), 0), iota((8, 384), 1)
    pick = jnp.zeros((8, 384), jnp.bool_)
    for a in range(4):
        pick |= (lane8 >= 96 * a + 24 * row8) & (lane8 < 96 * a + 24 * row8 + 24) & (row8 < 4)
        for j in range(4):
            spread |= (low_at >= 24 * a) & (low_at < 24 * a + 24) & (out_at - low_at == 72 * a + 24 * j)
    spread = spread.astype(BF)
    for t in range(8):
        found_b1 = dot_tn(wa[pl.ds(FF_OWN * t, FF_OWN), pl.ds(1152, 128)], spread)
        b1[:, pl.ds(384 * t, 384)] = jnp.sum(jnp.where(pick, found_b1[8:16], 0.0), 0, keepdims=True)

    def vec(i):
        return vecs[pl.ds(i, 1), :]

    def project_q(i):
        rows = tile(i, 512, 512)
        xb = x_ref[rows, :]
        q_s[rows, :] = ((dot(xb, wa[:, pl.ds(0, WIDTH)]) + vec(0)).astype(BF).astype(F32) * 0.125).astype(BF)

    def project_k(i):
        rows = tile(i, 512, 512)
        k_s[rows, :] = dot(x_ref[rows, :], wa[:, pl.ds(HALF, WIDTH)]).astype(BF)

    def project_v(i):
        rows = tile(i, 512, 512)
        xb = x_ref[rows, :]
        v_s[rows, pl.ds(0, cut)] = (dot(xb, wa[:, pl.ds(WIDTH, cut)]) + vecs[pl.ds(1, 1), pl.ds(0, cut)]).astype(BF)
        v_s[rows, pl.ds(cut, cut)] = (
            dot(xb, wa[:, pl.ds(HALF + WIDTH, cut)]) + vecs[pl.ds(1, 1), pl.ds(cut, cut)]
        ).astype(BF)

    run(weights, 1)
    weave([functools.partial(loop, 1, shifted(f, i)) for f in (project_q, project_k, project_v) for i in range(2)], (weights, RATE[3]), (x_parts, 0.5))

    q_rows[...] = dot(sel[...], q_s[...])

    def own_shares(pair):
        cols = pl.ds(128 * pair, 128) if isinstance(pair, int) else tile(pair, 128, 128)
        q2 = both(q_rows[:, cols])
        scores = jnp.where(seen2, dot_nt(q2, k_s[:, cols]), MASKED)
        powers = jnp.where(seen2, jnp.exp(scores - jnp.max(scores, -1, keepdims=True)), 0.0)
        total = jnp.sum(powers, -1, keepdims=True)
        return q2, powers * (1.0 / jnp.where(total > 0, total, 1.0))

    def own_attend(pair):
        cols = pl.ds(128 * pair, 128)
        unused, shares = own_shares(pair)
        out = dot(shares.astype(BF), v_s[:, cols])
        att_rows[:, cols] = jnp.where(low_lanes, out[:BLOCK], out[BLOCK:])

    weave([functools.partial(own_attend, pair) for pair in range(6)], (weights, RATE[4]), (x_parts, 0.5))
    run(x_parts)

    att_block[...] = for_chip(jnp.where(ours, att_rows[...], 0.0))
    cls_parts = cls_steps(place, sender, SLOTS + 21, att_block, att_merged, att_stage, cls_att)
    run(cls_parts, 1)

    def attend(pair, m):
        cols = pl.ds(128 * pair, 128)
        keys = pl.ds(m * STREAM, STREAM)
        k2, v2 = k_s[keys, cols], v_s[keys, cols].astype(F32)
        low_keys = iota((STREAM, 128), 1) < 64
        values = jnp.concatenate([jnp.where(low_keys, v2, 1.0), jnp.where(low_keys, 1.0, v2)], 1).astype(BF)
        low = iota((256, 128), 1) < 64
        for i in range(2):
            rows = pl.ds(m * STREAM + 256 * i, 256)
            q2 = q_s[rows, cols].astype(F32)
            heads = jnp.concatenate([jnp.where(low, q2, 0.0), jnp.where(low, 0.0, q2)], 0).astype(BF)
            scores = dot_nt(heads, k2)
            masked = bias[rows, :].astype(F32)
            powers = []
            for head in range(2):
                part_scores = scores[256 * head : 256 * head + 256] + masked
                powers.append(jnp.exp(part_scores - jnp.max(part_scores, -1, keepdims=True)).astype(BF))
            out = dot(jnp.concatenate(powers, 0), values)
            first, second = out[:256, :128], out[256:, 128:]
            sums_of = pltpu.roll(jnp.where(low, second, first), 64, 1)
            igrad_ref[rows, cols] = (jnp.where(low, first, second) * (1.0 / sums_of)).astype(BF)

    weave(
        [functools.partial(attend, pair, m) for pair in range(6) for m in range(MICRO)], (cls_parts, 1), (weights, RATE[0])
    )
    run(cls_parts)

    def cls_first(i):
        rows = tile(i, CLS, CLS)
        at = iota((CLS, 1), 0) + i * CLS
        group = jnp.zeros((CLS, 1), jnp.int32)
        for b in range(1, 16):
            group += (at >= BLOCK * b).astype(jnp.int32)
        xin = jnp.where(at - BLOCK * group < BLOCK - MICRO, cls[rows, :].astype(F32), 0.0)
        normed, inverse = centre(xin + (dot(cls_att[rows, :], wa[:, pl.ds(2560, WIDTH)]) + vec(2)))
        n1[rows, :] = normed
        columns[rows, pl.ds(0, 1)] = inverse
        h_low[rows, :] = (normed * vec(3) + vec(4)).astype(BF)

    run_to(weights, 2)
    loop(1, cls_first)
    run(weights, 1)

    at = iota((CLS, 1), 0)
    at_col = iota((1, CLS), 1)

    def kinds(index):
        group = jnp.zeros(index.shape, jnp.int32)
        for b in range(1, 16):
            group += (index >= BLOCK * b).astype(jnp.int32)
        inner = index - BLOCK * group
        query_m = (inner >= QS).astype(jnp.int32)
        is_q = inner < MICRO * QS
        passage_m = (inner >= MICRO * QS + PS).astype(jnp.int32)
        is_p = (inner >= MICRO * QS) & (inner < MICRO * (QS + PS))
        return group, inner, is_q, query_m, is_p, passage_m

    group, inner, is_q, query_m, unused, unused = kinds(at)
    source = (group * BLOCK + (BLOCK - MICRO) + query_m == at_col).astype(BF)
    codes = dot(source, cls[:, pl.ds(0, 128)])
    wanted = jnp.sum(jnp.where(iota((CLS, 128), 1) == inner - QS * query_m, codes, 0.0), 1, keepdims=True)
    wanted = wanted.astype(jnp.int32)
    target = 2 * wanted - (wanted & 1) + PS * query_m
    columns[:, pl.ds(2, 1)] = target.astype(F32)
    cls_sender.close()
    y_low = cls
    hid_blk = y_low.at[pl.ds(0, STREAM), :]

    def cls_inner(i):
        rows = pl.ds(0, CLS)
        cols = tile(i, 512, 512)
        wcols = pl.ds(pl.multiple_of(3328 + i * 512, 128), 512)
        u = dot(h_low[rows, :], wa[:, wcols]) + b1[:, cols]
        phi = 0.5 * (1.0 + lax.erf(u * 0.7071067811865476))
        act[rows, cols] = (u * phi).astype(BF)
        slope[rows, cols] = (phi + u * jnp.exp(-0.5 * u * u) * 0.3989422804014327).astype(BF)

    weave([functools.partial(loop, 1, shifted(cls_inner, i)) for i in range(3)], (weights, RATE[1]))
    run_to(weights, 4)
    weave([functools.partial(loop, 1, shifted(cls_inner, i)) for i in range(3, 6)], (weights, RATE[1]))
    run_to(weights, 6)

    def cls_second(i):
        rows = tile(i, CLS, CLS)
        r = h_low[rows, :].astype(F32) + (dot(act[rows, :], wb[...]) + vec(5))
        normed, inverse = centre(r)
        n2[rows, :] = normed
        columns[rows, pl.ds(1, 1)] = inverse
        y_low[rows, :] = (normed * vec(6) + vec(7)).astype(BF)

    loop(1, cls_second)

    unused, unused, is_q, query_m, unused, unused = kinds(iota((CLS, 1), 0))
    lane = iota((1, 128), 1)
    paired = is_q & (lane < 16 * MICRO * PS) & (((lane >> 1) & 1) == query_m)
    hit = paired & (columns[:, pl.ds(2, 1)] == lane.astype(F32))
    passage = iota((128, CLS), 0)
    chosen = BLOCK * (passage >> 2) + MICRO * QS + (passage & 3) == iota((128, CLS), 1)
    chosen = (chosen & (passage < 16 * MICRO * PS)).astype(BF)
    y_all = y_low[...]
    y_passages = dot(chosen, y_all).astype(BF)
    logits = jnp.where(paired, dot_nt(y_all, y_passages) * WIDTH ** -0.5, MASKED)
    powers = jnp.where(paired, jnp.exp(logits - jnp.max(logits, -1, keepdims=True)), 0.0)
    total = jnp.sum(powers, -1, keepdims=True)
    shares = powers * (1.0 / jnp.where(is_q, total, 1.0))
    d_logits = ((shares - hit.astype(F32)) * (1.0 / MICRO)).astype(BF)
    d_passages = dot_tn(d_logits, y_all)
    d_high = d_passages.astype(BF)
    d_rest = (d_passages - d_high.astype(F32)).astype(BF)
    d_y = (dot(d_logits, y_passages) + dot_tn(chosen, d_high) + dot_tn(chosen, d_rest)) * WIDTH ** -0.5
    normed = n2[...]
    sums[pl.ds(0, 1), :] = jnp.sum(d_y * normed, 0, keepdims=True)
    sums[pl.ds(1, 1), :] = jnp.sum(d_y, 0, keepdims=True)
    d_sum = centre_back(d_y * vec(6), normed, columns[:, pl.ds(1, 1)])
    n2[...] = d_sum
    d_out[...] = d_sum.astype(BF)
    sums[pl.ds(2, 1), :] = jnp.sum(d_out[...].astype(F32), 0, keepdims=True)

    def cls_inner_back(i):
        cols = tile(i, 512, 512)
        d_act = dot_nt(d_out[...], wb[cols, :])
        d_u = (d_act * slope[:, cols].astype(F32)).astype(BF)
        slope[:, cols] = d_u
        sums_b1[:, cols] = jnp.sum(d_u.astype(F32), 0, keepdims=True)

    loop(6, cls_inner_back)

    def cls_first_back(i):
        rows = tile(i, CLS, CLS)
        d_hidden = n2[rows, :] + dot_nt(slope[rows, :], wa[:, pl.ds(3328, FF)])
        normed = n1[rows, :]
        gains = jnp.sum(d_hidden * normed, 0, keepdims=True)
        shifts = jnp.sum(d_hidden, 0, keepdims=True)
        d_sum = centre_back(d_hidden * vec(3), normed, columns[rows, pl.ds(0, 1)])
        n2[rows, :] = d_sum
        d_low = d_sum.astype(BF)
        d_branch[rows, :] = d_low
        totals = (gains, shifts, jnp.sum(d_low.astype(F32), 0, keepdims=True))
        for place_in, value in enumerate(totals):
            line = pl.ds(3 + place_in, 1)
            sums[line, :] = jnp.where(i == 0, value, sums[line, :] + value)

    loop(1, cls_first_back)

    own_sum = jnp.where(ours, n2[tile(place.batch, BLOCK, BLOCK), :], 0.0)
    d_att = dot_nt(own_sum.astype(BF), wa[:, pl.ds(2560, WIDTH)]).astype(BF).astype(F32)
    att_rows[...] = d_att

    def own_back(pair):
        cols = tile(pair, 128, 128)
        d_a2 = both(att_rows[:, cols])
        k2, v2 = k_s[:, cols], v_s[:, cols]
        q2, shares = own_shares(pair)
        d_shares = dot_nt(d_a2, v2)
        d_scores = (shares * (d_shares - jnp.sum(d_shares * shares, -1, keepdims=True))).astype(BF)
        d_q2 = dot(d_scores, k2)
        dq[:, cols] = (jnp.where(low_lanes, d_q2[:BLOCK], d_q2[BLOCK:]) * 0.125).astype(BF)
        dkv[:, cols] = dot_tn(d_scores, q2).astype(BF)
        dkv[:, pl.ds(pl.multiple_of(WIDTH + 128 * pair, 128), 128)] = dot_tn(shares.astype(BF), d_a2).astype(BF)

    loop(6, own_back)

    part[:, pl.ds(0, WIDTH)] = dot_tn(x_rows[...].astype(BF), dq[...]).astype(BF)

    def project_back(i):
        out = dot_tn(x_ref[:, tile(i, 256, 256)], dkv[...])
        part[tile(i, 256, 256), pl.ds(WIDTH, 2 * WIDTH)] = out.astype(BF)

    line = iota((128, WIDTH), 0)
    q_line = jnp.sum(dq[...].astype(F32), 0, keepdims=True)
    v_line = jnp.sum(dkv[:, pl.ds(WIDTH, WIDTH)].astype(F32), 0, keepdims=True)
    lines = jnp.where(line == 0, q_line, jnp.where(line == 1, v_line, 0.0))
    part[:, pl.ds(3 * WIDTH, 128)] = lines.T.astype(BF)
    part[:, pl.ds(3 * WIDTH + 128, 128)] = jnp.zeros((WIDTH, 128), BF)
    for i, (first, last) in enumerate(((0, 5), (5, 10), (10, 16))):
        loop(1, shifted(project_back, i))
        sum_begin(place, sender, SLOTS + 39, part, stage_core, first, last)

    steps = sum_steps(place, sender, SLOTS + 39, part, work, stage_core, stage_pair, stage_z, final, stage_last, summed)
    run(steps, 5)

    leaving = []

    def leave(src, dst, rows, at):
        copy = pltpu.make_async_copy(src.at[rows, :], dst.at[rows, :], out_sems.at[at])
        copy.start()
        leaving.append(copy)

    def rows_first(i):
        rows = pl.ds(STREAM * i, STREAM)
        branch = dot(igrad_ref[rows, :], wa[:, pl.ds(2560, WIDTH)]) + vec(2)
        normed, unused = centre(x_ref[rows, :].astype(F32) + branch)
        low = (normed * vec(3) + vec(4)).astype(BF)
        hid_blk[...] = low
        scr[...] = low.astype(F32) + vec(5)

    def rows_inner(j):
        cols = tile(j, 512, 512)
        u = dot(hid_blk[...], wa[:, pl.ds(pl.multiple_of(3328 + j * 512, 128), 512)]) + b1[:, cols]
        active = (u * (0.5 * (1.0 + lax.erf(u * 0.7071067811865476)))).astype(BF)
        scr[...] += dot(active, wb[cols, :])

    def rows_second(i):
        normed, unused = centre(scr[...])
        valid = iota((STREAM, 1), 0) < ends[i][QS - 1]
        rows = pl.ds(STREAM * i, STREAM)
        hidden_ref[rows, :] = jnp.where(valid, normed * vec(6) + vec(7), 0.0).astype(BF)
        leave(hidden_ref, hidden_out, rows, i)

    units = []
    for i in range(MICRO):
        units.append(functools.partial(rows_first, i))
        units += [functools.partial(loop, 1, shifted(rows_inner, j)) for j in range(6)]
        units.append(functools.partial(rows_second, i))
    weave(units[:4])
    weave(units[4:], (steps, RATE[2]))

    back_rows = dot_nt(dq[...], wa[:, pl.ds(0, WIDTH)]) + own_sum
    q_s[:, pl.ds(0, 128)] = jnp.concatenate([sel[...].astype(F32), jnp.zeros((128 - BLOCK, ROWS), F32)], 0).T.astype(BF)
    back_low = jnp.concatenate([back_rows, jnp.zeros((128 - BLOCK, WIDTH), F32)], 0)
    back_rest = (back_low - back_low.astype(BF).astype(F32)).astype(BF)
    back_low = back_low.astype(BF)

    def input_back(i):
        rows = tile(i, 256, 256)
        total = dot_nt(dkv[rows, pl.ds(0, WIDTH)], wa[:, pl.ds(HALF, WIDTH)])
        total += dot_nt(dkv[rows, pl.ds(WIDTH, cut)], wa[:, pl.ds(WIDTH, cut)])
        total += dot_nt(dkv[rows, pl.ds(WIDTH + cut, cut)], wa[:, pl.ds(HALF + WIDTH, cut)])
        hit_rows = q_s[rows, pl.ds(0, 128)]
        total += dot(hit_rows, back_low) + dot(hit_rows, back_rest)
        igrad_ref[rows, :] = total.astype(BF)

    for i in range(MICRO):
        loop(2, shifted(input_back, 2 * i))
        leave(igrad_ref, igrad_out, pl.ds(STREAM * i, STREAM), 2 + i)
        run(steps, 1)

    tall_first = jnp.minimum(place.index * FF_OWN // 128, (FF - 256) // 128) * 128
    tall_at = place.index * FF_OWN - tall_first
    own_first = jnp.minimum(place.index * OWN // 128, (WIDTH - 256) // 128) * 128
    own_at = place.index * OWN - own_first

    window[...] = dot_tn(act[:, pl.ds(pl.multiple_of(tall_first, 128), 256)], d_out[...])
    tw_ref[...] = window[pl.ds(pl.multiple_of(tall_at, 8), FF_OWN), :]
    own_cols = pl.ds(pl.multiple_of(own_first, 128), 256)
    own_lines = pl.ds(pl.multiple_of(own_at, 8), OWN)
    window[...] = dot_tn(cls_att[:, own_cols], d_branch[...])
    ow_ref[...] = window[own_lines, :]
    for j in range(4):
        window[...] = dot_tn(h_low[:, own_cols], slope[:, pl.ds(WIDTH * j, WIDTH)])
        iw_ref[:, pl.ds(WIDTH * j, WIDTH)] = window[own_lines, :]

    def own_lanes(line, first, shift, size):
        window = jnp.broadcast_to(line[:, pl.ds(pl.multiple_of(first, 128), 256)], (8, 256))
        return pltpu.roll(window, 256 - shift, 1)[:1, :size]

    for ref, i in ((g2_ref, 0), (s2_ref, 1), (tb_ref, 2), (g1_ref, 3), (s1_ref, 4), (ob_ref, 5)):
        ref[...] = own_lanes(sums.at[pl.ds(i, 1), :], own_first, own_at, OWN)
    ib_ref[...] = own_lanes(sums_b1, tall_first, tall_at, FF_OWN)

    run(steps)
    qw_ref[...] = summed[:, pl.ds(0, WIDTH)]
    kw_ref[...] = summed[:, pl.ds(WIDTH, WIDTH)]
    vw_ref[...] = summed[:, pl.ds(2 * WIDTH, WIDTH)]
    lines = jnp.concatenate([summed[:, pl.ds(3 * WIDTH, 128)], jnp.zeros((128 - OWN, 128), F32)], 0).T
    qb_ref[...] = lines[0:1, :OWN]
    vb_ref[...] = lines[1:2, :OWN]
    for copy in leaving:
        copy.wait()
    sender.close()


def copy_kernel(count, *refs):
    ins, outs, held, sems = refs[:count], refs[count : 2 * count], refs[2 * count : 3 * count], refs[-1]
    pieces = []
    for i in range(count):
        rows = ins[i].shape[0]
        size = PIECE if rows > PIECE else rows
        pieces += [(i, pl.ds(at, size)) for at in range(0, rows, size)]
    first = [pltpu.make_async_copy(ins[i].at[at], held[i].at[at], sems.at[0, n]) for n, (i, at) in enumerate(pieces)]
    second = [pltpu.make_async_copy(held[i].at[at], outs[i].at[at], sems.at[1, n]) for n, (i, at) in enumerate(pieces)]
    for copy in first:
        copy.start()
    for before, after in zip(first, second):
        before.wait()
        after.start()
    for copy in second:
        copy.wait()


def fast(hidden_in, query_lengths, passage_lengths, positives, stored):
    (query_weight, query_bias, key_weight, value_weight, value_bias, output_weight, output_bias, first_gain,
     first_shift, inner_weight, inner_bias, outer_weight, outer_bias, second_gain, second_shift) = stored
    shapes = [
        ((ROWS, WIDTH), BF), ((ROWS, WIDTH), BF), ((OWN, WIDTH), F32), ((1, OWN), F32), ((OWN, WIDTH), F32),
        ((OWN, WIDTH), F32), ((1, OWN), F32), ((OWN, WIDTH), F32), ((1, OWN), F32), ((1, OWN), F32), ((1, OWN), F32),
        ((OWN, FF), F32), ((1, FF_OWN), F32), ((FF_OWN, WIDTH), F32), ((1, OWN), F32), ((1, OWN), F32), ((1, OWN), F32),
    ]
    scratch = [
        pltpu.VMEM((ROWS, WIDTH), BF), pltpu.VMEM((ROWS, WIDTH), BF),
        pltpu.VMEM((128, 128), F32), pltpu.VMEM((32, 6400), BF), pltpu.VMEM((32, 3200), BF), pltpu.VMEM((WIDTH, 6400), BF), pltpu.VMEM((FF, WIDTH), BF),
        pltpu.VMEM((16, WIDTH), F32), pltpu.VMEM((1, FF), F32),
        pltpu.VMEM((ROWS, WIDTH), BF), pltpu.VMEM((ROWS, WIDTH), BF), pltpu.VMEM((ROWS, WIDTH), BF),
        pltpu.VMEM((ROWS, STREAM), BF), pltpu.VMEM((BLOCK, ROWS), BF), pltpu.VMEM((8, ROWS), jnp.int32),
        pltpu.VMEM((2 * BLOCK, WIDTH), BF), pltpu.VMEM((2 * BLOCK, WIDTH // 2), BF),
        pltpu.VMEM((2, 2 * BLOCK, WIDTH // 2), BF), pltpu.VMEM((CLS, WIDTH), BF),
        pltpu.VMEM((2 * BLOCK, WIDTH), BF), pltpu.VMEM((2 * BLOCK, WIDTH // 2), BF),
        pltpu.VMEM((2, 2 * BLOCK, WIDTH // 2), BF), pltpu.VMEM((CLS, WIDTH), BF),
        pltpu.VMEM((CLS, WIDTH), F32), pltpu.VMEM((CLS, 128), F32), pltpu.VMEM((CLS, WIDTH), BF),
        pltpu.VMEM((CLS, FF), BF), pltpu.VMEM((CLS, FF), BF),
        pltpu.VMEM((CLS, WIDTH), F32), pltpu.VMEM((CLS, WIDTH), BF), pltpu.VMEM((CLS, WIDTH), BF),
        pltpu.VMEM((8, WIDTH), F32), pltpu.VMEM((1, FF), F32),
        pltpu.VMEM((BLOCK, WIDTH), F32), pltpu.VMEM((BLOCK, WIDTH), F32), pltpu.VMEM((BLOCK, WIDTH), F32),
        pltpu.VMEM((BLOCK, WIDTH), BF), pltpu.VMEM((ROWS, 2 * WIDTH), BF),
        pltpu.VMEM((WIDTH, 2 * HALF), BF),
        pltpu.VMEM((16, 2 * OWN, HALF), BF), pltpu.VMEM((16, 2 * OWN, HALF), BF), pltpu.VMEM((16, 2 * OWN, HALF), BF),
        pltpu.VMEM((4, 2 * OWN, HALF), BF), pltpu.VMEM((OWN, HALF), F32), pltpu.VMEM((OWN, HALF), F32),
        pltpu.VMEM((OWN, 2 * HALF), F32),
        pltpu.SemaphoreType.DMA((380,)), pltpu.SemaphoreType.DMA((20,)), pltpu.SemaphoreType.DMA((SLOTS + 92,)), pltpu.SemaphoreType.DMA((4,)),
    ]
    vmem = pl.BlockSpec(memory_space=pltpu.VMEM)
    smem = pl.BlockSpec(memory_space=pltpu.SMEM)
    outs = pl.pallas_call(
        layer_kernel,
        out_shape=[jax.ShapeDtypeStruct(shape, kind) for shape, kind in shapes],
        in_specs=[vmem] * 16 + [smem] * 3,
        out_specs=[pl.BlockSpec(memory_space=pl.ANY)] * 2 + [vmem] * (len(shapes) - 2),
        scratch_shapes=scratch,
        compiler_params=pltpu.CompilerParams(collective_id=0, has_side_effects=True, vmem_limit_bytes=63 * 2**20),
    )(
        hidden_in.reshape(ROWS, WIDTH), query_bias, value_bias, output_bias, first_gain, first_shift, outer_bias,
        second_gain, second_shift, inner_bias, query_weight, key_weight, value_weight, output_weight, inner_weight,
        outer_weight, query_lengths, passage_lengths, positives,
    )
    outs = pl.pallas_call(
        functools.partial(copy_kernel, len(shapes)),
        out_shape=[jax.ShapeDtypeStruct(shape, kind) for shape, kind in shapes],
        in_specs=[pl.BlockSpec(memory_space=pl.ANY)] * len(shapes),
        out_specs=[pl.BlockSpec(memory_space=pl.ANY)] * len(shapes),
        scratch_shapes=[pltpu.VMEM(shape, kind) for shape, kind in shapes] + [pltpu.SemaphoreType.DMA((2, len(shapes) + 2 * (ROWS // PIECE - 1)))],
    )(*outs)
    shape = hidden_in.shape
    return tuple(
        out.reshape(shape) if i < 2 else (out.reshape(-1) if out.shape[0] == 1 else out) for i, out in enumerate(outs)
    )


def local(
    hidden_in,
    query_lengths,
    passage_lengths,
    positives,
    query_weight,
    query_bias,
    key_weight,
    value_weight,
    value_bias,
    output_weight,
    output_bias,
    first_gain,
    first_shift,
    inner_weight,
    inner_bias,
    outer_weight,
    outer_bias,
    second_gain,
    second_shift,
):
    stored = (
        query_weight,
        query_bias,
        key_weight,
        value_weight,
        value_bias,
        output_weight,
        output_bias,
        first_gain,
        first_shift,
        inner_weight,
        inner_bias,
        outer_weight,
        outer_bias,
        second_gain,
        second_shift,
    )
    sizes = (lax.axis_size("tower"), lax.axis_size("batch"), hidden_in.shape, inner_weight.shape)
    if sizes == (2, 16, (MICRO, 1, STREAM, WIDTH), (OWN, FF)) and query_lengths.shape[1] == QS:
        return fast(hidden_in, query_lengths, passage_lengths, positives, stored)
    micro = hidden_in.shape[0]
    width = hidden_in.shape[3]
    cls_scale = width ** (-0.5)
    side = lax.axis_index("tower")
    is_query = side == 0
    slot_count = query_lengths.shape[1]
    passage_count = passage_lengths.shape[1]
    half_count = (slot_count + 1) // 2
    extra_rows = 2 * half_count - slot_count
    owners = lax.axis_size(("tower", "batch"))
    totals = tuple(
        (jnp.zeros((item.shape[0] * owners,) + item.shape[1:], jnp.float32) for item in stored)
    )
    half_totals = tuple(
        (jnp.zeros((item.shape[0] * owners // 2,) + item.shape[1:], jnp.float32) for item in stored)
    )
    shown_list = []
    grad_list = []
    for micro_step in range(micro):
        gathered = (
            lax.all_gather(query_weight, ("tower", "batch"), axis=0, tiled=True),
            lax.all_gather(query_bias, ("tower", "batch"), axis=0, tiled=True),
            lax.all_gather(key_weight, ("tower", "batch"), axis=0, tiled=True),
            lax.all_gather(value_weight, ("tower", "batch"), axis=0, tiled=True),
            lax.all_gather(value_bias, ("tower", "batch"), axis=0, tiled=True),
            lax.all_gather(output_weight, ("tower", "batch"), axis=0, tiled=True),
            lax.all_gather(output_bias, ("tower", "batch"), axis=0, tiled=True),
            lax.all_gather(first_gain, ("tower", "batch"), axis=0, tiled=True),
            lax.all_gather(first_shift, ("tower", "batch"), axis=0, tiled=True),
            lax.all_gather(inner_weight, ("tower", "batch"), axis=0, tiled=True),
            lax.all_gather(inner_bias, ("tower", "batch"), axis=0, tiled=True),
            lax.all_gather(outer_weight, ("tower", "batch"), axis=0, tiled=True),
            lax.all_gather(outer_bias, ("tower", "batch"), axis=0, tiled=True),
            lax.all_gather(second_gain, ("tower", "batch"), axis=0, tiled=True),
            lax.all_gather(second_shift, ("tower", "batch"), axis=0, tiled=True),
        )
        params = cast_params(gathered)
        inputs = hidden_in[micro_step, 0]
        passage_part = jnp.pad(passage_lengths[micro_step], (0, slot_count - passage_count))
        lengths = jnp.where(is_query, query_lengths[micro_step], passage_part)
        labels, valid, starts, live = segments(lengths, inputs.shape[0])
        saved, shown = forward(inputs, labels, valid, params)
        shown_list.append(shown)
        mine = jnp.where(live[:, None], shown[starts], 0.0)
        partner = partner_2(mine, "tower", 0)
        query_cls = jnp.where(is_query, mine, partner)
        passage_cls = jnp.where(is_query, partner, mine)[:passage_count]
        pooled = lax.all_gather(passage_cls, "batch", axis=0, tiled=True)
        padded_queries = jnp.pad(query_cls, ((0, extra_rows), (0, 0)))
        padded_targets = jnp.pad(positives[micro_step], (0, extra_rows))
        my_queries = lax.dynamic_slice_in_dim(padded_queries, side * half_count, half_count, 0)
        my_targets = lax.dynamic_slice_in_dim(padded_targets, side * half_count, half_count, 0)
        logits = product_nt(my_queries, pooled) * cls_scale
        highest = jnp.max(logits, -1, keepdims=True)
        powers = jnp.exp(logits - highest)
        shares = powers / jnp.sum(powers, -1, keepdims=True)
        columns = jnp.arange(pooled.shape[0], dtype=jnp.int32)
        target = (columns[None, :] == my_targets[:, None]).astype(jnp.float32)
        grad_logits = ((shares - target) / micro).astype(jnp.bfloat16)
        own_grad = product(grad_logits, pooled) * cls_scale
        pooled_grad = product_tn(grad_logits, my_queries) * cls_scale
        summed = lax.psum_scatter(pooled_grad, "batch", scatter_dimension=0, tiled=True)
        other_queries, other_passages = (
            partner_2(own_grad.astype(jnp.bfloat16), "tower", 0).astype(own_grad.dtype),
            partner_2(summed.astype(jnp.bfloat16), "tower", 0).astype(summed.dtype),
        )
        query_grad = jnp.concatenate([own_grad, other_queries], 0)[:slot_count]
        passage_grad = jnp.pad(summed + other_passages, ((0, slot_count - passage_count), (0, 0)))
        cotangent = jnp.where(is_query, query_grad, passage_grad)
        input_part, step_grads = backward(inputs, labels, cotangent, starts, live, saved, params)
        grad_list.append(input_part)
        totals = tuple((first + second for first, second in zip(totals, step_grads)))
    keep_all, give_all = split_halves(totals, side)
    came_all = jax.tree.map(
        lambda part, own: part.astype(own.dtype), partner_2(as_sent(give_all), "tower", 0), give_all
    )
    half_totals = tuple((first + second for first, second in zip(keep_all, came_all)))
    shards = lax.psum_scatter(half_totals, "batch", scatter_dimension=0, tiled=True)
    hidden_out = jnp.stack(shown_list)[:, None]
    input_grad = jnp.stack(grad_list)[:, None]
    return (
        hidden_out,
        input_grad,
        shards[0],
        shards[1],
        shards[2],
        shards[3],
        shards[4],
        shards[5],
        shards[6],
        shards[7],
        shards[8],
        shards[9],
        shards[10],
        shards[11],
        shards[12],
        shards[13],
        shards[14],
    )


def solution(mesh):
    placed = (
        P(None, "tower", "batch", None),
        P(None, "batch"),
        P(None, "batch"),
        P(None, "batch"),
        P(("tower", "batch"), None),
        P(("tower", "batch")),
        P(("tower", "batch"), None),
        P(("tower", "batch"), None),
        P(("tower", "batch")),
        P(("tower", "batch"), None),
        P(("tower", "batch")),
        P(("tower", "batch")),
        P(("tower", "batch")),
        P(("tower", "batch"), None),
        P(("tower", "batch")),
        P(("tower", "batch"), None),
        P(("tower", "batch")),
        P(("tower", "batch")),
        P(("tower", "batch")),
    )
    return jax.shard_map(
        local,
        mesh=mesh,
        in_specs=placed,
        out_specs=(
            P(None, "tower", "batch", None),
            P(None, "tower", "batch", None),
            P(("tower", "batch"), None),
            P(("tower", "batch")),
            P(("tower", "batch"), None),
            P(("tower", "batch"), None),
            P(("tower", "batch")),
            P(("tower", "batch"), None),
            P(("tower", "batch")),
            P(("tower", "batch")),
            P(("tower", "batch")),
            P(("tower", "batch"), None),
            P(("tower", "batch")),
            P(("tower", "batch"), None),
            P(("tower", "batch")),
            P(("tower", "batch")),
            P(("tower", "batch")),
        ),
        check_vma=False,
    )
```

```python
import functools

import jax
import jax.numpy as jnp
from jax import lax
from jax.experimental import pallas as pl
from jax.experimental.pallas import tpu as pltpu
from jax.sharding import PartitionSpec as P

HEADS = 12


EPSILON = 1e-12
MASKED = -1e30


def partner_2(x, axis, apart):
    return lax.ppermute(x, axis, [(i, i ^ 1 << apart) for i in range(lax.axis_size(axis))])


def as_sent(x):
    return jax.tree.map(lambda a: a.astype(jnp.bfloat16) if a.dtype == jnp.float32 else a, x)


def product(left, right):
    return jnp.dot(left, right, preferred_element_type=jnp.float32)


def product_tn(left, right):
    return jnp.einsum("ta,tb->ab", left, right, preferred_element_type=jnp.float32)


def product_nt(left, right):
    return jnp.einsum("ra,ba->rb", left, right, preferred_element_type=jnp.float32)


def normalize(values, gains, shifts):
    average = jnp.mean(values, -1, keepdims=True)
    centred = values - average
    inverse = lax.rsqrt(jnp.mean(centred * centred, -1, keepdims=True) + EPSILON)
    normed = centred * inverse
    return (normed * gains + shifts, normed, inverse)


def normalize_back(upstream, normed, inverse, gains):
    scaled = upstream * gains
    inner = (
        scaled
        - jnp.mean(scaled, -1, keepdims=True)
        - normed * jnp.mean(scaled * normed, -1, keepdims=True)
    )
    return (inner * inverse, jnp.sum(upstream * normed, 0), jnp.sum(upstream, 0))


def gelu_slope(values):
    return (
        0.5 * (1.0 + lax.erf(values * 0.7071067811865476))
        + values * jnp.exp(-0.5 * values * values) * 0.3989422804014327
    )


def segments(lengths, token_rows):
    ends = jnp.cumsum(lengths)
    places = jnp.arange(token_rows, dtype=jnp.int32)
    labels = jnp.sum((places[:, None] >= ends[None, :]).astype(jnp.int32), 1)
    starts = jnp.minimum(ends - lengths, token_rows - 1)
    return (labels, places < ends[-1], starts, lengths > 0)


def tail(inputs, attended, params):
    out_mat, out_vec, gain_one, shift_one = (params[5], params[6], params[7], params[8])
    inner_mat, inner_vec, outer_mat, outer_vec, gain_two, shift_two = params[9:15]
    branch = product(attended, out_mat) + out_vec
    hidden_full, normed_one, inverse_one = normalize(
        inputs.astype(jnp.float32) + branch, gain_one, shift_one
    )
    hidden_low = hidden_full.astype(jnp.bfloat16)
    inner = product(hidden_low, inner_mat) + inner_vec
    active = jax.nn.gelu(inner, approximate=False).astype(jnp.bfloat16)
    outer = product(active, outer_mat) + outer_vec
    result, normed_two, inverse_two = normalize(
        hidden_low.astype(jnp.float32) + outer, gain_two, shift_two
    )
    return (result, (normed_one, inverse_one, hidden_low, inner, active, normed_two, inverse_two))


def forward(inputs, labels, valid, params):
    query_mat, query_vec, key_mat, value_mat, value_vec = params[0:5]
    token_rows, width = inputs.shape
    head_size = width // HEADS
    scale = head_size ** (-0.5)
    queries = (product(inputs, query_mat) + query_vec).astype(jnp.bfloat16)
    keys = product(inputs, key_mat).astype(jnp.bfloat16)
    values = (product(inputs, value_mat) + value_vec).astype(jnp.bfloat16)
    block_rows = min(512, token_rows)

    def one_block(first_row):
        allowed = labels[:, None] == labels[None, :]

        def one_head(head_index):
            head_queries = lax.dynamic_slice_in_dim(queries, head_index * head_size, head_size, 1)
            head_keys = lax.dynamic_slice_in_dim(keys, head_index * head_size, head_size, 1)
            head_values = lax.dynamic_slice_in_dim(values, head_index * head_size, head_size, 1)
            scores = jnp.where(allowed, product_nt(head_queries, head_keys) * scale, MASKED)
            highest = jnp.max(scores, -1, keepdims=True)
            powers = jnp.exp(scores - highest)
            totals = jnp.sum(powers, -1, keepdims=True)
            shares = (powers / totals).astype(jnp.bfloat16)
            return (product(shares, head_values), (highest + jnp.log(totals))[:, 0])

        head_out, head_lse = lax.map(one_head, jnp.arange(HEADS, dtype=jnp.int32))
        attended = (
            jnp.transpose(head_out, (1, 0, 2)).reshape(block_rows, width).astype(jnp.bfloat16)
        )
        result, unused = tail(inputs, attended, params)
        shown = jnp.where(valid[:, None], result, 0.0).astype(jnp.bfloat16)
        return (attended, head_lse, shown)

    firsts = jnp.arange(token_rows // block_rows, dtype=jnp.int32) * block_rows
    attended, lse_blocks, shown = lax.map(one_block, firsts)
    attended = attended.reshape(token_rows, width)
    shown = shown.reshape(token_rows, width)
    lse_all = jnp.transpose(lse_blocks, (1, 0, 2)).reshape(HEADS, token_rows)
    return ((queries, keys, values, attended, lse_all), shown)


def backward(inputs, labels, cotangent, starts, live, saved, params):
    queries, keys, values, attended, lse_all = saved
    query_mat, key_mat, value_mat, out_mat = (params[0], params[2], params[3], params[5])
    gain_one, inner_mat, outer_mat, gain_two = (params[7], params[9], params[11], params[13])
    token_rows, width = inputs.shape
    head_size = width // HEADS
    scale = head_size ** (-0.5)
    slot_count = starts.shape[0]
    row_inputs = inputs[starts]
    row_attended = attended[starts]
    unused, kept = tail(row_inputs, row_attended, params)
    normed_one, inverse_one, hidden_low, inner, active, normed_two, inverse_two = kept
    upstream = jnp.where(live[:, None], cotangent, 0.0)
    grad_sum_two, grad_gain_two, grad_shift_two = normalize_back(
        upstream, normed_two, inverse_two, gain_two
    )
    grad_outer = grad_sum_two.astype(jnp.bfloat16)
    grad_outer_mat = product_tn(active, grad_outer)
    grad_outer_vec = jnp.sum(grad_outer.astype(jnp.float32), 0)
    grad_inner = (product_nt(grad_outer, outer_mat) * gelu_slope(inner)).astype(jnp.bfloat16)
    grad_inner_mat = product_tn(hidden_low, grad_inner)
    grad_inner_vec = jnp.sum(grad_inner.astype(jnp.float32), 0)
    grad_hidden = grad_sum_two + product_nt(grad_inner, inner_mat)
    grad_sum_one, grad_gain_one, grad_shift_one = normalize_back(
        grad_hidden, normed_one, inverse_one, gain_one
    )
    grad_branch = grad_sum_one.astype(jnp.bfloat16)
    grad_out_mat = product_tn(row_attended, grad_branch)
    grad_out_vec = jnp.sum(grad_branch.astype(jnp.float32), 0)
    grad_attended = (
        product_nt(grad_branch, out_mat).astype(jnp.bfloat16).reshape(slot_count, HEADS, head_size)
    )
    row_queries = queries[starts].reshape(slot_count, HEADS, head_size)
    keys_split = keys.reshape(token_rows, HEADS, head_size)
    values_split = values.reshape(token_rows, HEADS, head_size)
    allowed = labels[starts][None, :, None] == labels[None, None, :]
    scores = (
        jnp.einsum("rhd,thd->hrt", row_queries, keys_split, preferred_element_type=jnp.float32)
        * scale
    )
    shares = jnp.where(allowed, jnp.exp(scores - lse_all[:, starts][:, :, None]), 0.0)
    shares_low = shares.astype(jnp.bfloat16)
    grad_shares = jnp.einsum(
        "rhd,thd->hrt", grad_attended, values_split, preferred_element_type=jnp.float32
    )
    grad_scores = (
        shares * (grad_shares - jnp.sum(grad_shares * shares, -1, keepdims=True))
    ).astype(jnp.bfloat16)
    grad_queries = (
        jnp.einsum("hrt,thd->rhd", grad_scores, keys_split, preferred_element_type=jnp.float32)
        * scale
    )
    grad_queries = grad_queries.reshape(slot_count, width).astype(jnp.bfloat16)
    grad_keys = (
        jnp.einsum("hrt,rhd->thd", grad_scores, row_queries, preferred_element_type=jnp.float32)
        * scale
    )
    grad_keys = grad_keys.reshape(token_rows, width).astype(jnp.bfloat16)
    grad_values = jnp.einsum(
        "hrt,rhd->thd", shares_low, grad_attended, preferred_element_type=jnp.float32
    )
    grad_values = grad_values.reshape(token_rows, width).astype(jnp.bfloat16)
    grad_inputs = product_nt(grad_keys, key_mat) + product_nt(grad_values, value_mat)
    grad_inputs = grad_inputs.at[starts].add(product_nt(grad_queries, query_mat) + grad_sum_one)
    grads = (
        product_tn(row_inputs, grad_queries),
        jnp.sum(grad_queries.astype(jnp.float32), 0),
        product_tn(inputs, grad_keys),
        product_tn(inputs, grad_values),
        jnp.sum(grad_values.astype(jnp.float32), 0),
        grad_out_mat,
        grad_out_vec,
        grad_gain_one,
        grad_shift_one,
        grad_inner_mat,
        grad_inner_vec,
        grad_outer_mat,
        grad_outer_vec,
        grad_gain_two,
        grad_shift_two,
    )
    return (grad_inputs.astype(jnp.bfloat16), grads)


def cast_params(gathered):
    vector_places = (1, 4, 6, 7, 8, 10, 12, 13, 14)
    return tuple(
        (
            item.astype(jnp.float32) if place in vector_places else item
            for place, item in enumerate(gathered)
        )
    )


def split_halves(grads, side):
    keep_list = []
    give_list = []
    for item in grads:
        half = item.shape[0] // 2
        keep_list.append(lax.dynamic_slice_in_dim(item, side * half, half, 0))
        give_list.append(lax.dynamic_slice_in_dim(item, (1 - side) * half, half, 0))
    return (tuple(keep_list), tuple(give_list))


MESH = pl.DeviceIdType.MESH
BLOCK = 40
QS, PS, STREAM, WIDTH, FF, MICRO = 17, 2, 512, 768, 3072, 2
ROWS = MICRO * STREAM
CLS = 16 * BLOCK
HALF = 1280
PART = (HALF, 1152, 768)
FIRST = (0, 2560, 4864)
CHUNKS = (
    (0, 0, 640, 256, 384), (0, 640, 640, 256, 384), (1, 0, 768, 256, 512), (1, 768, 384, 128, 256), (2, 0, 768, 256, 512),
    (3, 0, 48, 16, 32), (3, 48, 48, 16, 32),
)
SHORT = (0, 1, 6)
EARLY = (5,)
SLOTS = 40 * len(CHUNKS)
OWN = 24
PIECE = 256
FF_OWN = 96
BF, F32 = jnp.bfloat16, jnp.float32
OFF = ()
RATE = (3, 4, 0.5, 1.5, 1, (6, 6, 6, 6, 6))
START = (0, 0, 1, 2, 3, 4, 5)
LEAD = 2


class Place:
    def __init__(self):
        self.x = lax.axis_index("tower")
        self.batch = lax.axis_index("batch")
        self.core = self.batch % 2
        self.y = (self.batch // 2) % 2
        self.z = self.batch // 4
        self.index = self.x * 16 + self.batch

    def device(self, x=None, y=None, z=None, core=None):
        x = self.x if x is None else x
        y = self.y if y is None else y
        z = self.z if z is None else z
        core = self.core if core is None else core
        return (x, z * 4 + y * 2 + core)

    def chip(self, x=None, y=None, z=None):
        x = self.x if x is None else x
        y = self.y if y is None else y
        z = self.z if z is None else z
        return x * 8 + z * 2 + y

    def layer(self, step):
        if step == 0:
            return self.z
        if step == 1:
            return self.z + 1 - 2 * (self.z % 2)
        if step == 2:
            return (self.z + 2) % 4
        return 3 - self.z

    @property
    def sibling(self):
        return self.device(core=1 - self.core)

    @property
    def over_x(self):
        return self.device(x=1 - self.x)

    @property
    def over_y(self):
        return self.device(y=1 - self.y)


def greet(place):
    barrier = pltpu.get_barrier_semaphore()
    peers = [place.device(z=place.layer(step)) for step in (1, 2, 3)]
    peers += [place.over_x, place.over_y, place.sibling]
    for peer in peers:
        pl.semaphore_signal(barrier, inc=1, device_id=peer, device_id_type=MESH)
    return lambda: pl.semaphore_wait(barrier, len(peers))


class Sender:
    def __init__(self, place, send_sems, recv_sems):
        self.place = place
        self.send_sems = send_sems
        self.recv_sems = recv_sems
        self.used = 0
        self.open = []

    def send(self, src, dst, slot, peer, only=None):
        copy = pltpu.make_async_remote_copy(
            src_ref=src,
            dst_ref=dst,
            send_sem=self.send_sems.at[self.used],
            recv_sem=self.recv_sems.at[slot],
            device_id=peer,
            device_id_type=MESH,
        )
        self.used += 1
        if only is None:
            copy.start()
        else:
            pl.when(only)(copy.start)
        self.open.append((copy, only))

    def arrived(self, dst, slot):
        pltpu.make_async_remote_copy(
            src_ref=dst,
            dst_ref=dst,
            send_sem=self.send_sems.at[0],
            recv_sem=self.recv_sems.at[slot],
            device_id=self.place.sibling,
            device_id_type=MESH,
        ).wait_recv()

    def close(self):
        for copy, only in self.open:
            if only is None:
                copy.wait_send()
            else:
                pl.when(only)(copy.wait_send)
        self.open = []


def tile(index, size, unit):
    return pl.ds(pl.multiple_of(index * unit, unit), size)


def loop(count, body):
    if getattr(body, '__name__', '') in OFF or 'all' in OFF:
        return
    def step(index, carry):
        body(index)
        return carry

    lax.fori_loop(0, count, step, 0)


def shifted(body, by):
    def moved(index):
        body(index + by)
    moved.__name__ = body.__name__
    return moved


def dot(left, right):
    return jnp.dot(left, right, preferred_element_type=F32)


def dot_nt(left, right):
    return lax.dot_general(left, right, (((1,), (1,)), ((), ())), preferred_element_type=F32)


def dot_tn(left, right):
    return lax.dot_general(left, right, (((0,), (0,)), ((), ())), preferred_element_type=F32)


def iota(shape, dim):
    return lax.broadcasted_iota(jnp.int32, shape, dim)


def centre(values):
    average = jnp.mean(values, -1, keepdims=True)
    centred = values - average
    inverse = lax.rsqrt(jnp.mean(centred * centred, -1, keepdims=True) + EPSILON)
    return centred * inverse, inverse


def centre_back(scaled, normed, inverse):
    return inverse * (
        scaled - jnp.mean(scaled, -1, keepdims=True) - normed * jnp.mean(scaled * normed, -1, keepdims=True)
    )


def weight_steps(place, sender, all_wide, all_tall):
    middle = (place.z == 1) | (place.z == 2)

    def view(chunk, core, chip, start=0, stop=None):
        part, offset, size, unused, unused = CHUNKS[chunk]
        size = (size if stop is None else stop) - start
        if part < 3:
            first = pl.multiple_of(FIRST[part] + core * PART[part] + offset + start, 128)
            return all_wide.at[tile(chip, 2 * OWN, 2 * OWN), pl.ds(first, size)]
        first = pl.multiple_of((chip * 2 + core) * FF_OWN + offset + start, 16)
        return all_tall.at[pl.ds(first, size), :]

    def slot(chunk, kind, layer):
        return (chunk * 10 + kind) * 4 + layer

    def along_z(chunk, block, at):
        sender.send(block, block, at, place.device(z=place.layer(1)))
        sender.send(block, block, at, place.device(z=place.layer(2)))
        sender.send(block, block, at, place.device(z=place.layer(3)), only=None if chunk in SHORT else middle)

    def begin_across(chunk):
        own = view(chunk, place.core, place.chip())
        sender.send(own, own, slot(chunk, 1, place.z), place.over_x)
        sender.send(own, own, slot(chunk, 2, place.z), place.over_y)
        sender.send(own, own, slot(chunk, 5, place.z), place.sibling)

    def begin(chunk):
        own = view(chunk, place.core, place.chip())
        along_z(chunk, own, slot(chunk, 0, place.z))
        if chunk not in EARLY:
            begin_across(chunk)

    def along(chunk, step):
        layer = place.layer(step)
        block = view(chunk, place.core, place.chip(z=layer))
        sender.arrived(block, slot(chunk, 0, layer))
        if step == 2 and chunk not in SHORT:
            sender.send(block, block, slot(chunk, 0, layer), place.device(z=place.layer(1)), only=middle)
        sender.send(block, block, slot(chunk, 1, layer), place.over_x)
        sender.send(block, block, slot(chunk, 2, layer), place.over_y)
        sender.send(block, block, slot(chunk, 5, layer), place.sibling)

    def across(chunk, step):
        layer = place.layer(step)
        chip_x, chip_y = place.chip(x=1 - place.x, z=layer), place.chip(y=1 - place.y, z=layer)
        short = chunk in SHORT
        first, second = CHUNKS[chunk][3:]
        from_x, from_y = view(chunk, place.core, chip_x), view(chunk, place.core, chip_y)
        sender.arrived(from_x, slot(chunk, 1, layer))
        if step < (2 if short else 1):
            piece = from_x if short else view(chunk, place.core, chip_x, 0, second if step == 0 else first)
            sender.send(piece, piece, slot(chunk, 3, layer), place.over_y)
        sender.send(from_x, from_x, slot(chunk, 6, layer), place.sibling)
        sender.arrived(from_y, slot(chunk, 2, layer))
        if step >= (2 if short else 1):
            piece = from_y if short else view(chunk, place.core, chip_y, 0, first)
            sender.send(piece, piece, slot(chunk, 3, layer), place.over_x)
        if step == 0 and not short:
            piece = view(chunk, place.core, chip_y, second)
            sender.send(piece, piece, slot(chunk, 4, layer), place.over_x)
        sender.send(from_y, from_y, slot(chunk, 7, layer), place.sibling)

    def far(layer):
        return place.chip(x=1 - place.x, y=1 - place.y, z=layer)

    def corner(chunk):
        first, second = CHUNKS[chunk][3:]
        sender.arrived(view(chunk, place.core, far(place.z), 0, second), slot(chunk, 3, place.z))
        sender.arrived(view(chunk, place.core, far(place.z), second), slot(chunk, 4, place.z))
        rest = view(chunk, place.core, far(place.z), first)
        along_z(chunk, rest, slot(chunk, 4, place.z))
        block = view(chunk, place.core, far(place.z))
        sender.send(block, block, slot(chunk, 8, place.z), place.sibling)

    def corner_along(chunk, step):
        layer = place.layer(step)
        rest = view(chunk, place.core, far(layer), CHUNKS[chunk][3])
        sender.arrived(rest, slot(chunk, 4, layer))
        if step == 2:
            sender.send(rest, rest, slot(chunk, 4, layer), place.device(z=place.layer(1)), only=middle)
        sender.send(rest, rest, slot(chunk, 9, layer), place.sibling)

    def corner_third(chunk, step):
        layer = place.layer(step)
        piece = view(chunk, place.core, far(layer), 0, None if chunk in SHORT else CHUNKS[chunk][3])
        sender.arrived(piece, slot(chunk, 3, layer))
        sender.send(piece, piece, slot(chunk, 8, layer), place.sibling)

    def twin(chunk):
        core = 1 - place.core
        for step in range(4):
            layer = place.layer(step)
            sender.arrived(view(chunk, core, place.chip(z=layer)), slot(chunk, 5, layer))
            sender.arrived(view(chunk, core, place.chip(x=1 - place.x, z=layer)), slot(chunk, 6, layer))
            sender.arrived(view(chunk, core, place.chip(y=1 - place.y, z=layer)), slot(chunk, 7, layer))
            if step == 0 or chunk in SHORT:
                sender.arrived(view(chunk, core, far(layer)), slot(chunk, 8, layer))
            else:
                sender.arrived(view(chunk, core, far(layer), 0, CHUNKS[chunk][3]), slot(chunk, 8, layer))
                sender.arrived(view(chunk, core, far(layer), CHUNKS[chunk][3]), slot(chunk, 9, layer))

    def steps():
        usual = (
            (5, twin, (None,)), (4, corner_along, (3,)), (3, corner_along, (1, 2)), (3, corner_third, (3,)),
            (2, corner, (None,)), (2, corner_third, (1, 2)), (2, across, (3,)), (1, across, (0, 1, 2)),
            (1, along, (3,)), (0, along, (1, 2)),
        )
        short = ((3, twin, (None,)), (2, corner_third, (0, 1, 2, 3)), (1, across, (0, 1, 2, 3)), (0, along, (1, 2, 3)))
        count = len(CHUNKS)
        for turn in range(START[-1] + 6):
            for chunk in range(count):
                for late, stage, places in short if chunk in SHORT else usual:
                    if START[chunk] == turn - late:
                        for step in places:
                            if step is None:
                                stage(chunk)
                            else:
                                stage(chunk, step)
                            yield chunk if stage is twin else None
            for chunk in range(count):
                if START[chunk] == turn + LEAD:
                    begin(chunk)

    return begin, begin_across, steps


def cls_steps(place, sender, base, block_ref, merged, stage, out_ref):
    rows, half = 2 * BLOCK, WIDTH // 2
    mine = tile(place.core, half, half)
    other = tile(1 - place.core, half, half)

    def view(core, y, z):
        return out_ref.at[tile(z * 2 + y, rows, rows), tile(core, half, half)]

    sender.send(block_ref.at[:, other], stage.at[0], base, place.sibling)
    yield
    sender.arrived(stage.at[0], base)
    merged[...] = (block_ref[:, mine].astype(F32) + stage[0].astype(F32)).astype(BF)
    sender.send(merged, stage.at[1], base + 1, place.over_x)
    yield
    sender.arrived(stage.at[1], base + 1)
    own = view(place.core, place.y, place.z)
    own[...] = (merged[...].astype(F32) + stage[1].astype(F32)).astype(BF)
    middle = (place.z == 1) | (place.z == 2)
    sender.send(own, own, base + 2 + place.z, place.device(z=place.layer(2)))
    sender.send(own, own, base + 2 + place.z, place.device(z=place.layer(3)), only=middle)
    sender.send(own, own, base + 2 + place.z, place.device(z=place.layer(1)))
    for step in (0, 2, 1, 3):
        layer = place.layer(step)
        block = view(place.core, place.y, layer)
        if step > 0:
            yield
            sender.arrived(block, base + 2 + layer)
        if step == 2:
            sender.send(block, block, base + 2 + layer, place.device(z=place.layer(1)), only=middle)
        sender.send(block, block, base + 6 + layer, place.over_y)
        sender.send(block, block, base + 10 + layer, place.sibling)
    for step in (0, 2, 1, 3):
        yield
        layer = place.layer(step)
        block = view(place.core, 1 - place.y, layer)
        sender.arrived(block, base + 6 + layer)
        sender.send(block, block, base + 14 + layer, place.sibling)
    yield
    for step in range(4):
        layer = place.layer(step)
        sender.arrived(view(1 - place.core, place.y, layer), base + 10 + layer)
        sender.arrived(view(1 - place.core, 1 - place.y, layer), base + 14 + layer)


def sum_begin(place, sender, base, part_ref, stage_core, first, last):
    other = tile(1 - place.core, HALF, HALF)
    for chip in range(first, last):
        sender.send(part_ref.at[pl.ds(2 * OWN * chip, 2 * OWN), other], stage_core.at[chip], base + chip, place.sibling)


def sum_steps(place, sender, base, part_ref, work, stage_core, stage_pair, stage_z, final, stage_last, out_ref):
    mine = tile(place.core, HALF, HALF)
    other = tile(1 - place.core, HALF, HALF)
    order = (3, 2, 1, 0)
    blocks = [(dx, dy, step) for step in order for dx, dy in ((1, 1), (1, 0), (0, 1), (0, 0))]

    def x_first(step):
        return step % 2 == 0

    def chip_of(dx, dy, step):
        return place.chip(1 - place.x if dx else place.x, 1 - place.y if dy else place.y, place.layer(step))

    def add(index, landed):
        work[index] = (work[index].astype(F32) + landed.astype(F32)).astype(BF)

    for index, at in enumerate(blocks):
        if index % 4 == 0:
            yield
        dx, dy, step = at
        chip = chip_of(*at)
        sender.arrived(stage_core.at[chip], base + chip)
        work[index] = (part_ref[tile(chip, 2 * OWN, 2 * OWN), mine].astype(F32) + stage_core[chip].astype(F32)).astype(BF)
        if (dx if x_first(step) else dy) == 1:
            peer = place.over_x if x_first(step) else place.over_y
            sender.send(work.at[index], stage_pair.at[index], base + 16 + index, peer)

    def first_add(step):
        for second in (1, 0):
            keep = (0, second) if x_first(step) else (second, 0)
            sent = (1, second) if x_first(step) else (second, 1)
            index, source = blocks.index(keep + (step,)), blocks.index(sent + (step,))
            sender.arrived(stage_pair.at[source], base + 16 + source)
            add(index, stage_pair[source])
            if second:
                peer = place.over_y if x_first(step) else place.over_x
                sender.send(work.at[index], stage_pair.at[index], base + 32 + index, peer)

    def second_add(step):
        index = blocks.index((0, 0, step))
        source = blocks.index(((0, 1) if x_first(step) else (1, 0)) + (step,))
        sender.arrived(stage_pair.at[source], base + 32 + source)
        add(index, stage_pair[source])
        if step:
            sender.send(work.at[index], stage_z.at[step], base + 48 + step, place.device(z=place.layer(step)))

    yield
    first_add(3)
    yield
    first_add(2)
    yield
    second_add(3)
    yield
    first_add(1)
    yield
    second_add(2)
    yield
    first_add(0)
    yield
    second_add(1)
    yield
    second_add(0)
    yield
    total = work[blocks.index((0, 0, 0))].astype(F32)
    for step in (3, 2, 1):
        sender.arrived(stage_z.at[step], base + 48 + step)
        total = total + stage_z[step].astype(F32)
    top, low = total[:OWN], total[OWN:]
    is_first = place.core == 0
    final[...] = jnp.where(is_first, low, top)
    sender.send(final, stage_last, base + 52, place.sibling)
    out_ref[:, mine] = jnp.where(is_first, top, low)
    yield
    sender.arrived(stage_last, base + 52)
    out_ref[:, other] = stage_last[...]


def weave(units, *steps):
    for index, unit in enumerate(units):
        unit()
        for generator, count in steps:
            run(generator, int((index + 1) * count) - int(index * count))


def run_to(steps, chunk):
    for done in steps:
        if done == chunk:
            return


def run(steps, count=None):
    while count is None or count > 0:
        if next(steps, "end") == "end":
            return
        if count is not None:
            count -= 1


def layer_kernel(
    x_ref, bq_ref, bv_ref, bo_ref, g1_in, s1_in, b2_ref, g2_in, s2_in, b1_ref, wq_ref, wk_ref, wv_ref, wo_ref, w1_ref, w2_ref, qlen_ref, plen_ref, pos_ref,
    hidden_out, igrad_out, qw_ref, qb_ref, kw_ref, vw_ref, vb_ref, ow_ref, ob_ref, g1_ref, s1_ref, iw_ref, ib_ref,
    tw_ref, tb_ref, g2_ref, s2_ref,
    hidden_ref, igrad_ref, lines_s, wide, stage, wa, wb, vecs, b1, q_s, k_s, v_s, bias, sel, code,
    block, merged, cls_stage, cls, att_block, att_merged, att_stage, cls_att, n1, columns, h_low, slope, act, n2, d_out, d_branch, sums, sums_b1,
    q_rows, x_rows, att_rows, dq, dkv, part, work, stage_core, stage_pair, stage_z, final, stage_last, summed,
    send_sems, cls_sems, recv_sems, out_sems,
):
    place = Place()
    sender = Sender(place, send_sems, recv_sems)
    cls_sender = Sender(place, cls_sems, recv_sems)
    is_query = place.x == 0
    core = place.core
    scr = n1.at[pl.ds(0, STREAM), :]
    window = n1.at[pl.ds(0, 256), :]

    all_here = greet(place)

    cut = WIDTH // 2
    lines_s[...] = jnp.zeros_like(lines_s)
    for i, ref in enumerate((bq_ref, bv_ref, bo_ref, g1_in, s1_in, b2_ref, g2_in, s2_in)):
        lines_s[pl.ds(i, 1), pl.ds(0, OWN)] = ref[...].astype(F32).reshape(1, OWN)
    lines_s[pl.ds(16, 1), pl.ds(0, FF_OWN)] = b1_ref[...].astype(F32).reshape(1, FF_OWN)
    long_line = jnp.broadcast_to(lines_s[pl.ds(16, 1), :], (8, 128))
    for i in range(4):
        turned = long_line if i == 0 else pltpu.roll(long_line, 128 - OWN * i, 1)
        lines_s[pl.ds(8 + i, 1), :] = turned[:1, :]
    vec_cols = lines_s[...].T[:OWN, :].astype(BF)
    filled = (
        (wq_ref, 0, WIDTH, 0), (wv_ref, 0, cut, 768), (wk_ref, 0, WIDTH, 1280), (wv_ref, cut, cut, 2048),
        (wo_ref, 0, WIDTH, 2560), (w1_ref, 0, FF, 3328),
    )
    for at in (1152, 2432):
        wide[:, pl.ds(at, 128)] = jnp.zeros((32, 128), BF)
    for ref, start, size, at in filled:
        wide[pl.ds(0, OWN), pl.ds(at, size)] = ref[:, pl.ds(start, size)]
        wide[pl.ds(OWN, 8), pl.ds(at, size)] = jnp.zeros((8, size), BF)
    wide[pl.ds(0, OWN), pl.ds(1152, 128)] = vec_cols
    all_here()

    begin, begin_across, weight_parts = weight_steps(place, sender, wa, wb)
    offsets = (0, HALF, HALF + PART[1])
    for chunk in range(3):
        first = pl.multiple_of(FIRST[chunk] + (1 - core) * PART[chunk], 128)
        landing = stage.at[:, pl.ds(offsets[chunk], PART[chunk])]
        sender.send(wide.at[:, pl.ds(first, PART[chunk])], landing, SLOTS + chunk, place.sibling)
    wb[tile(place.index, FF_OWN, FF_OWN), :] = w2_ref[...]
    for chunk in EARLY:
        begin_across(chunk)

    def assemble(chunk):
        sender.arrived(stage.at[:, pl.ds(offsets[chunk], PART[chunk])], SLOTS + chunk)
        first = pl.multiple_of(FIRST[chunk] + core * PART[chunk], 128)
        mine = wide[pl.ds(0, OWN), pl.ds(first, PART[chunk])].astype(F32)
        other = stage[pl.ds(0, OWN), pl.ds(offsets[chunk], PART[chunk])].astype(F32)
        top, low = jnp.where(core == 0, mine, other), jnp.where(core == 0, other, mine)
        wa[tile(place.chip(), 2 * OWN, 2 * OWN), pl.ds(first, PART[chunk])] = jnp.concatenate([top, low], 0).astype(BF)

    assemble(0)
    for chunk in range(len(CHUNKS)):
        if START[chunk] == 0:
            begin(chunk)
    assemble(1)
    assemble(2)
    for chunk in range(len(CHUNKS)):
        if 0 < START[chunk] < LEAD:
            begin(chunk)

    ends, starts = [], []
    for m in range(MICRO):
        end = jnp.int32(0)
        ends.append([])
        starts.append([])
        for i in range(QS):
            length = jnp.where(is_query, qlen_ref[m, i], plen_ref[m, i] if i < PS else 0)
            starts[m].append(end)
            end = end + length
            ends[m].append(end)
    def cls_places(rows, offset):
        at = iota((rows, 128), 0)
        found = jnp.full((rows, 128), -1, jnp.int32)
        label = jnp.full((rows, 128), -1, jnp.int32)
        for m in range(MICRO):
            for i in range(QS):
                row = jnp.where(is_query, QS * m + i, MICRO * QS + PS * m + i if i < PS else -1000) + offset
                found = jnp.where(at == row, m * STREAM + starts[m][i], found)
                label = jnp.where(at == row, m * 64 + i, label)
        return found[:, :1], label[:, :1]

    found, label = cls_places(BLOCK, 0)
    sel[...] = (found == iota((BLOCK, ROWS), 1)).astype(BF)
    ours = label >= 0
    low_lanes = iota((BLOCK, 128), 1) < 64
    coded = jnp.zeros((BLOCK, 128), jnp.int32)
    at_row, at_lane = iota((BLOCK, 128), 0), iota((BLOCK, 128), 1)
    for m in range(MICRO):
        for i in range(QS):
            here = (at_row == jnp.where(is_query, -1000, BLOCK - MICRO + m)) & (at_lane == i)
            coded = jnp.where(here, pos_ref[m, i], coded)
    coded = coded.astype(F32)

    def both(rows):
        return jnp.concatenate([jnp.where(low_lanes, rows, 0.0), jnp.where(low_lanes, 0.0, rows)], 0).astype(BF)

    def for_chip(rows):
        nothing = jnp.zeros_like(rows)
        return jnp.concatenate([jnp.where(core == 0, rows, nothing), jnp.where(core == 0, nothing, rows)], 0).astype(BF)

    x_rows[...] = dot(sel[...], x_ref[...])
    block[...] = for_chip(x_rows[...])
    block[:, pl.ds(0, 128)] = for_chip(x_rows[:, pl.ds(0, 128)] + coded)
    x_parts = cls_steps(place, cls_sender, SLOTS + 3, block, merged, cls_stage, cls)
    run(x_parts, 1)
    weights = weight_parts()

    row_of_key = iota((8, STREAM), 1)
    row_of_query = iota((STREAM, 128), 0)
    for m in range(MICRO):
        key_label = jnp.zeros((8, STREAM), jnp.int32)
        query_label = jnp.zeros((STREAM, 128), jnp.int32)
        for end in ends[m]:
            key_label += (row_of_key >= end).astype(jnp.int32)
            query_label += (row_of_query >= end).astype(jnp.int32)
        code[:, pl.ds(m * STREAM, STREAM)] = key_label + m * 64
        same = query_label[:, :1] == key_label[:1, :]
        bias[pl.ds(m * STREAM, STREAM), :] = jnp.where(same, 0.0, MASKED).astype(BF)

    seen = (label == code[pl.ds(0, 1), :]).astype(F32)
    seen2 = jnp.concatenate([seen, seen], 0) > 0.5
    for count in RATE[5]:
        run(x_parts, 1)
        run(weights, count)
    run_to(weights, 1)

    vecs[...] = wa[:, pl.ds(1152, 128)].astype(F32).T[:16, :]
    low_at, out_at = iota((FF_OWN, 384), 0), iota((FF_OWN, 384), 1)
    spread = jnp.zeros((FF_OWN, 384), jnp.bool_)
    row8, lane8 = iota((8, 384), 0), iota((8, 384), 1)
    pick = jnp.zeros((8, 384), jnp.bool_)
    for a in range(4):
        pick |= (lane8 >= 96 * a + 24 * row8) & (lane8 < 96 * a + 24 * row8 + 24) & (row8 < 4)
        for j in range(4):
            spread |= (low_at >= 24 * a) & (low_at < 24 * a + 24) & (out_at - low_at == 72 * a + 24 * j)
    spread = spread.astype(BF)
    for t in range(8):
        found_b1 = dot_tn(wa[pl.ds(FF_OWN * t, FF_OWN), pl.ds(1152, 128)], spread)
        b1[:, pl.ds(384 * t, 384)] = jnp.sum(jnp.where(pick, found_b1[8:16], 0.0), 0, keepdims=True)

    def vec(i):
        return vecs[pl.ds(i, 1), :]

    def project_q(i):
        rows = tile(i, 512, 512)
        xb = x_ref[rows, :]
        q_s[rows, :] = ((dot(xb, wa[:, pl.ds(0, WIDTH)]) + vec(0)).astype(BF).astype(F32) * 0.125).astype(BF)

    def project_k(i):
        rows = tile(i, 512, 512)
        k_s[rows, :] = dot(x_ref[rows, :], wa[:, pl.ds(HALF, WIDTH)]).astype(BF)

    def project_v(i):
        rows = tile(i, 512, 512)
        xb = x_ref[rows, :]
        v_s[rows, pl.ds(0, cut)] = (dot(xb, wa[:, pl.ds(WIDTH, cut)]) + vecs[pl.ds(1, 1), pl.ds(0, cut)]).astype(BF)
        v_s[rows, pl.ds(cut, cut)] = (
            dot(xb, wa[:, pl.ds(HALF + WIDTH, cut)]) + vecs[pl.ds(1, 1), pl.ds(cut, cut)]
        ).astype(BF)

    run(weights, 1)
    weave([functools.partial(loop, 1, shifted(f, i)) for f in (project_q, project_k, project_v) for i in range(2)], (weights, RATE[3]), (x_parts, 0.5))

    q_rows[...] = dot(sel[...], q_s[...])

    def own_shares(pair):
        cols = pl.ds(128 * pair, 128) if isinstance(pair, int) else tile(pair, 128, 128)
        q2 = both(q_rows[:, cols])
        scores = jnp.where(seen2, dot_nt(q2, k_s[:, cols]), MASKED)
        powers = jnp.where(seen2, jnp.exp(scores - jnp.max(scores, -1, keepdims=True)), 0.0)
        total = jnp.sum(powers, -1, keepdims=True)
        return q2, powers * (1.0 / jnp.where(total > 0, total, 1.0))

    def own_attend(pair):
        cols = pl.ds(128 * pair, 128)
        unused, shares = own_shares(pair)
        out = dot(shares.astype(BF), v_s[:, cols])
        att_rows[:, cols] = jnp.where(low_lanes, out[:BLOCK], out[BLOCK:])

    weave([functools.partial(own_attend, pair) for pair in range(6)], (weights, RATE[4]), (x_parts, 0.5))
    run(x_parts)

    att_block[...] = for_chip(jnp.where(ours, att_rows[...], 0.0))
    cls_parts = cls_steps(place, sender, SLOTS + 21, att_block, att_merged, att_stage, cls_att)
    run(cls_parts, 1)

    def attend(pair, m):
        cols = pl.ds(128 * pair, 128)
        keys = pl.ds(m * STREAM, STREAM)
        k2, v2 = k_s[keys, cols], v_s[keys, cols].astype(F32)
        low_keys = iota((STREAM, 128), 1) < 64
        values = jnp.concatenate([jnp.where(low_keys, v2, 1.0), jnp.where(low_keys, 1.0, v2)], 1).astype(BF)
        low = iota((256, 128), 1) < 64
        for i in range(2):
            rows = pl.ds(m * STREAM + 256 * i, 256)
            q2 = q_s[rows, cols].astype(F32)
            heads = jnp.concatenate([jnp.where(low, q2, 0.0), jnp.where(low, 0.0, q2)], 0).astype(BF)
            scores = dot_nt(heads, k2)
            masked = bias[rows, :].astype(F32)
            powers = []
            for head in range(2):
                part_scores = scores[256 * head : 256 * head + 256] + masked
                powers.append(jnp.exp(part_scores - jnp.max(part_scores, -1, keepdims=True)).astype(BF))
            out = dot(jnp.concatenate(powers, 0), values)
            first, second = out[:256, :128], out[256:, 128:]
            sums_of = pltpu.roll(jnp.where(low, second, first), 64, 1)
            igrad_ref[rows, cols] = (jnp.where(low, first, second) * (1.0 / sums_of)).astype(BF)

    weave(
        [functools.partial(attend, pair, m) for pair in range(6) for m in range(MICRO)], (cls_parts, 1), (weights, RATE[0])
    )
    run(cls_parts)

    def cls_first(i):
        rows = tile(i, CLS, CLS)
        at = iota((CLS, 1), 0) + i * CLS
        group = jnp.zeros((CLS, 1), jnp.int32)
        for b in range(1, 16):
            group += (at >= BLOCK * b).astype(jnp.int32)
        xin = jnp.where(at - BLOCK * group < BLOCK - MICRO, cls[rows, :].astype(F32), 0.0)
        normed, inverse = centre(xin + (dot(cls_att[rows, :], wa[:, pl.ds(2560, WIDTH)]) + vec(2)))
        n1[rows, :] = normed
        columns[rows, pl.ds(0, 1)] = inverse
        h_low[rows, :] = (normed * vec(3) + vec(4)).astype(BF)

    run_to(weights, 2)
    loop(1, cls_first)
    run(weights, 1)

    at = iota((CLS, 1), 0)
    at_col = iota((1, CLS), 1)

    def kinds(index):
        group = jnp.zeros(index.shape, jnp.int32)
        for b in range(1, 16):
            group += (index >= BLOCK * b).astype(jnp.int32)
        inner = index - BLOCK * group
        query_m = (inner >= QS).astype(jnp.int32)
        is_q = inner < MICRO * QS
        passage_m = (inner >= MICRO * QS + PS).astype(jnp.int32)
        is_p = (inner >= MICRO * QS) & (inner < MICRO * (QS + PS))
        return group, inner, is_q, query_m, is_p, passage_m

    group, inner, is_q, query_m, unused, unused = kinds(at)
    source = (group * BLOCK + (BLOCK - MICRO) + query_m == at_col).astype(BF)
    codes = dot(source, cls[:, pl.ds(0, 128)])
    wanted = jnp.sum(jnp.where(iota((CLS, 128), 1) == inner - QS * query_m, codes, 0.0), 1, keepdims=True)
    wanted = wanted.astype(jnp.int32)
    target = 2 * wanted - (wanted & 1) + PS * query_m
    columns[:, pl.ds(2, 1)] = target.astype(F32)
    cls_sender.close()
    y_low = cls
    hid_blk = y_low.at[pl.ds(0, STREAM), :]

    def cls_inner(i):
        rows = pl.ds(0, CLS)
        cols = tile(i, 512, 512)
        wcols = pl.ds(pl.multiple_of(3328 + i * 512, 128), 512)
        u = dot(h_low[rows, :], wa[:, wcols]) + b1[:, cols]
        phi = 0.5 * (1.0 + lax.erf(u * 0.7071067811865476))
        act[rows, cols] = (u * phi).astype(BF)
        slope[rows, cols] = (phi + u * jnp.exp(-0.5 * u * u) * 0.3989422804014327).astype(BF)

    weave([functools.partial(loop, 1, shifted(cls_inner, i)) for i in range(3)], (weights, RATE[1]))
    run_to(weights, 4)
    weave([functools.partial(loop, 1, shifted(cls_inner, i)) for i in range(3, 6)], (weights, RATE[1]))
    run_to(weights, 6)

    def cls_second(i):
        rows = tile(i, CLS, CLS)
        r = h_low[rows, :].astype(F32) + (dot(act[rows, :], wb[...]) + vec(5))
        normed, inverse = centre(r)
        n2[rows, :] = normed
        columns[rows, pl.ds(1, 1)] = inverse
        y_low[rows, :] = (normed * vec(6) + vec(7)).astype(BF)

    loop(1, cls_second)

    unused, unused, is_q, query_m, unused, unused = kinds(iota((CLS, 1), 0))
    lane = iota((1, 128), 1)
    paired = is_q & (lane < 16 * MICRO * PS) & (((lane >> 1) & 1) == query_m)
    hit = paired & (columns[:, pl.ds(2, 1)] == lane.astype(F32))
    passage = iota((128, CLS), 0)
    chosen = BLOCK * (passage >> 2) + MICRO * QS + (passage & 3) == iota((128, CLS), 1)
    chosen = (chosen & (passage < 16 * MICRO * PS)).astype(BF)
    y_all = y_low[...]
    y_passages = dot(chosen, y_all).astype(BF)
    logits = jnp.where(paired, dot_nt(y_all, y_passages) * WIDTH ** -0.5, MASKED)
    powers = jnp.where(paired, jnp.exp(logits - jnp.max(logits, -1, keepdims=True)), 0.0)
    total = jnp.sum(powers, -1, keepdims=True)
    shares = powers * (1.0 / jnp.where(is_q, total, 1.0))
    d_logits = ((shares - hit.astype(F32)) * (1.0 / MICRO)).astype(BF)
    d_passages = dot_tn(d_logits, y_all)
    d_high = d_passages.astype(BF)
    d_rest = (d_passages - d_high.astype(F32)).astype(BF)
    d_y = (dot(d_logits, y_passages) + dot_tn(chosen, d_high) + dot_tn(chosen, d_rest)) * WIDTH ** -0.5
    normed = n2[...]
    sums[pl.ds(0, 1), :] = jnp.sum(d_y * normed, 0, keepdims=True)
    sums[pl.ds(1, 1), :] = jnp.sum(d_y, 0, keepdims=True)
    d_sum = centre_back(d_y * vec(6), normed, columns[:, pl.ds(1, 1)])
    n2[...] = d_sum
    d_out[...] = d_sum.astype(BF)
    sums[pl.ds(2, 1), :] = jnp.sum(d_out[...].astype(F32), 0, keepdims=True)

    def cls_inner_back(i):
        cols = tile(i, 512, 512)
        d_act = dot_nt(d_out[...], wb[cols, :])
        d_u = (d_act * slope[:, cols].astype(F32)).astype(BF)
        slope[:, cols] = d_u
        sums_b1[:, cols] = jnp.sum(d_u.astype(F32), 0, keepdims=True)

    loop(6, cls_inner_back)

    def cls_first_back(i):
        rows = tile(i, CLS, CLS)
        d_hidden = n2[rows, :] + dot_nt(slope[rows, :], wa[:, pl.ds(3328, FF)])
        normed = n1[rows, :]
        gains = jnp.sum(d_hidden * normed, 0, keepdims=True)
        shifts = jnp.sum(d_hidden, 0, keepdims=True)
        d_sum = centre_back(d_hidden * vec(3), normed, columns[rows, pl.ds(0, 1)])
        n2[rows, :] = d_sum
        d_low = d_sum.astype(BF)
        d_branch[rows, :] = d_low
        totals = (gains, shifts, jnp.sum(d_low.astype(F32), 0, keepdims=True))
        for place_in, value in enumerate(totals):
            line = pl.ds(3 + place_in, 1)
            sums[line, :] = jnp.where(i == 0, value, sums[line, :] + value)

    loop(1, cls_first_back)

    own_sum = jnp.where(ours, n2[tile(place.batch, BLOCK, BLOCK), :], 0.0)
    d_att = dot_nt(own_sum.astype(BF), wa[:, pl.ds(2560, WIDTH)]).astype(BF).astype(F32)
    att_rows[...] = d_att

    def own_back(pair):
        cols = tile(pair, 128, 128)
        d_a2 = both(att_rows[:, cols])
        k2, v2 = k_s[:, cols], v_s[:, cols]
        q2, shares = own_shares(pair)
        d_shares = dot_nt(d_a2, v2)
        d_scores = (shares * (d_shares - jnp.sum(d_shares * shares, -1, keepdims=True))).astype(BF)
        d_q2 = dot(d_scores, k2)
        dq[:, cols] = (jnp.where(low_lanes, d_q2[:BLOCK], d_q2[BLOCK:]) * 0.125).astype(BF)
        dkv[:, cols] = dot_tn(d_scores, q2).astype(BF)
        dkv[:, pl.ds(pl.multiple_of(WIDTH + 128 * pair, 128), 128)] = dot_tn(shares.astype(BF), d_a2).astype(BF)

    loop(6, own_back)

    part[:, pl.ds(0, WIDTH)] = dot_tn(x_rows[...].astype(BF), dq[...]).astype(BF)

    def project_back(i):
        out = dot_tn(x_ref[:, tile(i, 256, 256)], dkv[...])
        part[tile(i, 256, 256), pl.ds(WIDTH, 2 * WIDTH)] = out.astype(BF)

    line = iota((128, WIDTH), 0)
    q_line = jnp.sum(dq[...].astype(F32), 0, keepdims=True)
    v_line = jnp.sum(dkv[:, pl.ds(WIDTH, WIDTH)].astype(F32), 0, keepdims=True)
    lines = jnp.where(line == 0, q_line, jnp.where(line == 1, v_line, 0.0))
    part[:, pl.ds(3 * WIDTH, 128)] = lines.T.astype(BF)
    part[:, pl.ds(3 * WIDTH + 128, 128)] = jnp.zeros((WIDTH, 128), BF)
    for i, (first, last) in enumerate(((0, 5), (5, 10), (10, 16))):
        loop(1, shifted(project_back, i))
        sum_begin(place, sender, SLOTS + 39, part, stage_core, first, last)

    steps = sum_steps(place, sender, SLOTS + 39, part, work, stage_core, stage_pair, stage_z, final, stage_last, summed)
    run(steps, 5)

    leaving = []

    def leave(src, dst, rows, at):
        copy = pltpu.make_async_copy(src.at[rows, :], dst.at[rows, :], out_sems.at[at])
        copy.start()
        leaving.append(copy)

    def rows_first(i):
        rows = pl.ds(STREAM * i, STREAM)
        branch = dot(igrad_ref[rows, :], wa[:, pl.ds(2560, WIDTH)]) + vec(2)
        normed, unused = centre(x_ref[rows, :].astype(F32) + branch)
        low = (normed * vec(3) + vec(4)).astype(BF)
        hid_blk[...] = low
        scr[...] = low.astype(F32) + vec(5)

    def rows_inner(j):
        cols = tile(j, 512, 512)
        u = dot(hid_blk[...], wa[:, pl.ds(pl.multiple_of(3328 + j * 512, 128), 512)]) + b1[:, cols]
        active = (u * (0.5 * (1.0 + lax.erf(u * 0.7071067811865476)))).astype(BF)
        scr[...] += dot(active, wb[cols, :])

    def rows_second(i):
        normed, unused = centre(scr[...])
        valid = iota((STREAM, 1), 0) < ends[i][QS - 1]
        rows = pl.ds(STREAM * i, STREAM)
        hidden_ref[rows, :] = jnp.where(valid, normed * vec(6) + vec(7), 0.0).astype(BF)
        leave(hidden_ref, hidden_out, rows, i)

    units = []
    for i in range(MICRO):
        units.append(functools.partial(rows_first, i))
        units += [functools.partial(loop, 1, shifted(rows_inner, j)) for j in range(6)]
        units.append(functools.partial(rows_second, i))
    weave(units[:4])
    weave(units[4:], (steps, RATE[2]))

    back_rows = dot_nt(dq[...], wa[:, pl.ds(0, WIDTH)]) + own_sum
    q_s[:, pl.ds(0, 128)] = jnp.concatenate([sel[...].astype(F32), jnp.zeros((128 - BLOCK, ROWS), F32)], 0).T.astype(BF)
    back_low = jnp.concatenate([back_rows, jnp.zeros((128 - BLOCK, WIDTH), F32)], 0)
    back_rest = (back_low - back_low.astype(BF).astype(F32)).astype(BF)
    back_low = back_low.astype(BF)

    def input_back(i):
        rows = tile(i, 256, 256)
        total = dot_nt(dkv[rows, pl.ds(0, WIDTH)], wa[:, pl.ds(HALF, WIDTH)])
        total += dot_nt(dkv[rows, pl.ds(WIDTH, cut)], wa[:, pl.ds(WIDTH, cut)])
        total += dot_nt(dkv[rows, pl.ds(WIDTH + cut, cut)], wa[:, pl.ds(HALF + WIDTH, cut)])
        hit_rows = q_s[rows, pl.ds(0, 128)]
        total += dot(hit_rows, back_low) + dot(hit_rows, back_rest)
        igrad_ref[rows, :] = total.astype(BF)

    for i in range(MICRO):
        loop(2, shifted(input_back, 2 * i))
        leave(igrad_ref, igrad_out, pl.ds(STREAM * i, STREAM), 2 + i)
        run(steps, 1)

    tall_first = jnp.minimum(place.index * FF_OWN // 128, (FF - 256) // 128) * 128
    tall_at = place.index * FF_OWN - tall_first
    own_first = jnp.minimum(place.index * OWN // 128, (WIDTH - 256) // 128) * 128
    own_at = place.index * OWN - own_first

    window[...] = dot_tn(act[:, pl.ds(pl.multiple_of(tall_first, 128), 256)], d_out[...])
    tw_ref[...] = window[pl.ds(pl.multiple_of(tall_at, 8), FF_OWN), :]
    own_cols = pl.ds(pl.multiple_of(own_first, 128), 256)
    own_lines = pl.ds(pl.multiple_of(own_at, 8), OWN)
    window[...] = dot_tn(cls_att[:, own_cols], d_branch[...])
    ow_ref[...] = window[own_lines, :]
    for j in range(4):
        window[...] = dot_tn(h_low[:, own_cols], slope[:, pl.ds(WIDTH * j, WIDTH)])
        iw_ref[:, pl.ds(WIDTH * j, WIDTH)] = window[own_lines, :]

    def own_lanes(line, first, shift, size):
        window = jnp.broadcast_to(line[:, pl.ds(pl.multiple_of(first, 128), 256)], (8, 256))
        return pltpu.roll(window, 256 - shift, 1)[:1, :size]

    for ref, i in ((g2_ref, 0), (s2_ref, 1), (tb_ref, 2), (g1_ref, 3), (s1_ref, 4), (ob_ref, 5)):
        ref[...] = own_lanes(sums.at[pl.ds(i, 1), :], own_first, own_at, OWN)
    ib_ref[...] = own_lanes(sums_b1, tall_first, tall_at, FF_OWN)

    run(steps)
    qw_ref[...] = summed[:, pl.ds(0, WIDTH)]
    kw_ref[...] = summed[:, pl.ds(WIDTH, WIDTH)]
    vw_ref[...] = summed[:, pl.ds(2 * WIDTH, WIDTH)]
    lines = jnp.concatenate([summed[:, pl.ds(3 * WIDTH, 128)], jnp.zeros((128 - OWN, 128), F32)], 0).T
    qb_ref[...] = lines[0:1, :OWN]
    vb_ref[...] = lines[1:2, :OWN]
    for copy in leaving:
        copy.wait()
    sender.close()


def copy_kernel(count, *refs):
    ins, outs, held, sems = refs[:count], refs[count : 2 * count], refs[2 * count : 3 * count], refs[-1]
    pieces = []
    for i in range(count):
        rows = ins[i].shape[0]
        size = PIECE if rows > PIECE else rows
        pieces += [(i, pl.ds(at, size)) for at in range(0, rows, size)]
    first = [pltpu.make_async_copy(ins[i].at[at], held[i].at[at], sems.at[0, n]) for n, (i, at) in enumerate(pieces)]
    second = [pltpu.make_async_copy(held[i].at[at], outs[i].at[at], sems.at[1, n]) for n, (i, at) in enumerate(pieces)]
    for copy in first:
        copy.start()
    for before, after in zip(first, second):
        before.wait()
        after.start()
    for copy in second:
        copy.wait()


def fast(hidden_in, query_lengths, passage_lengths, positives, stored):
    (query_weight, query_bias, key_weight, value_weight, value_bias, output_weight, output_bias, first_gain,
     first_shift, inner_weight, inner_bias, outer_weight, outer_bias, second_gain, second_shift) = stored
    shapes = [
        ((ROWS, WIDTH), BF), ((ROWS, WIDTH), BF), ((OWN, WIDTH), F32), ((1, OWN), F32), ((OWN, WIDTH), F32),
        ((OWN, WIDTH), F32), ((1, OWN), F32), ((OWN, WIDTH), F32), ((1, OWN), F32), ((1, OWN), F32), ((1, OWN), F32),
        ((OWN, FF), F32), ((1, FF_OWN), F32), ((FF_OWN, WIDTH), F32), ((1, OWN), F32), ((1, OWN), F32), ((1, OWN), F32),
    ]
    scratch = [
        pltpu.VMEM((ROWS, WIDTH), BF), pltpu.VMEM((ROWS, WIDTH), BF),
        pltpu.VMEM((128, 128), F32), pltpu.VMEM((32, 6400), BF), pltpu.VMEM((32, 3200), BF), pltpu.VMEM((WIDTH, 6400), BF), pltpu.VMEM((FF, WIDTH), BF),
        pltpu.VMEM((16, WIDTH), F32), pltpu.VMEM((1, FF), F32),
        pltpu.VMEM((ROWS, WIDTH), BF), pltpu.VMEM((ROWS, WIDTH), BF), pltpu.VMEM((ROWS, WIDTH), BF),
        pltpu.VMEM((ROWS, STREAM), BF), pltpu.VMEM((BLOCK, ROWS), BF), pltpu.VMEM((8, ROWS), jnp.int32),
        pltpu.VMEM((2 * BLOCK, WIDTH), BF), pltpu.VMEM((2 * BLOCK, WIDTH // 2), BF),
        pltpu.VMEM((2, 2 * BLOCK, WIDTH // 2), BF), pltpu.VMEM((CLS, WIDTH), BF),
        pltpu.VMEM((2 * BLOCK, WIDTH), BF), pltpu.VMEM((2 * BLOCK, WIDTH // 2), BF),
        pltpu.VMEM((2, 2 * BLOCK, WIDTH // 2), BF), pltpu.VMEM((CLS, WIDTH), BF),
        pltpu.VMEM((CLS, WIDTH), F32), pltpu.VMEM((CLS, 128), F32), pltpu.VMEM((CLS, WIDTH), BF),
        pltpu.VMEM((CLS, FF), BF), pltpu.VMEM((CLS, FF), BF),
        pltpu.VMEM((CLS, WIDTH), F32), pltpu.VMEM((CLS, WIDTH), BF), pltpu.VMEM((CLS, WIDTH), BF),
        pltpu.VMEM((8, WIDTH), F32), pltpu.VMEM((1, FF), F32),
        pltpu.VMEM((BLOCK, WIDTH), F32), pltpu.VMEM((BLOCK, WIDTH), F32), pltpu.VMEM((BLOCK, WIDTH), F32),
        pltpu.VMEM((BLOCK, WIDTH), BF), pltpu.VMEM((ROWS, 2 * WIDTH), BF),
        pltpu.VMEM((WIDTH, 2 * HALF), BF),
        pltpu.VMEM((16, 2 * OWN, HALF), BF), pltpu.VMEM((16, 2 * OWN, HALF), BF), pltpu.VMEM((16, 2 * OWN, HALF), BF),
        pltpu.VMEM((4, 2 * OWN, HALF), BF), pltpu.VMEM((OWN, HALF), F32), pltpu.VMEM((OWN, HALF), F32),
        pltpu.VMEM((OWN, 2 * HALF), F32),
        pltpu.SemaphoreType.DMA((380,)), pltpu.SemaphoreType.DMA((20,)), pltpu.SemaphoreType.DMA((SLOTS + 92,)), pltpu.SemaphoreType.DMA((4,)),
    ]
    vmem = pl.BlockSpec(memory_space=pltpu.VMEM)
    smem = pl.BlockSpec(memory_space=pltpu.SMEM)
    outs = pl.pallas_call(
        layer_kernel,
        out_shape=[jax.ShapeDtypeStruct(shape, kind) for shape, kind in shapes],
        in_specs=[vmem] * 16 + [smem] * 3,
        out_specs=[pl.BlockSpec(memory_space=pl.ANY)] * 2 + [vmem] * (len(shapes) - 2),
        scratch_shapes=scratch,
        compiler_params=pltpu.CompilerParams(collective_id=0, has_side_effects=True, vmem_limit_bytes=63 * 2**20),
    )(
        hidden_in.reshape(ROWS, WIDTH), query_bias, value_bias, output_bias, first_gain, first_shift, outer_bias,
        second_gain, second_shift, inner_bias, query_weight, key_weight, value_weight, output_weight, inner_weight,
        outer_weight, query_lengths, passage_lengths, positives,
    )
    outs = pl.pallas_call(
        functools.partial(copy_kernel, len(shapes)),
        out_shape=[jax.ShapeDtypeStruct(shape, kind) for shape, kind in shapes],
        in_specs=[pl.BlockSpec(memory_space=pl.ANY)] * len(shapes),
        out_specs=[pl.BlockSpec(memory_space=pl.ANY)] * len(shapes),
        scratch_shapes=[pltpu.VMEM(shape, kind) for shape, kind in shapes] + [pltpu.SemaphoreType.DMA((2, len(shapes) + 2 * (ROWS // PIECE - 1)))],
    )(*outs)
    shape = hidden_in.shape
    return tuple(
        out.reshape(shape) if i < 2 else (out.reshape(-1) if out.shape[0] == 1 else out) for i, out in enumerate(outs)
    )


def local(
    hidden_in,
    query_lengths,
    passage_lengths,
    positives,
    query_weight,
    query_bias,
    key_weight,
    value_weight,
    value_bias,
    output_weight,
    output_bias,
    first_gain,
    first_shift,
    inner_weight,
    inner_bias,
    outer_weight,
    outer_bias,
    second_gain,
    second_shift,
):
    stored = (
        query_weight,
        query_bias,
        key_weight,
        value_weight,
        value_bias,
        output_weight,
        output_bias,
        first_gain,
        first_shift,
        inner_weight,
        inner_bias,
        outer_weight,
        outer_bias,
        second_gain,
        second_shift,
    )
    sizes = (lax.axis_size("tower"), lax.axis_size("batch"), hidden_in.shape, inner_weight.shape)
    if sizes == (2, 16, (MICRO, 1, STREAM, WIDTH), (OWN, FF)) and query_lengths.shape[1] == QS:
        return fast(hidden_in, query_lengths, passage_lengths, positives, stored)
    micro = hidden_in.shape[0]
    width = hidden_in.shape[3]
    cls_scale = width ** (-0.5)
    side = lax.axis_index("tower")
    is_query = side == 0
    slot_count = query_lengths.shape[1]
    passage_count = passage_lengths.shape[1]
    half_count = (slot_count + 1) // 2
    extra_rows = 2 * half_count - slot_count
    owners = lax.axis_size(("tower", "batch"))
    totals = tuple(
        (jnp.zeros((item.shape[0] * owners,) + item.shape[1:], jnp.float32) for item in stored)
    )
    half_totals = tuple(
        (jnp.zeros((item.shape[0] * owners // 2,) + item.shape[1:], jnp.float32) for item in stored)
    )
    shown_list = []
    grad_list = []
    for micro_step in range(micro):
        gathered = (
            lax.all_gather(query_weight, ("tower", "batch"), axis=0, tiled=True),
            lax.all_gather(query_bias, ("tower", "batch"), axis=0, tiled=True),
            lax.all_gather(key_weight, ("tower", "batch"), axis=0, tiled=True),
            lax.all_gather(value_weight, ("tower", "batch"), axis=0, tiled=True),
            lax.all_gather(value_bias, ("tower", "batch"), axis=0, tiled=True),
            lax.all_gather(output_weight, ("tower", "batch"), axis=0, tiled=True),
            lax.all_gather(output_bias, ("tower", "batch"), axis=0, tiled=True),
            lax.all_gather(first_gain, ("tower", "batch"), axis=0, tiled=True),
            lax.all_gather(first_shift, ("tower", "batch"), axis=0, tiled=True),
            lax.all_gather(inner_weight, ("tower", "batch"), axis=0, tiled=True),
            lax.all_gather(inner_bias, ("tower", "batch"), axis=0, tiled=True),
            lax.all_gather(outer_weight, ("tower", "batch"), axis=0, tiled=True),
            lax.all_gather(outer_bias, ("tower", "batch"), axis=0, tiled=True),
            lax.all_gather(second_gain, ("tower", "batch"), axis=0, tiled=True),
            lax.all_gather(second_shift, ("tower", "batch"), axis=0, tiled=True),
        )
        params = cast_params(gathered)
        inputs = hidden_in[micro_step, 0]
        passage_part = jnp.pad(passage_lengths[micro_step], (0, slot_count - passage_count))
        lengths = jnp.where(is_query, query_lengths[micro_step], passage_part)
        labels, valid, starts, live = segments(lengths, inputs.shape[0])
        saved, shown = forward(inputs, labels, valid, params)
        shown_list.append(shown)
        mine = jnp.where(live[:, None], shown[starts], 0.0)
        partner = partner_2(mine, "tower", 0)
        query_cls = jnp.where(is_query, mine, partner)
        passage_cls = jnp.where(is_query, partner, mine)[:passage_count]
        pooled = lax.all_gather(passage_cls, "batch", axis=0, tiled=True)
        padded_queries = jnp.pad(query_cls, ((0, extra_rows), (0, 0)))
        padded_targets = jnp.pad(positives[micro_step], (0, extra_rows))
        my_queries = lax.dynamic_slice_in_dim(padded_queries, side * half_count, half_count, 0)
        my_targets = lax.dynamic_slice_in_dim(padded_targets, side * half_count, half_count, 0)
        logits = product_nt(my_queries, pooled) * cls_scale
        highest = jnp.max(logits, -1, keepdims=True)
        powers = jnp.exp(logits - highest)
        shares = powers / jnp.sum(powers, -1, keepdims=True)
        columns = jnp.arange(pooled.shape[0], dtype=jnp.int32)
        target = (columns[None, :] == my_targets[:, None]).astype(jnp.float32)
        grad_logits = ((shares - target) / micro).astype(jnp.bfloat16)
        own_grad = product(grad_logits, pooled) * cls_scale
        pooled_grad = product_tn(grad_logits, my_queries) * cls_scale
        summed = lax.psum_scatter(pooled_grad, "batch", scatter_dimension=0, tiled=True)
        other_queries, other_passages = (
            partner_2(own_grad.astype(jnp.bfloat16), "tower", 0).astype(own_grad.dtype),
            partner_2(summed.astype(jnp.bfloat16), "tower", 0).astype(summed.dtype),
        )
        query_grad = jnp.concatenate([own_grad, other_queries], 0)[:slot_count]
        passage_grad = jnp.pad(summed + other_passages, ((0, slot_count - passage_count), (0, 0)))
        cotangent = jnp.where(is_query, query_grad, passage_grad)
        input_part, step_grads = backward(inputs, labels, cotangent, starts, live, saved, params)
        grad_list.append(input_part)
        totals = tuple((first + second for first, second in zip(totals, step_grads)))
    keep_all, give_all = split_halves(totals, side)
    came_all = jax.tree.map(
        lambda part, own: part.astype(own.dtype), partner_2(as_sent(give_all), "tower", 0), give_all
    )
    half_totals = tuple((first + second for first, second in zip(keep_all, came_all)))
    shards = lax.psum_scatter(half_totals, "batch", scatter_dimension=0, tiled=True)
    hidden_out = jnp.stack(shown_list)[:, None]
    input_grad = jnp.stack(grad_list)[:, None]
    return (
        hidden_out,
        input_grad,
        shards[0],
        shards[1],
        shards[2],
        shards[3],
        shards[4],
        shards[5],
        shards[6],
        shards[7],
        shards[8],
        shards[9],
        shards[10],
        shards[11],
        shards[12],
        shards[13],
        shards[14],
    )


def solution(mesh):
    placed = (
        P(None, "tower", "batch", None),
        P(None, "batch"),
        P(None, "batch"),
        P(None, "batch"),
        P(("tower", "batch"), None),
        P(("tower", "batch")),
        P(("tower", "batch"), None),
        P(("tower", "batch"), None),
        P(("tower", "batch")),
        P(("tower", "batch"), None),
        P(("tower", "batch")),
        P(("tower", "batch")),
        P(("tower", "batch")),
        P(("tower", "batch"), None),
        P(("tower", "batch")),
        P(("tower", "batch"), None),
        P(("tower", "batch")),
        P(("tower", "batch")),
        P(("tower", "batch")),
    )
    return jax.shard_map(
        local,
        mesh=mesh,
        in_specs=placed,
        out_specs=(
            P(None, "tower", "batch", None),
            P(None, "tower", "batch", None),
            P(("tower", "batch"), None),
            P(("tower", "batch")),
            P(("tower", "batch"), None),
            P(("tower", "batch"), None),
            P(("tower", "batch")),
            P(("tower", "batch"), None),
            P(("tower", "batch")),
            P(("tower", "batch")),
            P(("tower", "batch")),
            P(("tower", "batch"), None),
            P(("tower", "batch")),
            P(("tower", "batch"), None),
            P(("tower", "batch")),
            P(("tower", "batch")),
            P(("tower", "batch")),
        ),
        check_vma=False,
    )
```
